256 devices in a mesh: dp: 2 (over z_hi), blk: 16 (over z_lo, x), head: 8 (over y, core).
Axes of the slice: x: 4, y: 4, z: 8 (z_hi: 2, z_lo: 4; z = z_hi * 4 + z_lo), core: 2. Of those that a mesh axis runs over, the one named last changes fastest.
Arguments:
- video_q: bfloat16 [2, 4096, 2048], P('dp', ('blk', 'head')), may hold values from -6 to 6
- video_k: bfloat16 [2, 4096, 2048], P('dp', ('blk', 'head')), may hold values from -6 to 6
- video_v: bfloat16 [2, 4096, 2048], P('dp', ('blk', 'head')), may hold values from -6 to 6
- video_out: bfloat16 [2, 4096, 2048], P('dp', ('blk', 'head')), may hold values from -6 to 6
- video_dout: bfloat16 [2, 4096, 2048], P('dp', ('blk', 'head')), may hold values from -48 to 48
- text_q: bfloat16 [2, 256, 2048], P('dp', 'head'), may hold values from -6 to 6
- text_k: bfloat16 [2, 256, 2048], P('dp', 'head'), may hold values from -6 to 6
- text_v: bfloat16 [2, 256, 2048], P('dp', 'head'), may hold values from -6 to 6
- text_out: bfloat16 [2, 256, 2048], P('dp', 'head'), may hold values from -6 to 6
- text_dout: bfloat16 [2, 256, 2048], P('dp', 'head'), may hold values from -48 to 48
- video_lse: float32 [2, 16, 4096], P('dp', 'head', 'blk'), may hold values from 7.5 to 9
- text_lse: float32 [2, 16, 256], P('dp', 'head'), may hold values from 7.5 to 9
- video_norm: bfloat16 [2, 4096, 3072], P('dp', ('blk', 'head')), may hold values from -24 to 24
- text_norm: bfloat16 [2, 256, 3072], P('dp', 'head'), may hold values from -6 to 6
- video_mod: float32 [2, 2, 3072], P('dp'), may hold values from -3 to 3
- text_mod: float32 [2, 2, 3072], P('dp'), may hold values from -3 to 3
- video_weight: bfloat16 [3072, 3, 2048], P(None, None, 'head'), may hold values from -0.109375 to 0.109375
- text_weight: bfloat16 [3072, 3, 2048], P(None, None, 'head'), may hold values from -0.109375 to 0.109375
Outputs:
- video_dnorm: bfloat16 [2, 4096, 3072], P('dp', ('blk', 'head'))
- text_dnorm: bfloat16 [2, 256, 3072], P('dp', 'head')
- video_wgrad: float32 [3072, 3, 2048], P(('dp', 'blk'), None, 'head')
- text_wgrad: float32 [3072, 3, 2048], P(('dp', 'blk'), None, 'head')
- video_mod_grad: float32 [2, 2, 3072], P('dp')
- text_mod_grad: float32 [2, 2, 3072], P('dp')
The draws below stay inside these ranges and needn't reach their ends.
All inputs are finite; a program needn't handle non-finite values.
Results may differ from the reference program's by a relative error of at most 0.029.
Values may be sent and summed in bfloat16 or wider, within the bound.
A program may use at most 128 MiB of HBM per device.

```python
import jax
import jax.numpy as jnp
from jax import lax

D = 3072
H = 16
DH = 128
TT = 256
VBLK = 256
HEAD_DEV = 2
SV = 4096
CLIPS = 2
N_BLK = 16
N_HEAD = 8


def with_spikes(entries, own_key, source, target, parts, factor):
    def block_of(axis_at):
        return (jnp.arange(entries.shape[axis_at]) // (entries.shape[axis_at] // parts)).reshape((-1,) + (1,) * (entries.ndim - 1 - axis_at))

    near = jax.random.permutation(own_key, parts)[block_of(target)]
    other_side = (block_of(target) + parts // 2) % parts
    return jnp.where((block_of(source) == near) | (block_of(source) == other_side), factor * entries, entries)


def levels(key, dims, shards, smallest, high):
    def one(position, parts):
        draws = jax.random.uniform(jax.random.fold_in(jax.random.fold_in(key, 6), position), (parts,), jnp.float32, smallest / len(shards), high / len(shards))
        return jnp.repeat(jnp.exp(draws), dims[position] // parts).reshape((-1,) + (1,) * (len(dims) - position - 1))

    level = one(*shards[0])
    for cut in shards[1:]:
        level = level * one(*cut)
    return level


def centred(own_key, shape, spread, bound, shards=(), held_as=jnp.bfloat16):
    drawn = spread * jax.random.normal(own_key, shape, jnp.float32)
    if shards:
        drawn = drawn * levels(own_key, shape, shards, -0.22, 0.18)
    return jnp.clip(drawn, -bound, bound).astype(held_as)


def bell_draw_with(key, extent, scale, bound, split, heavy, kind=jnp.bfloat16):
    drawn = scale * jax.random.normal(key, extent, jnp.float32)
    if split:
        drawn = drawn * levels(key, extent, split, -0.22, 0.18)
    return jnp.clip(with_spikes(drawn, jax.random.fold_in(key, 3), *heavy), -bound, bound).astype(kind)


def setup_inputs(seed: int = 0) -> dict:
    key_of = jax.random.split(jax.random.key(seed), 19)
    return {
        "video_q": centred(key_of[0], (CLIPS, SV, H * DH), 1.0, 6.0, ((0, 2), (1, 128))),
        "video_k": centred(key_of[1], (CLIPS, SV, H * DH), 1.0, 6.0, ((0, 2), (1, 128))),
        "video_v": centred(key_of[2], (CLIPS, SV, H * DH), 1.0, 6.0, ((0, 2), (1, 128))),
        "video_out": centred(key_of[3], (CLIPS, SV, H * DH), 1.0, 6.0, ((0, 2), (1, 128))),
        "video_dout": centred(key_of[4], (CLIPS, SV, H * DH), 8.0, 48.0, ((0, 2), (1, 128))),
        "text_q": centred(key_of[5], (CLIPS, TT, H * DH), 1.0, 6.0, ((0, 2), (1, 8))),
        "text_k": centred(key_of[6], (CLIPS, TT, H * DH), 1.0, 6.0, ((0, 2), (1, 8))),
        "text_v": centred(key_of[7], (CLIPS, TT, H * DH), 1.0, 6.0, ((0, 2), (1, 8))),
        "text_out": centred(key_of[8], (CLIPS, TT, H * DH), 1.0, 6.0, ((0, 2), (1, 8))),
        "text_dout": centred(key_of[9], (CLIPS, TT, H * DH), 8.0, 48.0, ((0, 2), (1, 8))),
        "video_lse": jnp.clip(7.5 + 1.5 * jax.random.uniform(key_of[10], (CLIPS, H, SV), jnp.float32) ** levels(key_of[10], (CLIPS, H, SV), ((0, 2), (1, 8), (2, 16)), -0.2, 0.2), 7.5, 9.0),
        "text_lse": jnp.clip(7.5 + 1.5 * jax.random.uniform(key_of[11], (CLIPS, H, TT), jnp.float32) ** levels(key_of[11], (CLIPS, H, TT), ((0, 2), (1, 8)), -0.2, 0.2), 7.5, 9.0),
        "video_norm": bell_draw_with(key_of[12], (CLIPS, SV, D), 1.0, 24.0, ((0, 2), (1, 128)), (1, 2, 128, 5.5)),
        "text_norm": centred(key_of[13], (CLIPS, TT, D), 1.0, 6.0, ((0, 2), (1, 8))),
        "video_mod": centred(key_of[14], (CLIPS, 2, D), 0.5, 3.0, ((0, 2),), jnp.float32),
        "text_mod": centred(key_of[15], (CLIPS, 2, D), 0.5, 3.0, ((0, 2),), jnp.float32),
        "video_weight": centred(key_of[16], (D, 3, H * DH), D ** -0.5, 0.109375, ((2, 8),)),
        "text_weight": centred(key_of[17], (D, 3, H * DH), D ** -0.5, 0.109375, ((2, 8),)),
    }


HIGH = lax.Precision.HIGHEST


def product(left, right):
    return jnp.dot(left.astype(jnp.float32), right.astype(jnp.float32), precision=HIGH)


def rounded(values):
    return lax.optimization_barrier(values.astype(jnp.bfloat16)).astype(jnp.float32)


def head_grads(operands):
    query, keys, values, output, dout, lse = operands
    factor = DH ** -0.5
    delta = jnp.sum(dout.astype(jnp.float32) * output.astype(jnp.float32), axis=1)
    total_rows = query.shape[0]
    count = total_rows // TT
    query_f = query.astype(jnp.float32)
    keys_f = keys.astype(jnp.float32)
    values_f = values.astype(jnp.float32)
    dout_f = dout.astype(jnp.float32)

    def visit(carry, index):
        grad_k, grad_v = carry
        start = (index * TT).astype(jnp.int32)
        rows_q = lax.dynamic_slice_in_dim(query_f, start, TT, 0)
        rows_d = lax.dynamic_slice_in_dim(dout_f, start, TT, 0)
        rows_lse = lax.dynamic_slice_in_dim(lse, start, TT, 0)
        rows_delta = lax.dynamic_slice_in_dim(delta, start, TT, 0)
        scores = product(rows_q, keys_f.T) * factor
        probs = jnp.exp(scores - rows_lse[:, None])
        dprobs = product(rows_d, values_f.T)
        dscores = rounded(probs * (dprobs - rows_delta[:, None]))
        probs_b = rounded(probs)
        grad_q = product(dscores, keys_f) * factor
        grad_k = grad_k + product(dscores.T, rows_q) * factor
        grad_v = grad_v + product(probs_b.T, rows_d)
        return (grad_k, grad_v), grad_q

    zeros = jnp.zeros(keys.shape, jnp.float32)
    (grad_k, grad_v), grad_q = lax.scan(visit, (zeros, zeros), jnp.arange(count, dtype=jnp.int32))
    return grad_q.reshape(total_rows, DH), grad_k, grad_v


def split_heads(array):
    return array.reshape(array.shape[0], H, DH).transpose(1, 0, 2)


def clip_grads(arrays):
    joint = [jnp.concatenate([arrays[index], arrays[index + 5]], axis=0) for index in range(5)]
    lse = jnp.concatenate([arrays[10], arrays[11]], axis=1)
    grads = lax.map(head_grads, tuple(split_heads(array) for array in joint) + (lse,))
    stacked = jnp.stack(grads, axis=1)
    total_rows = stacked.shape[2]
    return stacked.transpose(2, 1, 0, 3).reshape(total_rows, 3, H * DH).astype(jnp.bfloat16)


def back_proj(grads, weight):
    rows = grads.shape[0]
    grouped = grads.reshape(rows, 3, N_HEAD, HEAD_DEV * DH)
    weight_grouped = weight.reshape(D, 3, N_HEAD, HEAD_DEV * DH)
    total = jnp.zeros((rows, D), jnp.float32)
    for group in range(N_HEAD):
        term = jnp.einsum("rcf,dcf->rd", grouped[:, :, group].astype(jnp.float32),
                          weight_grouped[:, :, group].astype(jnp.float32), precision=HIGH)
        total = total + rounded(term)
    return total


def weight_term(inputs, grads):
    return rounded(jnp.einsum("rd,rcf->dcf", inputs.astype(jnp.float32), grads.astype(jnp.float32), precision=HIGH))


def reference(video_q, video_k, video_v, video_out, video_dout, text_q, text_k, text_v, text_out, text_dout,
              video_lse, text_lse, video_norm, text_norm, video_mod, text_mod, video_weight, text_weight):
    video_dn, text_dn, video_mg, text_mg = [], [], [], []
    video_wg = jnp.zeros((D, 3, H * DH), jnp.float32)
    text_wg = jnp.zeros((D, 3, H * DH), jnp.float32)
    for clip in range(CLIPS):
        grads = clip_grads((video_q[clip], video_k[clip], video_v[clip], video_out[clip], video_dout[clip],
                            text_q[clip], text_k[clip], text_v[clip], text_out[clip], text_dout[clip],
                            video_lse[clip], text_lse[clip]))
        video_grads = grads[:SV]
        text_grads = grads[SV:]
        video_back = back_proj(video_grads, video_weight)
        text_back = back_proj(text_grads, text_weight)
        video_nf = video_norm[clip].astype(jnp.float32)
        text_nf = text_norm[clip].astype(jnp.float32)
        video_dn.append(((1.0 + video_mod[clip, 1]) * video_back).astype(jnp.bfloat16))
        text_dn.append(((1.0 + text_mod[clip, 1]) * text_back).astype(jnp.bfloat16))
        video_mg.append(jnp.stack([jnp.sum(video_back, axis=0), jnp.sum(video_back * video_nf, axis=0)]))
        text_mg.append(jnp.stack([jnp.sum(text_back, axis=0), jnp.sum(text_back * text_nf, axis=0)]))
        video_in = ((1.0 + video_mod[clip, 1]) * video_nf + video_mod[clip, 0]).astype(jnp.bfloat16)
        text_in = ((1.0 + text_mod[clip, 1]) * text_nf + text_mod[clip, 0]).astype(jnp.bfloat16)

        def add_block(carry, index):
            start = (index * VBLK).astype(jnp.int32)
            rows_in = lax.dynamic_slice_in_dim(video_in, start, VBLK, 0)
            rows_grad = lax.dynamic_slice_in_dim(video_grads, start, VBLK, 0)
            return carry + weight_term(rows_in, rows_grad), None

        video_wg, unused = lax.scan(add_block, video_wg, jnp.arange(N_BLK, dtype=jnp.int32))
        text_wg = text_wg + weight_term(text_in, text_grads)
    return (jnp.stack(video_dn), jnp.stack(text_dn), video_wg, text_wg, jnp.stack(video_mg), jnp.stack(text_mg))
```

```python
import functools

import jax
import jax.numpy as jnp
from jax import lax
from jax.experimental import pallas as pl
from jax.experimental.pallas import tpu as pltpu
from jax.sharding import PartitionSpec as P

MESH = pl.DeviceIdType.MESH
D = 3072
DH = 128
SET = 512
ROWS = 544
TXT = 32
FACTOR = DH ** (-0.5)
LOG2E = 1.4426950408889634
F32 = jnp.float32
BF16 = jnp.bfloat16

NAMES = (
    "a_q", "a_d", "a_k", "a_v", "a_st", "a_lse", "a_tq", "a_td", "a_tk", "a_tv",
    "b_kv", "b_qc", "b_sc", "b_qz", "b_sz", "b_qf", "b_sf", "vin", "tin",
    "d_kv", "d_qc", "d_qz", "e0", "e1", "e2", "tz", "te", "w0", "w1", "w2",
    "bc", "by", "tr", "tdn", "ts", "tsx", "s1", "s2", "s3", "s4", "tw",
)
SEM = {name: index for index, name in enumerate(NAMES)}
LOCALS = ("out", "dout", "tout", "tdout", "nrm", "tnrm", "w", "tw", "lse", "tlse", "mod", "tmod")


def nt(left, right):
    return lax.dot_general(left, right, (((1,), (1,)), ((), ())), preferred_element_type=F32)


def tn(left, right):
    return lax.dot_general(left, right, (((0,), (0,)), ((), ())), preferred_element_type=F32)


def nn(left, right):
    return jnp.dot(left, right, preferred_element_type=F32)


def kernel(
    q, k, v, out, dout, tq, tk, tv, tout, tdout, lse, tlse, norm, tnorm, mod, tmod, weight, tweight,
    o_dn, o_tdn, o_wg, o_twg, o_vs, o_ts,
    l_out, l_dout, l_tout, l_tdout, l_nrm, l_tnrm, l_w, l_tw, l_lse, l_tlse, l_mod, l_tmod,
    qd, kv, st, d_send, d_recv, l_send, l_recv,
    gk_acc, gv_acc, gq_acc, dkv_s, dkv_r, dqc_s, dqc_r, dqz_s, dqz_r, g_fin,
    vin_s, vin_all, tin_s, tin_all, gr, tz, tg, gs,
    w_send, w_recv, w_own, b_send, b_recv, b_own, y_send, y_recv,
    t_tmp, tr_send, tr_recv, tdn_all, ts_buf, tsx_buf, s1_s, s1_r, s2_buf, s3_buf, s4_buf, tw_s, tw_r,
    rs, ss, ls,
):
    dp = lax.axis_index("dp")
    blk = lax.axis_index("blk")
    head = lax.axis_index("head")
    z, x, y, c = blk // 4, blk % 4, head // 2, head % 2
    me = y * 4 + x
    mine = x // 2
    half = x % 2

    def dev(dz=None, dx=None, dy=None, dc=None, ddp=None):
        zz = z if dz is None else dz
        xx = x if dx is None else dx
        yy = y if dy is None else dy
        cc = c if dc is None else dc
        return {"dp": dp if ddp is None else ddp, "blk": zz * 4 + xx, "head": yy * 2 + cc}

    def remote(src, dst, name, to):
        return pltpu.make_async_remote_copy(
            src_ref=src, dst_ref=dst, send_sem=ss.at[SEM[name]], recv_sem=rs.at[SEM[name]],
            device_id=to, device_id_type=MESH)

    def local(src, dst, name):
        return pltpu.make_async_copy(src, dst, rs.at[SEM[name]])

    def got(ref, name):
        pltpu.make_async_copy(ref, ref, rs.at[SEM[name]]).wait()

    def sent(ref, name):
        pltpu.make_async_copy(ref, ref, ss.at[SEM[name]]).wait()

    def rows32(index):
        return pl.ds(pl.multiple_of(index * 32, 32), 32)

    def lanes(index, width=128):
        return pl.ds(pl.multiple_of(index * width, 128), width)

    def send_a(t, carry):
        to = dev(dx=t % 4, dy=t // 4)
        for src, dst, name in ((k, kv.at[0, 0], "a_k"), (v, kv.at[0, 1], "a_v"),
                               (q, qd.at[0, 0], "a_q"), (dout, qd.at[0, 1], "a_d")):
            piece = src.at[:, lanes(t)]
            place = dst.at[rows32(me)]

            @pl.when(t != me)
            def _():
                remote(piece, place, name, to).start()

            @pl.when(t == me)
            def _():
                local(piece, place, name).start()
        return carry

    lax.fori_loop(0, 16, send_a, 0)

    @pl.when(y == z)
    def _():
        for t in range(4):
            for src, dst, name in ((tk, kv.at[0, 0], "a_tk"), (tv, kv.at[0, 1], "a_tv"),
                                   (tq, qd.at[0, 0], "a_tq"), (tdout, qd.at[0, 1], "a_td")):
                piece = src.at[:, lanes(4 * t + x)]
                place = dst.at[pl.ds(SET, TXT)]

                @pl.when(t != y)
                def _():
                    remote(piece, place, name, dev(dy=t)).start()

                @pl.when(t == y)
                def _():
                    local(piece, place, name).start()

    loads = {
        "out": (out, l_out), "dout": (dout, l_dout), "tout": (tout, l_tout), "tdout": (tdout, l_tdout),
        "nrm": (norm, l_nrm), "tnrm": (tnorm, l_tnrm), "lse": (lse, l_lse), "tlse": (tlse, l_tlse),
        "mod": (mod, l_mod), "tmod": (tmod, l_tmod), "w": (weight, l_w),
        "tw": (tweight.at[:, pl.ds(pl.multiple_of(x * 768, 768), 768), :], l_tw),
    }
    copies = {n: pltpu.make_async_copy(s, d, ls.at[LOCALS.index(n)]) for n, (s, d) in loads.items()}
    for name in ("out", "dout", "lse", "tlse", "tout", "tdout", "nrm", "mod", "tnrm", "tmod", "w", "tw"):
        copies[name].start()

    lane = lax.broadcasted_iota(jnp.int32, (16, 128), 1)
    ones = jnp.where(
        lax.broadcasted_iota(jnp.int32, (16, 2048), 1) // DH
        == lax.broadcasted_iota(jnp.int32, (16, 2048), 0), 1.0, 0.0).astype(BF16)

    def delta_rows(a_ref, b_ref):
        total = jnp.zeros((16, 128), F32)
        products = a_ref[...].astype(F32) * b_ref[...].astype(F32)
        high = products.astype(BF16)
        low = (products - high.astype(F32)).astype(BF16)
        for part in (high, low):
            total = total + nt(ones, jnp.concatenate([part] * 4, axis=0))
        return total

    copies["out"].wait()
    copies["dout"].wait()
    video_delta = jnp.where(lane // 32 == x, delta_rows(l_out, l_dout), 0.0)
    copies["tout"].wait()
    copies["tdout"].wait()
    text_delta = jnp.where(lane < 32, delta_rows(l_tout, l_tdout), 0.0)
    d_send[...] = jnp.zeros_like(d_send)
    for h in range(16):
        d_send[h, 0:1, :] = video_delta[h:h + 1, :]
        d_send[h, 1:2, :] = text_delta[h:h + 1, :]

    def send_delta(t, carry):
        @pl.when(t != me)
        def _():
            remote(d_send.at[t], d_recv.at[me], "a_st", dev(dx=t % 4, dy=t // 4)).start()

        @pl.when(t == me)
        def _():
            local(d_send.at[t], d_recv.at[me], "a_st").start()
        return carry

    lax.fori_loop(0, 16, send_delta, 0)

    copies["lse"].wait()
    copies["tlse"].wait()
    lane8 = lax.broadcasted_iota(jnp.int32, (8, 128), 1)
    l_send[...] = jnp.zeros_like(l_send)
    for j in range(2):
        for cc in range(2):
            for yy in range(4):
                row = jnp.broadcast_to(l_lse[j:j + 1, 128 * (yy // 2):128 * (yy // 2) + 128], (8, 128))
                shift = (32 * x + 256 - (yy % 2) * 64 - cc * 32) % 128
                row = jnp.where(lane8 // 32 == x, pltpu.roll(row, shift, 1), 0.0)
                l_send[j, cc, yy:yy + 1, :] = row[0:1, :]
            row = jnp.broadcast_to(l_tlse[j:j + 1, pl.ds(pl.multiple_of((z // 2) * 128, 128), 128)], (8, 128))
            shift = (256 - (z % 2) * 64 - cc * 32) % 128
            row = jnp.where(lane8 < 32, pltpu.roll(row, shift, 1), 0.0)
            l_send[j, cc, 4:5, :] = row[0:1, :]
    for j in range(2):
        for cc in range(2):
            own = jnp.logical_and(x == 2 * c + j, c == cc)

            @pl.when(jnp.logical_not(own))
            def _():
                remote(l_send.at[j, cc], l_recv.at[x], "a_lse", dev(dx=2 * c + j, dc=cc)).start()

            @pl.when(own)
            def _():
                local(l_send.at[j, cc], l_recv.at[x], "a_lse").start()

    copies["nrm"].wait()
    copies["mod"].wait()
    gain = 1.0 + l_mod[1:2, :]
    vin = (gain * l_nrm[...].astype(F32) + l_mod[0:1, :])
    for xx in range(4):
        parts = [vin[:, 384 * m + 96 * xx:384 * m + 96 * xx + 96] for m in range(8)]
        vin_s[xx] = jnp.concatenate(parts, axis=1).astype(BF16)
    copies["tnrm"].wait()
    copies["tmod"].wait()
    tgain = 1.0 + l_tmod[1:2, :]
    tin_s[...] = (tgain * l_tnrm[...].astype(F32) + l_tmod[0:1, :]).astype(BF16)

    gk_acc[...] = jnp.zeros_like(gk_acc)
    gv_acc[...] = jnp.zeros_like(gv_acc)
    gq_acc[...] = jnp.zeros_like(gq_acc)

    got(kv.at[0, 0, pl.ds(0, SET)], "a_k")
    got(kv.at[0, 1, pl.ds(0, SET)], "a_v")
    got(kv.at[0, 0, pl.ds(SET, TXT)], "a_tk")
    got(kv.at[0, 1, pl.ds(SET, TXT)], "a_tv")
    zn = z + 1 - 2 * (z % 2)
    zf = (z + 2) % 4
    remote(kv.at[0], kv.at[1], "b_kv", dev(dz=zn)).start()
    got(qd.at[0, 0, pl.ds(0, SET)], "a_q")
    got(qd.at[0, 1, pl.ds(0, SET)], "a_d")
    got(qd.at[0, 0, pl.ds(SET, TXT)], "a_tq")
    got(qd.at[0, 1, pl.ds(SET, TXT)], "a_td")
    remote(qd.at[0], qd.at[1], "b_qz", dev(dz=zf)).start()
    remote(qd.at[0], qd.at[2], "b_qc", dev(dc=1 - c)).start()
    got(d_recv, "a_st")
    got(l_recv, "a_lse")
    for yy in range(4):
        st[0, yy:yy + 1, :] = LOG2E * (l_recv[0, yy:yy + 1, :] + l_recv[1, yy:yy + 1, :]
                                       + l_recv[2, yy:yy + 1, :] + l_recv[3, yy:yy + 1, :])
        st[0, 4 + yy:5 + yy, :] = (d_recv[4 * yy, 0:1, :] + d_recv[4 * yy + 1, 0:1, :]
                                   + d_recv[4 * yy + 2, 0:1, :] + d_recv[4 * yy + 3, 0:1, :])
    st[0, 8:9, :] = LOG2E * l_recv[0, 4:5, :]
    st[0, 9:10, :] = d_recv[z * 4 + x, 1:2, :]
    st[0, 10:16, :] = jnp.zeros((6, 128), F32)
    remote(st.at[0], st.at[1], "b_sz", dev(dz=zf)).start()
    remote(st.at[0], st.at[2], "b_sc", dev(dc=1 - c)).start()

    def send_vin(t, carry):
        hd, xx = t // 4, t % 4
        place = vin_all.at[pl.ds(pl.multiple_of(c * SET + me * 32, 32), 32)]
        own = jnp.logical_and(hd == head, xx == x)

        @pl.when(jnp.logical_not(own))
        def _():
            remote(vin_s.at[xx], place, "vin", dev(dx=xx, dy=hd // 2, dc=hd % 2)).start()

        @pl.when(own)
        def _():
            local(vin_s.at[xx], place, "vin").start()
        return carry

    lax.fori_loop(0, 32, send_vin, 0)

    window = jnp.minimum((blk * 96) // 128 * 128, 1280)

    def send_tin(hd, carry):
        for other in range(2):
            piece = tin_s.at[:, pl.ds(pl.multiple_of(other * 1536 + window, 128), 256)]
            place = tin_all.at[rows32(head), pl.ds(other * 256, 256)]

            @pl.when(hd != head)
            def _():
                remote(piece, place, "tin", dev(dy=hd // 2, dc=hd % 2)).start()

            @pl.when(hd == head)
            def _():
                local(piece, place, "tin").start()
        return carry

    lax.fori_loop(0, 8, send_tin, 0)

    def pair(lse_row, delta_row, query, dquery, keys, values):
        probs = jnp.exp2(nt(keys, query) * (FACTOR * LOG2E) - lse_row)
        dscores = (probs * (nt(values, dquery) - delta_row)).astype(BF16)
        return probs.astype(BF16), dscores

    def row512(i, first):
        return jnp.concatenate([st[i, first + n:first + n + 1, :] for n in range(4)], axis=1)

    def attend(step, carry):
        i = (step % 2) * 2 + step // 4
        j = ((step + 2) // 4) % 2

        @pl.when(step == 1)
        def _():
            got(qd.at[2], "b_qc")
            got(st.at[2], "b_sc")

        @pl.when(step == 2)
        def _():
            got(kv.at[1], "b_kv")

        @pl.when(step == 4)
        def _():
            got(qd.at[1], "b_qz")
            remote(qd.at[1], qd.at[3], "b_qf", dev(dc=1 - c)).start()
            got(st.at[1], "b_sz")
            remote(st.at[1], st.at[3], "b_sf", dev(dc=1 - c)).start()

        @pl.when(step == 5)
        def _():
            got(qd.at[3], "b_qf")
            got(st.at[3], "b_sf")

        query, dquery = qd[i, 0, 0:SET, :], qd[i, 1, 0:SET, :]
        keys, values = kv[j, 0], kv[j, 1]
        probs, dscores = pair(row512(i, 0), row512(i, 4), query, dquery, keys, values)
        gv_acc[j] += nn(probs, dquery)
        gk_acc[j] += nn(dscores, query)
        gq_acc[i, 0:SET, :] += tn(dscores, keys)
        return carry

    def attend_text(j):
        query = jnp.concatenate([qd[i, 0, SET:ROWS, :] for i in range(4)], axis=0)
        dquery = jnp.concatenate([qd[i, 1, SET:ROWS, :] for i in range(4)], axis=0)
        lse_row = jnp.zeros((8, 128), F32)
        delta_row = jnp.zeros((8, 128), F32)
        for i in range(4):
            one, two = (jnp.broadcast_to(st[i, r:r + 1, :], (8, 128)) for r in (8, 9))
            lse_row = lse_row + (pltpu.roll(one, 32 * i, 1) if i else one)
            delta_row = delta_row + (pltpu.roll(two, 32 * i, 1) if i else two)
        keys, values = kv[j, 0], kv[j, 1]
        probs, dscores = pair(lse_row[0:1, :], delta_row[0:1, :], query, dquery, keys, values)
        gv_acc[j] += nn(probs, dquery)
        gk_acc[j] += nn(dscores, query)
        from_text = tn(dscores, keys)
        for i in range(4):
            gq_acc[i, SET:ROWS, :] += from_text[32 * i:32 * i + 32, :]

    lax.fori_loop(0, 6, attend, 0)
    attend_text(1)
    dkv_s[0] = (gk_acc[1] * FACTOR).astype(BF16)
    dkv_s[1] = gv_acc[1].astype(BF16)
    remote(dkv_s, dkv_r, "d_kv", dev(dz=zn)).start()
    lax.fori_loop(6, 8, attend, 0)
    attend_text(0)
    dqc_s[0] = (gq_acc[2] * FACTOR).astype(BF16)
    dqc_s[1] = (gq_acc[3] * FACTOR).astype(BF16)
    remote(dqc_s, dqc_r, "d_qc", dev(dc=1 - c)).start()
    got(dqc_r, "d_qc")
    dqz_s[...] = (gq_acc[1] * FACTOR + dqc_r[1].astype(F32)).astype(BF16)
    remote(dqz_s, dqz_r, "d_qz", dev(dz=zf)).start()

    def send_grads(ch):
        for xx in range(4):
            own = jnp.logical_and(x == xx, c == mine)
            piece = g_fin.at[ch, pl.ds(0, SET)]
            place = gr.at[ch, pl.ds(pl.multiple_of(c * SET, SET), SET), lanes(half)]

            @pl.when(jnp.logical_not(own))
            def _():
                remote(piece, place, "e%d" % ch, dev(dx=xx, dc=mine)).start()

            @pl.when(own)
            def _():
                local(piece, place, "e%d" % ch).start()

    got(dkv_r, "d_kv")
    g_fin[1] = (gk_acc[0] * FACTOR + dkv_r[0].astype(F32)).astype(BF16)
    send_grads(1)
    g_fin[2] = (gv_acc[0] + dkv_r[1].astype(F32)).astype(BF16)
    send_grads(2)
    got(dqz_r, "d_qz")
    g_fin[0] = (gq_acc[0] * FACTOR + dqc_r[0].astype(F32) + dqz_r[...].astype(F32)).astype(BF16)
    send_grads(0)

    for zz in range(4):
        piece = g_fin.at[:, pl.ds(SET, TXT)]

        @pl.when(z != zz)
        def _():
            remote(piece, tz.at[:, z], "tz", dev(dz=zz)).start()

        @pl.when(z == zz)
        def _():
            local(piece, tz.at[:, z], "tz").start()
    got(tz, "tz")
    for xx in range(4):
        own = jnp.logical_and(x == xx, c == mine)
        place = tg.at[:, :, c, :, lanes(half)]

        @pl.when(jnp.logical_not(own))
        def _():
            remote(tz, place, "te", dev(dx=xx, dc=mine)).start()

        @pl.when(own)
        def _():
            local(tz, place, "te").start()

    pos = dp * 4 + z
    got(vin_all, "vin")
    for ch in (1, 2, 0):
        got(gr.at[ch], "e%d" % ch)
        grads = gr[ch]
        for other in range(8):
            if other % 4 == 0:
                term = tn(vin_all[:, 96 * other:96 * other + 384], grads)
            piece = term[96 * (other % 4):96 * (other % 4) + 96, :]
            w_send[other, ch] = piece.astype(BF16)

            @pl.when(pos != other)
            def _():
                remote(w_send.at[other, ch], w_recv.at[pos, ch], "w%d" % ch,
                       dev(ddp=other // 4, dz=other % 4)).start()

            @pl.when(pos == other)
            def _():
                w_own[ch] = piece

    for ch in range(3):
        for cc in range(2):
            for yy in range(4):
                first = pl.multiple_of(cc * SET + (yy * 4 + x) * 32, 32)
                gs[ch, cc * 128 + yy * 32:cc * 128 + yy * 32 + 32, :] = gr[ch, pl.ds(first, 32), :]
    copies["w"].wait()
    for n in range(6):
        cols = slice(512 * n, 512 * n + 512)
        term = (nt(gs[0], l_w[0, cols, :]) + nt(gs[1], l_w[1, cols, :]) + nt(gs[2], l_w[2, cols, :]))

        @pl.when(c == 0)
        def _():
            b_own[:, cols] = term[0:128, :]
            b_send[:, cols] = term[128:256, :].astype(BF16)

        @pl.when(c == 1)
        def _():
            b_own[:, cols] = term[128:256, :]
            b_send[:, cols] = term[0:128, :].astype(BF16)
    remote(b_send, b_recv, "bc", dev(dc=1 - c)).start()

    got(tg, "te")
    got(tin_all, "tin")
    first = pl.multiple_of(blk * 96 - window, 32)
    for ch in range(3):
        grads = tg[ch].reshape(256, 256)
        term = tn(tin_all[...], grads)
        t_tmp[...] = term.astype(BF16)
        away = pl.multiple_of((1 - dp) * 256 + first, 32)
        near = pl.multiple_of(dp * 256 + first, 32)
        tw_s[ch] = t_tmp[pl.ds(away, 96), :]
        o_twg[ch] = t_tmp[pl.ds(near, 96), :].astype(F32)
    remote(tw_s, tw_r, "tw", dev(ddp=1 - dp)).start()
    copies["tw"].wait()
    term = (nt(tg[0].reshape(256, 256), l_tw[0]) + nt(tg[1].reshape(256, 256), l_tw[1])
            + nt(tg[2].reshape(256, 256), l_tw[2]))
    for hd in range(8):
        tr_send[hd] = term[32 * hd:32 * hd + 32, :].astype(BF16)

        @pl.when(hd != head)
        def _():
            remote(tr_send.at[hd], tr_recv.at[head], "tr", dev(dy=hd // 2, dc=hd % 2)).start()

        @pl.when(hd == head)
        def _():
            local(tr_send.at[hd], tr_recv.at[head], "tr").start()

    got(b_recv, "bc")
    total = b_own[...] + b_recv[...].astype(F32)
    b_own[...] = total
    for yy in range(4):
        y_send[yy] = total[32 * yy:32 * yy + 32, :].astype(BF16)

        @pl.when(yy != y)
        def _():
            remote(y_send.at[yy], y_recv.at[y], "by", dev(dy=yy)).start()

    got(tr_recv, "tr")
    tback = tr_recv[0].astype(F32)
    for hd in range(1, 8):
        tback = tback + tr_recv[hd].astype(F32)
    cols = pl.ds(pl.multiple_of(x * 768, 768), 768)
    tdn_all[x] = ((1.0 + l_tmod[1:2, cols]) * tback).astype(BF16)
    tnf = l_tnrm[:, cols].astype(F32)
    ts_buf[head] = jnp.concatenate([jnp.sum(tback, axis=0, keepdims=True),
                                    jnp.sum(tback * tnf, axis=0, keepdims=True)], axis=0)
    for xx in range(4):
        @pl.when(xx != x)
        def _():
            remote(tdn_all.at[x], tdn_all.at[x], "tdn", dev(dx=xx)).start()
    for hd in range(8):
        @pl.when(hd != head)
        def _():
            remote(ts_buf.at[head], ts_buf.at[head], "ts", dev(dy=hd // 2, dc=hd % 2)).start()
    got(ts_buf.at[pl.ds(0, 7)], "ts")
    tstat = ts_buf[0]
    for hd in range(1, 8):
        tstat = tstat + ts_buf[hd]
    tsx_buf[x] = tstat
    for xx in range(4):
        @pl.when(xx != x)
        def _():
            remote(tsx_buf.at[x], tsx_buf.at[x], "tsx", dev(dx=xx)).start()

    got(y_recv.at[pl.ds(0, 3)], "by")
    back = b_own[rows32(y), :]
    for yy in range(4):
        back = back + jnp.where(yy == y, 0.0, y_recv[yy].astype(F32))
    o_dn[...] = ((1.0 + l_mod[1:2, :]) * back).astype(BF16)
    stat = jnp.concatenate([jnp.sum(back, axis=0, keepdims=True),
                            jnp.sum(back * l_nrm[...].astype(F32), axis=0, keepdims=True)], axis=0)
    s1_s[0] = stat[:, 0:1536]
    s1_s[1] = stat[:, 1536:3072]
    remote(s1_s.at[1 - c], s1_r, "s1", dev(dc=1 - c)).start()
    got(s1_r, "s1")
    s2_buf[me] = s1_s[c] + s1_r[...]

    def send_s2(t, carry):
        @pl.when(t != me)
        def _():
            remote(s2_buf.at[me], s2_buf.at[me], "s2", dev(dx=t % 4, dy=t // 4)).start()
        return carry

    lax.fori_loop(0, 16, send_s2, 0)
    got(s2_buf.at[pl.ds(0, 15)], "s2")
    stat = s2_buf[0]
    for t in range(1, 16):
        stat = stat + s2_buf[t]
    s3_buf[z] = stat
    for zz in range(4):
        @pl.when(zz != z)
        def _():
            remote(s3_buf.at[z], s3_buf.at[z], "s3", dev(dz=zz)).start()
    got(s3_buf.at[pl.ds(0, 3)], "s3")
    s4_buf[c] = s3_buf[0] + s3_buf[1] + s3_buf[2] + s3_buf[3]
    remote(s4_buf.at[c], s4_buf.at[c], "s4", dev(dc=1 - c)).start()
    got(s4_buf.at[0], "s4")
    o_vs[:, 0:1536] = s4_buf[0]
    o_vs[:, 1536:3072] = s4_buf[1]

    got(tdn_all.at[pl.ds(0, 3)], "tdn")
    got(tsx_buf.at[pl.ds(0, 3)], "tsx")
    for xx in range(4):
        o_tdn[:, 768 * xx:768 * xx + 768] = tdn_all[xx]
        o_ts[:, 768 * xx:768 * xx + 768] = tsx_buf[xx]
    got(tw_r, "tw")
    o_twg[...] += tw_r[...].astype(F32)

    for ch in (1, 2, 0):
        got(w_recv.at[pl.ds(0, 7), 0], "w%d" % ch)
        total = w_own[ch]
        for other in range(8):
            total = total + jnp.where(pos == other, 0.0, w_recv[other, ch].astype(F32))
        o_wg[ch] = total

    for name in ("a_k", "a_v", "a_q", "a_d"):
        sent(kv.at[0, 0, pl.ds(0, 480)], name)

    @pl.when(y == z)
    def _():
        for name in ("a_tk", "a_tv", "a_tq", "a_td"):
            sent(kv.at[0, 0, pl.ds(0, 96)], name)
    sent(d_recv.at[pl.ds(0, 15)], "a_st")

    @pl.when(c == mine)
    def _():
        sent(l_recv.at[pl.ds(0, 3)], "a_lse")
        for ch in range(3):
            sent(kv.at[:, 0, pl.ds(0, 512)], "e%d" % ch)
            sent(kv.at[0, 0, pl.ds(0, 512)], "e%d" % ch)
        for _ in range(3):
            sent(tz, "te")

    @pl.when(c != mine)
    def _():
        sent(l_recv, "a_lse")
        for ch in range(3):
            sent(gr.at[ch], "e%d" % ch)
        for _ in range(4):
            sent(tz, "te")
    sent(kv.at[0], "b_kv")
    for name in ("b_qz", "b_qc", "b_qf"):
        sent(qd.at[0], name)
    for name in ("b_sz", "b_sc", "b_sf"):
        sent(st.at[0], name)
    sent(vin_all.at[pl.ds(0, 31 * 32)], "vin")
    sent(tin_all.at[pl.ds(0, 7 * 32)], "tin")
    sent(dkv_s, "d_kv")
    sent(dqc_s, "d_qc")
    sent(dqz_s, "d_qz")
    sent(tz.at[:, pl.ds(0, 3)], "tz")
    for ch in range(3):
        sent(w_recv.at[pl.ds(0, 7), 0], "w%d" % ch)
    sent(b_send, "bc")
    sent(y_send.at[pl.ds(0, 3)], "by")
    sent(tr_recv.at[pl.ds(0, 7)], "tr")
    sent(tdn_all.at[pl.ds(0, 3)], "tdn")
    sent(ts_buf.at[pl.ds(0, 7)], "ts")
    sent(tsx_buf.at[pl.ds(0, 3)], "tsx")
    sent(s1_r, "s1")
    sent(s2_buf.at[pl.ds(0, 15)], "s2")
    sent(s3_buf.at[pl.ds(0, 3)], "s3")
    sent(s4_buf.at[0], "s4")
    sent(tw_s, "tw")


SCRATCH = (
    ((32, 2048), BF16), ((32, 2048), BF16), ((32, 2048), BF16), ((32, 2048), BF16),
    ((32, D), BF16), ((32, D), BF16), ((3, D, 256), BF16), ((3, 768, 256), BF16),
    ((2, 256), F32), ((2, 256), F32), ((2, D), F32), ((2, D), F32),
    ((4, 2, ROWS, 128), BF16), ((2, 2, ROWS, 128), BF16), ((4, 16, 128), F32),
    ((16, 8, 128), F32), ((16, 8, 128), F32), ((2, 2, 8, 128), F32), ((4, 8, 128), F32),
    ((2, ROWS, 128), F32), ((2, ROWS, 128), F32), ((4, ROWS, 128), F32),
    ((2, ROWS, 128), BF16), ((2, ROWS, 128), BF16), ((2, ROWS, 128), BF16), ((2, ROWS, 128), BF16),
    ((ROWS, 128), BF16), ((ROWS, 128), BF16), ((3, ROWS, 128), BF16),
    ((4, 32, 768), BF16), ((1024, 768), BF16), ((32, D), BF16), ((256, 512), BF16),
    ((3, 1024, 256), BF16), ((3, 4, 32, 128), BF16), ((3, 4, 2, 32, 256), BF16), ((3, 256, 256), BF16),
    ((8, 3, 96, 256), BF16), ((8, 3, 96, 256), BF16), ((3, 96, 256), F32),
    ((128, D), BF16), ((128, D), BF16), ((128, D), F32), ((4, 32, D), BF16), ((4, 32, D), BF16),
    ((512, 256), BF16), ((8, 32, 768), BF16), ((8, 32, 768), BF16), ((4, 32, 768), BF16), ((8, 2, 768), F32), ((4, 2, 768), F32),
    ((2, 2, 1536), F32), ((2, 1536), F32), ((16, 2, 1536), F32), ((4, 2, 1536), F32), ((2, 2, 1536), F32),
    ((3, 96, 256), BF16), ((3, 96, 256), BF16),
)


def body(
    video_q, video_k, video_v, video_out, video_dout, text_q, text_k, text_v, text_out, text_dout,
    video_lse, text_lse, video_norm, text_norm, video_mod, text_mod, video_weight, text_weight,
):
    args = [a[0] for a in (
        video_q, video_k, video_v, video_out, video_dout, text_q, text_k, text_v, text_out, text_dout,
        video_lse, text_lse, video_norm, text_norm, video_mod, text_mod)]
    args += [jnp.transpose(w, (1, 0, 2)) for w in (video_weight, text_weight)]
    vmem = pl.BlockSpec(memory_space=pltpu.VMEM)
    dn, tdn, wg, twg, vs, ts = pl.pallas_call(
        kernel,
        out_shape=(
            jax.ShapeDtypeStruct((32, D), BF16), jax.ShapeDtypeStruct((32, D), BF16),
            jax.ShapeDtypeStruct((3, 96, 256), F32), jax.ShapeDtypeStruct((3, 96, 256), F32),
            jax.ShapeDtypeStruct((2, D), F32), jax.ShapeDtypeStruct((2, D), F32),
        ),
        in_specs=[pl.BlockSpec(memory_space=pl.ANY)] * len(args),
        out_specs=(vmem,) * 6,
        scratch_shapes=[pltpu.VMEM(shape, kind) for shape, kind in SCRATCH] + [
            pltpu.SemaphoreType.DMA((len(NAMES),)),
            pltpu.SemaphoreType.DMA((len(NAMES),)),
            pltpu.SemaphoreType.DMA((len(LOCALS),)),
        ],
        compiler_params=pltpu.CompilerParams(has_side_effects=True, vmem_limit_bytes=60 * 1024 * 1024),
    )(*args)
    return (
        dn[None], tdn[None], jnp.transpose(wg, (1, 0, 2)), jnp.transpose(twg, (1, 0, 2)), vs[None], ts[None],
    )


def solution(mesh):
    tokens = P("dp", ("blk", "head"), None)
    text = P("dp", "head", None)
    whole = P("dp", None, None)
    columns = P(None, None, "head")
    return jax.shard_map(
        body,
        mesh=mesh,
        in_specs=(tokens,) * 5 + (text,) * 5 + (
            P("dp", "head", "blk"), P("dp", "head", None), tokens, text, whole, whole, columns, columns),
        out_specs=(
            tokens, text, P(("dp", "blk"), None, "head"), P(("dp", "blk"), None, "head"), whole, whole),
        check_vma=False,
    )
```

```python
import functools

import jax
import jax.numpy as jnp
from jax import lax
from jax.experimental import pallas as pl
from jax.experimental.pallas import tpu as pltpu
from jax.sharding import PartitionSpec as P

MESH = pl.DeviceIdType.MESH
D = 3072
DH = 128
SET = 512
ROWS = 544
TXT = 32
FACTOR = DH ** (-0.5)
LOG2E = 1.4426950408889634
F32 = jnp.float32
BF16 = jnp.bfloat16

NAMES = (
    "a_q", "a_d", "a_k", "a_v", "a_st", "a_lse", "a_tq", "a_td", "a_tk", "a_tv",
    "b_kv", "b_qc", "b_sc", "b_qz", "b_sz", "b_qf", "b_sf", "vin", "vf", "tin",
    "d_kv", "d_qc", "d_qz", "e0", "e1", "e2", "tz", "te", "w0", "w1", "w2",
    "bc0", "bc1", "bc2", "bc3", "bc4", "bc5", "by", "tr", "tdn", "ts", "tsx", "s1", "s2", "s3", "tw",
)
SEM = {name: index for index, name in enumerate(NAMES)}
LOCALS = ("out", "dout", "tout", "tdout", "nrm", "tnrm", "w", "tw", "lse", "tlse", "mod", "tmod")


def nt(left, right):
    return lax.dot_general(left, right, (((1,), (1,)), ((), ())), preferred_element_type=F32)


def tn(left, right):
    return lax.dot_general(left, right, (((0,), (0,)), ((), ())), preferred_element_type=F32)


def nn(left, right):
    return jnp.dot(left, right, preferred_element_type=F32)


def kernel(*refs):
    drains = []
    kernel_body(drains, *refs)
    drains[0]()


def kernel_body(
    drains,
    q, k, v, out, dout, tq, tk, tv, tout, tdout, lse, tlse, norm, tnorm, mod, tmod, weight, tweight,
    o_dn, o_tdn, o_wg, o_twg, o_vs, o_ts,
    l_out, l_dout, l_tout, l_tdout, l_nrm, l_tnrm, l_w, l_tw, l_lse, l_tlse, l_mod, l_tmod,
    qd, kv, st, d_send, d_recv, l_send, l_recv,
    gk_acc, gv_acc, gq_acc, dkv_s, dkv_r, dqc_s, dqc_r, dqz_s, dqz_r, g_fin,
    vin_s, vin_all, p_mod, gain_col, shift_col, m_acc, s_acc, tin_s, tin_all, gr, tz, tg, gs,
    w_send, w_recv, w_own, b_send, b_recv, b_own, y_send, y_recv,
    t_tmp, tr_send, tr_recv, tdn_all, ts_buf, tsx_buf, s1_buf, s2_buf, s3_buf, tw_s, tw_r,
    rs, ss, ls,
):
    dp = lax.axis_index("dp")
    blk = lax.axis_index("blk")
    head = lax.axis_index("head")
    z, x, y, c = blk // 4, blk % 4, head // 2, head % 2
    me = y * 4 + x
    mine = x // 2
    half = x % 2

    def dev(dz=None, dx=None, dy=None, dc=None, ddp=None):
        zz = z if dz is None else dz
        xx = x if dx is None else dx
        yy = y if dy is None else dy
        cc = c if dc is None else dc
        return {"dp": dp if ddp is None else ddp, "blk": zz * 4 + xx, "head": yy * 2 + cc}

    def remote(src, dst, name, to):
        return pltpu.make_async_remote_copy(
            src_ref=src, dst_ref=dst, send_sem=ss.at[SEM[name]], recv_sem=rs.at[SEM[name]],
            device_id=to, device_id_type=MESH)

    def local(src, dst, name):
        return pltpu.make_async_copy(src, dst, rs.at[SEM[name]])

    def got(ref, name):
        pltpu.make_async_copy(ref, ref, rs.at[SEM[name]]).wait()
        if name in expected:
            expected[name].pop(0)

    def sent(ref, name):
        pltpu.make_async_copy(ref, ref, ss.at[SEM[name]]).wait()

    expected = {}
    copies = {}
    leaving = []

    def expect(name, *refs):
        expected[name] = list(refs)

    def drain():
        for name, refs in list(expected.items()):
            for ref in list(refs):
                got(ref, name)
        for n_, cp in list(copies.items()):
            if n_ not in waited:
                cp.wait()
        for fn in leaving:
            fn()

    waited = set()
    drains.append(drain)

    def ready(name):
        copies[name].wait()
        waited.add(name)

    def leave(ref, name, times=1):
        def fn():
            for _ in range(times):
                sent(ref, name)
        leaving.append(fn)

    def leave_if(cond, ref, name, times=1):
        def fn():
            @pl.when(cond)
            def _():
                for _ in range(times):
                    sent(ref, name)
        leaving.append(fn)

    def rows32(index):
        return pl.ds(pl.multiple_of(index * 32, 32), 32)

    def lanes(index, width=128):
        return pl.ds(pl.multiple_of(index * width, 128), width)

    barrier = pltpu.get_barrier_semaphore()

    def greet(t, carry):
        hd, xx = t // 4, t % 4

        @pl.when(jnp.logical_or(hd != head, xx != x))
        def _():
            pl.semaphore_signal(barrier, inc=1, device_id=dev(dx=xx, dy=hd // 2, dc=hd % 2), device_id_type=MESH)
        return carry

    def greet_line(t, carry):
        @pl.when(t != dp * 4 + z)
        def _():
            pl.semaphore_signal(barrier, inc=1, device_id=dev(ddp=t // 4, dz=t % 4), device_id_type=MESH)
        return carry

    lax.fori_loop(0, 32, greet, 0)
    lax.fori_loop(0, 8, greet_line, 0)
    pl.semaphore_wait(barrier, 38)

    def send_a(table):
        def step(t, carry):
            to = dev(dx=t % 4, dy=t // 4)
            for src, dst, name in table:
                piece = src.at[:, lanes(t)]
                place = dst.at[rows32(me)]

                @pl.when(t != me)
                def _():
                    remote(piece, place, name, to).start()

                @pl.when(t == me)
                def _():
                    local(piece, place, name).start()
            return carry

        lax.fori_loop(0, 16, step, 0)

    def send_text(table):
        @pl.when(y == z)
        def _():
            for t in range(4):
                for src, dst, name in table:
                    piece = src.at[:, lanes(4 * t + x)]
                    place = dst.at[pl.ds(SET, TXT)]

                    @pl.when(t != y)
                    def _():
                        remote(piece, place, name, dev(dy=t)).start()

                    @pl.when(t == y)
                    def _():
                        local(piece, place, name).start()

    send_a(((k, kv.at[0, 0], "a_k"), (v, kv.at[0, 1], "a_v")))
    send_text(((tk, kv.at[0, 0], "a_tk"), (tv, kv.at[0, 1], "a_tv")))
    send_a(((q, qd.at[0, 0], "a_q"), (dout, qd.at[0, 1], "a_d")))
    send_text(((tq, qd.at[0, 0], "a_tq"), (tdout, qd.at[0, 1], "a_td")))
    for name, ref in (("a_k", kv.at[0, 0, pl.ds(0, SET)]), ("a_v", kv.at[0, 1, pl.ds(0, SET)]),
                      ("a_q", qd.at[0, 0, pl.ds(0, SET)]), ("a_d", qd.at[0, 1, pl.ds(0, SET)])):
        expect(name, ref)
        leave(kv.at[0, 0, pl.ds(0, 480)], name)
    for name, ref in (("a_tk", kv.at[0, 0, pl.ds(SET, TXT)]), ("a_tv", kv.at[0, 1, pl.ds(SET, TXT)]),
                      ("a_tq", qd.at[0, 0, pl.ds(SET, TXT)]), ("a_td", qd.at[0, 1, pl.ds(SET, TXT)])):
        expect(name, ref)
        leave_if(y == z, kv.at[0, 0, pl.ds(0, 96)], name)

    loads = {
        "out": (out, l_out), "dout": (dout, l_dout), "tout": (tout, l_tout), "tdout": (tdout, l_tdout),
        "nrm": (norm, l_nrm), "tnrm": (tnorm, l_tnrm), "lse": (lse, l_lse), "tlse": (tlse, l_tlse),
        "mod": (mod, l_mod), "tmod": (tmod, l_tmod), "w": (weight, l_w),
        "tw": (tweight.at[:, pl.ds(pl.multiple_of(x * 768, 768), 768), :], l_tw),
    }
    copies.update({n: pltpu.make_async_copy(s, d, ls.at[LOCALS.index(n)]) for n, (s, d) in loads.items()})
    for name in ("out", "dout", "lse", "tlse", "tout", "tdout", "nrm", "mod", "tnrm", "tmod", "w", "tw"):
        copies[name].start()


    lane = lax.broadcasted_iota(jnp.int32, (16, 128), 1)
    ones = jnp.where(
        lax.broadcasted_iota(jnp.int32, (16, 2048), 1) // DH
        == lax.broadcasted_iota(jnp.int32, (16, 2048), 0), 1.0, 0.0).astype(BF16)

    def delta_rows(a_ref, b_ref):
        total = jnp.zeros((16, 128), F32)
        products = a_ref[...].astype(F32) * b_ref[...].astype(F32)
        high = products.astype(BF16)
        low = (products - high.astype(F32)).astype(BF16)
        for part in (high, low):
            total = total + nt(ones, jnp.concatenate([part] * 4, axis=0))
        return total

    ready("out")
    ready("dout")
    video_delta = jnp.where(lane // 32 == x, delta_rows(l_out, l_dout), 0.0)
    ready("tout")
    ready("tdout")
    text_delta = jnp.where(lane < 32, delta_rows(l_tout, l_tdout), 0.0)
    d_send[...] = jnp.zeros_like(d_send)
    for h in range(16):
        d_send[h, 0:1, :] = video_delta[h:h + 1, :]
        d_send[h, 1:2, :] = text_delta[h:h + 1, :]

    def send_delta(t, carry):
        @pl.when(t != me)
        def _():
            remote(d_send.at[t], d_recv.at[me], "a_st", dev(dx=t % 4, dy=t // 4)).start()

        @pl.when(t == me)
        def _():
            local(d_send.at[t], d_recv.at[me], "a_st").start()
        return carry

    lax.fori_loop(0, 16, send_delta, 0)
    expect("a_st", d_recv)
    leave(d_recv.at[pl.ds(0, 15)], "a_st")

    ready("lse")
    ready("tlse")
    lane8 = lax.broadcasted_iota(jnp.int32, (8, 128), 1)
    l_send[...] = jnp.zeros_like(l_send)
    for j in range(2):
        for cc in range(2):
            for yy in range(4):
                row = jnp.broadcast_to(l_lse[j:j + 1, 128 * (yy // 2):128 * (yy // 2) + 128], (8, 128))
                shift = (32 * x + 256 - (yy % 2) * 64 - cc * 32) % 128
                row = jnp.where(lane8 // 32 == x, pltpu.roll(row, shift, 1), 0.0)
                l_send[j, cc, yy:yy + 1, :] = row[0:1, :]
            row = jnp.broadcast_to(l_tlse[j:j + 1, pl.ds(pl.multiple_of((z // 2) * 128, 128), 128)], (8, 128))
            shift = (256 - (z % 2) * 64 - cc * 32) % 128
            row = jnp.where(lane8 < 32, pltpu.roll(row, shift, 1), 0.0)
            l_send[j, cc, 4:5, :] = row[0:1, :]
    for j in range(2):
        for cc in range(2):
            own = jnp.logical_and(x == 2 * c + j, c == cc)

            @pl.when(jnp.logical_not(own))
            def _():
                remote(l_send.at[j, cc], l_recv.at[x], "a_lse", dev(dx=2 * c + j, dc=cc)).start()

            @pl.when(own)
            def _():
                local(l_send.at[j, cc], l_recv.at[x], "a_lse").start()

    expect("a_lse", l_recv)
    leave_if(c == mine, l_recv.at[pl.ds(0, 3)], "a_lse")
    leave_if(c != mine, l_recv, "a_lse")

    ready("nrm")
    ready("mod")

    def group(value, xx):
        return jnp.concatenate([value[:, 384 * m + 96 * xx:384 * m + 96 * xx + 96] for m in range(8)], axis=1)

    nrm = l_nrm[...].astype(F32)
    for xx in range(4):
        vin_s[xx] = group(nrm, xx).astype(BF16)
        p_mod[xx, 0:2, :] = group(l_mod[...], xx)
    ready("tnrm")
    ready("tmod")
    tgain = 1.0 + l_tmod[1:2, :]
    tin_s[...] = (tgain * l_tnrm[...].astype(F32) + l_tmod[0:1, :]).astype(BF16)

    gk_acc[...] = jnp.zeros_like(gk_acc)
    gv_acc[...] = jnp.zeros_like(gv_acc)
    gq_acc[...] = jnp.zeros_like(gq_acc)

    got(kv.at[0, 0, pl.ds(0, SET)], "a_k")
    got(kv.at[0, 1, pl.ds(0, SET)], "a_v")
    got(kv.at[0, 0, pl.ds(SET, TXT)], "a_tk")
    got(kv.at[0, 1, pl.ds(SET, TXT)], "a_tv")
    zn = z + 1 - 2 * (z % 2)
    zf = (z + 2) % 4
    remote(kv.at[0], kv.at[1], "b_kv", dev(dz=zn)).start()
    expect("b_kv", kv.at[1])
    leave(kv.at[0], "b_kv")
    got(qd.at[0, 0, pl.ds(0, SET)], "a_q")
    got(qd.at[0, 1, pl.ds(0, SET)], "a_d")
    got(qd.at[0, 0, pl.ds(SET, TXT)], "a_tq")
    got(qd.at[0, 1, pl.ds(SET, TXT)], "a_td")
    remote(qd.at[0], qd.at[1], "b_qz", dev(dz=zf)).start()
    remote(qd.at[0], qd.at[2], "b_qc", dev(dc=1 - c)).start()
    expect("b_qc", qd.at[2])
    expect("b_qz", qd.at[1])
    leave(qd.at[0], "b_qc")
    leave(qd.at[0], "b_qz")
    got(d_recv, "a_st")
    got(l_recv, "a_lse")
    for yy in range(4):
        st[0, yy:yy + 1, :] = LOG2E * (l_recv[0, yy:yy + 1, :] + l_recv[1, yy:yy + 1, :]
                                       + l_recv[2, yy:yy + 1, :] + l_recv[3, yy:yy + 1, :])
        st[0, 4 + yy:5 + yy, :] = (d_recv[4 * yy, 0:1, :] + d_recv[4 * yy + 1, 0:1, :]
                                   + d_recv[4 * yy + 2, 0:1, :] + d_recv[4 * yy + 3, 0:1, :])
    st[0, 8:9, :] = LOG2E * l_recv[0, 4:5, :]
    st[0, 9:10, :] = d_recv[z * 4 + x, 1:2, :]
    st[0, 10:16, :] = jnp.zeros((6, 128), F32)
    remote(st.at[0], st.at[1], "b_sz", dev(dz=zf)).start()
    remote(st.at[0], st.at[2], "b_sc", dev(dc=1 - c)).start()
    expect("b_sc", st.at[2])
    expect("b_sz", st.at[1])
    leave(st.at[0], "b_sc")
    leave(st.at[0], "b_sz")

    def send_vin(t, carry):
        place = vin_all.at[pl.ds(pl.multiple_of(c * SET + me * 32, 32), 32)]

        @pl.when(t != me)
        def _():
            remote(vin_s.at[t % 4], place, "vin", dev(dx=t % 4, dy=t // 4)).start()

        @pl.when(t == me)
        def _():
            local(vin_s.at[t % 4], place, "vin").start()
        return carry

    lax.fori_loop(0, 16, send_vin, 0)
    own_rows = pl.ds(pl.multiple_of(c * SET, SET), SET)
    expect("vin", vin_all.at[own_rows])
    leave(vin_all.at[pl.ds(0, 15 * 32)], "vin")

    window = jnp.minimum((blk * 96) // 128 * 128, 1280)

    def send_tin(hd, carry):
        for other in range(2):
            piece = tin_s.at[:, pl.ds(pl.multiple_of(other * 1536 + window, 128), 256)]
            place = tin_all.at[rows32(head), pl.ds(other * 256, 256)]

            @pl.when(hd != head)
            def _():
                remote(piece, place, "tin", dev(dy=hd // 2, dc=hd % 2)).start()

            @pl.when(hd == head)
            def _():
                local(piece, place, "tin").start()
        return carry

    lax.fori_loop(0, 8, send_tin, 0)
    expect("tin", tin_all)
    leave(tin_all.at[pl.ds(0, 7 * 32)], "tin")

    def pair(lse_row, delta_row, query, dquery, keys, values):
        probs = jnp.exp2(nt(keys, query) * (FACTOR * LOG2E) - lse_row)
        dscores = (probs * (nt(values, dquery) - delta_row)).astype(BF16)
        return probs.astype(BF16), dscores

    def row512(i, first):
        return jnp.concatenate([st[i, first + n:first + n + 1, :] for n in range(4)], axis=1)

    def attend(step, carry):
        i = (step % 2) * 2 + step // 4
        j = ((step + 2) // 4) % 2

        @pl.when(step == 1)
        def _():
            got(qd.at[2], "b_qc")
            got(st.at[2], "b_sc")

        @pl.when(step == 2)
        def _():
            got(kv.at[1], "b_kv")

        @pl.when(step == 4)
        def _():
            got(qd.at[1], "b_qz")
            remote(qd.at[1], qd.at[3], "b_qf", dev(dc=1 - c)).start()
            got(st.at[1], "b_sz")
            remote(st.at[1], st.at[3], "b_sf", dev(dc=1 - c)).start()

        @pl.when(step == 5)
        def _():
            got(qd.at[3], "b_qf")
            got(st.at[3], "b_sf")

        query, dquery = qd[i, 0, 0:SET, :], qd[i, 1, 0:SET, :]
        keys, values = kv[j, 0], kv[j, 1]
        probs, dscores = pair(row512(i, 0), row512(i, 4), query, dquery, keys, values)
        gv_acc[j] += nn(probs, dquery)
        gk_acc[j] += nn(dscores, query)
        gq_acc[i, 0:SET, :] += tn(dscores, keys)
        return carry

    def attend_text(j):
        query = jnp.concatenate([qd[i, 0, SET:ROWS, :] for i in range(4)], axis=0)
        dquery = jnp.concatenate([qd[i, 1, SET:ROWS, :] for i in range(4)], axis=0)
        lse_row = jnp.zeros((8, 128), F32)
        delta_row = jnp.zeros((8, 128), F32)
        for i in range(4):
            one, two = (jnp.broadcast_to(st[i, r:r + 1, :], (8, 128)) for r in (8, 9))
            lse_row = lse_row + (pltpu.roll(one, 32 * i, 1) if i else one)
            delta_row = delta_row + (pltpu.roll(two, 32 * i, 1) if i else two)
        keys, values = kv[j, 0], kv[j, 1]
        probs, dscores = pair(lse_row[0:1, :], delta_row[0:1, :], query, dquery, keys, values)
        gv_acc[j] += nn(probs, dquery)
        gk_acc[j] += nn(dscores, query)
        from_text = tn(dscores, keys)
        for i in range(4):
            gq_acc[i, SET:ROWS, :] += from_text[32 * i:32 * i + 32, :]

    lax.fori_loop(0, 6, attend, 0)
    leave(qd.at[0], "b_qf")
    leave(st.at[0], "b_sf")
    attend_text(1)
    dkv_s[0] = (gk_acc[1] * FACTOR).astype(BF16)
    dkv_s[1] = gv_acc[1].astype(BF16)
    remote(dkv_s, dkv_r, "d_kv", dev(dz=zn)).start()
    expect("d_kv", dkv_r)
    leave(dkv_s, "d_kv")
    got(vin_all.at[own_rows], "vin")
    remote(vin_all.at[own_rows], vin_all.at[own_rows], "vf", dev(dc=1 - c)).start()
    expect("vf", vin_all.at[own_rows])
    leave(vin_all.at[own_rows], "vf")
    lax.fori_loop(6, 8, attend, 0)
    attend_text(0)
    dqc_s[0] = (gq_acc[2] * FACTOR).astype(BF16)
    dqc_s[1] = (gq_acc[3] * FACTOR).astype(BF16)
    remote(dqc_s, dqc_r, "d_qc", dev(dc=1 - c)).start()
    expect("d_qc", dqc_r)
    leave(dqc_s, "d_qc")
    got(dqc_r, "d_qc")
    dqz_s[...] = (gq_acc[1] * FACTOR + dqc_r[1].astype(F32)).astype(BF16)
    remote(dqz_s, dqz_r, "d_qz", dev(dz=zf)).start()
    expect("d_qz", dqz_r)
    leave(dqz_s, "d_qz")

    def send_grads(ch):
        for xx in range(4):
            own = jnp.logical_and(x == xx, c == mine)
            piece = g_fin.at[ch, pl.ds(0, SET)]
            place = gr.at[ch, pl.ds(pl.multiple_of(c * SET, SET), SET), lanes(half)]

            @pl.when(jnp.logical_not(own))
            def _():
                remote(piece, place, "e%d" % ch, dev(dx=xx, dc=mine)).start()

            @pl.when(own)
            def _():
                local(piece, place, "e%d" % ch).start()

    got(dkv_r, "d_kv")
    g_fin[1] = (gk_acc[0] * FACTOR + dkv_r[0].astype(F32)).astype(BF16)
    send_grads(1)
    g_fin[2] = (gv_acc[0] + dkv_r[1].astype(F32)).astype(BF16)
    send_grads(2)
    got(dqz_r, "d_qz")
    g_fin[0] = (gq_acc[0] * FACTOR + dqc_r[0].astype(F32) + dqz_r[...].astype(F32)).astype(BF16)
    send_grads(0)
    for ch in range(3):
        name = "e%d" % ch
        expect(name, gr.at[ch])
        leave_if(c == mine, kv.at[:, 0, pl.ds(0, SET)], name)
        leave_if(c == mine, kv.at[0, 0, pl.ds(0, SET)], name)
        leave_if(c != mine, gr.at[ch], name)

    for zz in range(4):
        piece = g_fin.at[:, pl.ds(SET, TXT)]

        @pl.when(z != zz)
        def _():
            remote(piece, tz.at[:, z], "tz", dev(dz=zz)).start()

        @pl.when(z == zz)
        def _():
            local(piece, tz.at[:, z], "tz").start()
    got(tz, "tz")
    leave(tz.at[:, pl.ds(0, 3)], "tz")
    for xx in range(4):
        own = jnp.logical_and(x == xx, c == mine)
        place = tg.at[:, :, c, :, lanes(half)]

        @pl.when(jnp.logical_not(own))
        def _():
            remote(tz, place, "te", dev(dx=xx, dc=mine)).start()

        @pl.when(own)
        def _():
            local(tz, place, "te").start()

    expect("te", tg)
    leave_if(c == mine, tz, "te", 3)
    leave_if(c != mine, tz, "te", 4)

    pos = dp * 4 + z
    wide = jnp.ones((8, 1024), BF16)

    def project(ch):
        if ch:
            got(gr.at[ch], "e%d" % ch)
        grads = gr[ch]
        m_acc[...] = tn(vin_all[...], grads)
        col = nn(wide, grads)[0:1, :]
        for other in range(8):
            rows = slice(96 * other, 96 * other + 96)
            part = m_acc[rows, :]
            gain = jnp.concatenate([gain_col[rows, :]] * 2, axis=1)
            shift = jnp.concatenate([shift_col[rows, :]] * 2, axis=1)
            term = gain * part + shift * col
            w_send[other, ch] = term.astype(BF16)

            @pl.when(pos != other)
            def _():
                remote(w_send.at[other, ch], w_recv.at[pos, ch], "w%d" % ch,
                       dev(ddp=other // 4, dz=other % 4)).start()

            @pl.when(pos == other)
            def _():
                w_own[ch] = term
        expect("w%d" % ch, w_recv.at[pl.ds(0, 7), ch])
        leave(w_recv.at[pl.ds(0, 7), ch], "w%d" % ch)
        for other in range(8):
            rows = slice(96 * other, 96 * other + 96)
            first = pl.multiple_of((other // 4) * 1536 + (other % 4) * 384 + x * 96, 32)
            wq = l_w[ch, pl.ds(first, 96), :].astype(F32)
            zero, one = wq * col, wq * m_acc[rows, :]
            s_acc[0, rows, :] += zero[:, 0:128] + zero[:, 128:256]
            s_acc[1, rows, :] += one[:, 0:128] + one[:, 128:256]

    quarter = jnp.broadcast_to(p_mod[x, 0:1, :], (128, 768))
    shift_col[...] = jnp.transpose(quarter)
    quarter = jnp.broadcast_to(1.0 + p_mod[x, 1:2, :], (128, 768))
    gain_col[...] = jnp.transpose(quarter)
    s_acc[...] = jnp.zeros_like(s_acc)
    ready("w")
    got(vin_all.at[own_rows], "vf")
    project(1)
    project(2)

    got(gr.at[0], "e0")

    for ch in range(3):
        for cc in range(2):
            for yy in range(4):
                first = pl.multiple_of(cc * SET + (yy * 4 + x) * 32, 32)
                gs[ch, cc * 128 + yy * 32:cc * 128 + yy * 32 + 32, :] = gr[ch, pl.ds(first, 32), :]
    def gather_chunk(n):
        cols = slice(512 * n, 512 * n + 512)
        got(b_recv.at[:, cols], "bc%d" % n)
        total = b_own[:, cols] + b_recv[:, cols].astype(F32)
        b_own[:, cols] = total
        for yy in range(4):
            y_send[yy, :, cols] = total[32 * yy:32 * yy + 32, :].astype(BF16)

            @pl.when(yy != y)
            def _():
                remote(y_send.at[yy, :, cols], y_recv.at[y, :, cols], "by", dev(dy=yy)).start()

    for n in range(6):
        cols = slice(512 * n, 512 * n + 512)
        term = (nt(gs[0], l_w[0, cols, :]) + nt(gs[1], l_w[1, cols, :]) + nt(gs[2], l_w[2, cols, :]))

        @pl.when(c == 0)
        def _():
            b_own[:, cols] = term[0:128, :]
            b_send[:, cols] = term[128:256, :].astype(BF16)

        @pl.when(c == 1)
        def _():
            b_own[:, cols] = term[128:256, :]
            b_send[:, cols] = term[0:128, :].astype(BF16)
        remote(b_send.at[:, cols], b_recv.at[:, cols], "bc%d" % n, dev(dc=1 - c)).start()
        leave(b_send.at[:, cols], "bc%d" % n)
        if n:
            gather_chunk(n - 1)
    gather_chunk(5)
    expect("by", y_recv.at[pl.ds(0, 3)])
    leave(y_send.at[pl.ds(0, 3)], "by")
    project(0)
    for n in range(2):
        s1_buf[head, n:n + 1, :] = jnp.sum(jnp.transpose(s_acc[n]), axis=0, keepdims=True)
    for hd in range(8):
        @pl.when(hd != head)
        def _():
            remote(s1_buf.at[head], s1_buf.at[head], "s1", dev(dy=hd // 2, dc=hd % 2)).start()
    expect("s1", s1_buf.at[pl.ds(0, 7)])
    leave(s1_buf.at[pl.ds(0, 7)], "s1")

    got(tg, "te")
    got(tin_all, "tin")
    first = pl.multiple_of(blk * 96 - window, 32)
    for ch in range(3):
        grads = tg[ch].reshape(256, 256)
        term = tn(tin_all[...], grads)
        t_tmp[...] = term.astype(BF16)
        away = pl.multiple_of((1 - dp) * 256 + first, 32)
        near = pl.multiple_of(dp * 256 + first, 32)
        tw_s[ch] = t_tmp[pl.ds(away, 96), :]
        o_twg[ch] = t_tmp[pl.ds(near, 96), :].astype(F32)
    remote(tw_s, tw_r, "tw", dev(ddp=1 - dp)).start()
    expect("tw", tw_r)
    leave(tw_s, "tw")
    ready("tw")
    term = (nt(tg[0].reshape(256, 256), l_tw[0]) + nt(tg[1].reshape(256, 256), l_tw[1])
            + nt(tg[2].reshape(256, 256), l_tw[2]))
    for hd in range(8):
        tr_send[hd] = term[32 * hd:32 * hd + 32, :].astype(BF16)

        @pl.when(hd != head)
        def _():
            remote(tr_send.at[hd], tr_recv.at[head], "tr", dev(dy=hd // 2, dc=hd % 2)).start()

        @pl.when(hd == head)
        def _():
            local(tr_send.at[hd], tr_recv.at[head], "tr").start()

    expect("tr", tr_recv)
    leave(tr_recv.at[pl.ds(0, 7)], "tr")

    got(s1_buf.at[pl.ds(0, 7)], "s1")
    stat = s1_buf[0]
    for hd in range(1, 8):
        stat = stat + s1_buf[hd]
    s2_buf[z] = stat
    for zz in range(4):
        @pl.when(zz != z)
        def _():
            remote(s2_buf.at[z], s2_buf.at[z], "s2", dev(dz=zz)).start()
    expect("s2", s2_buf.at[pl.ds(0, 3)])
    leave(s2_buf.at[pl.ds(0, 3)], "s2")

    got(tr_recv, "tr")
    tback = tr_recv[0].astype(F32)
    for hd in range(1, 8):
        tback = tback + tr_recv[hd].astype(F32)
    cols = pl.ds(pl.multiple_of(x * 768, 768), 768)
    tdn_all[x] = ((1.0 + l_tmod[1:2, cols]) * tback).astype(BF16)
    tnf = l_tnrm[:, cols].astype(F32)
    ts_buf[head] = jnp.concatenate([jnp.sum(tback, axis=0, keepdims=True),
                                    jnp.sum(tback * tnf, axis=0, keepdims=True)], axis=0)
    for xx in range(4):
        @pl.when(xx != x)
        def _():
            remote(tdn_all.at[x], tdn_all.at[x], "tdn", dev(dx=xx)).start()
    expect("tdn", tdn_all.at[pl.ds(0, 3)])
    leave(tdn_all.at[pl.ds(0, 3)], "tdn")
    for hd in range(8):
        @pl.when(hd != head)
        def _():
            remote(ts_buf.at[head], ts_buf.at[head], "ts", dev(dy=hd // 2, dc=hd % 2)).start()
    leave(ts_buf.at[pl.ds(0, 7)], "ts")
    got(s2_buf.at[pl.ds(0, 3)], "s2")
    s3_buf[x] = s2_buf[0] + s2_buf[1] + s2_buf[2] + s2_buf[3]
    for xx in range(4):
        @pl.when(xx != x)
        def _():
            remote(s3_buf.at[x], s3_buf.at[x], "s3", dev(dx=xx)).start()
    expect("s3", s3_buf.at[pl.ds(0, 3)])
    leave(s3_buf.at[pl.ds(0, 3)], "s3")
    got(ts_buf.at[pl.ds(0, 7)], "ts")
    tstat = ts_buf[0]
    for hd in range(1, 8):
        tstat = tstat + ts_buf[hd]
    tsx_buf[x] = tstat
    for xx in range(4):
        @pl.when(xx != x)
        def _():
            remote(tsx_buf.at[x], tsx_buf.at[x], "tsx", dev(dx=xx)).start()
    expect("tsx", tsx_buf.at[pl.ds(0, 3)])
    leave(tsx_buf.at[pl.ds(0, 3)], "tsx")


    got(y_recv.at[pl.ds(0, 3)], "by")
    back = b_own[rows32(y), :]
    for yy in range(4):
        back = back + jnp.where(yy == y, 0.0, y_recv[yy].astype(F32))
    o_dn[...] = ((1.0 + l_mod[1:2, :]) * back).astype(BF16)
    got(s3_buf.at[pl.ds(0, 3)], "s3")
    for m in range(8):
        o_vs[:, 384 * m:384 * m + 384] = jnp.concatenate(
            [s3_buf[xx, 0:2, 96 * m:96 * m + 96] for xx in range(4)], axis=1)

    got(tdn_all.at[pl.ds(0, 3)], "tdn")
    got(tsx_buf.at[pl.ds(0, 3)], "tsx")
    for xx in range(4):
        o_tdn[:, 768 * xx:768 * xx + 768] = tdn_all[xx]
        o_ts[:, 768 * xx:768 * xx + 768] = tsx_buf[xx]
    got(tw_r, "tw")
    o_twg[...] += tw_r[...].astype(F32)

    for ch in (1, 2, 0):
        got(w_recv.at[pl.ds(0, 7), 0], "w%d" % ch)
        total = w_own[ch]
        for other in range(8):
            total = total + jnp.where(pos == other, 0.0, w_recv[other, ch].astype(F32))
        o_wg[ch] = total

def finish(*refs):
    into = [pltpu.make_async_copy(refs[n], refs[12 + n], refs[18].at[n]) for n in range(6)]
    back = [pltpu.make_async_copy(refs[12 + n], refs[6 + n], refs[18].at[n]) for n in range(6)]
    for copy in into:
        copy.start()
    for first, second in zip(into, back):
        first.wait()
        second.start()
    for copy in back:
        copy.wait()


SCRATCH = (
    ((32, 2048), BF16), ((32, 2048), BF16), ((32, 2048), BF16), ((32, 2048), BF16),
    ((32, D), BF16), ((32, D), BF16), ((3, D, 256), BF16), ((3, 768, 256), BF16),
    ((2, 256), F32), ((2, 256), F32), ((2, D), F32), ((2, D), F32),
    ((4, 2, ROWS, 128), BF16), ((2, 2, ROWS, 128), BF16), ((4, 16, 128), F32),
    ((16, 8, 128), F32), ((16, 8, 128), F32), ((2, 2, 8, 128), F32), ((4, 8, 128), F32),
    ((2, ROWS, 128), F32), ((2, ROWS, 128), F32), ((4, ROWS, 128), F32),
    ((2, ROWS, 128), BF16), ((2, ROWS, 128), BF16), ((2, ROWS, 128), BF16), ((2, ROWS, 128), BF16),
    ((ROWS, 128), BF16), ((ROWS, 128), BF16), ((3, ROWS, 128), BF16),
    ((4, 32, 768), BF16), ((1024, 768), BF16), ((4, 8, 768), F32), ((768, 128), F32), ((768, 128), F32),
    ((768, 256), F32), ((2, 768, 128), F32), ((32, D), BF16), ((256, 512), BF16),
    ((3, 1024, 256), BF16), ((3, 4, 32, 128), BF16), ((3, 4, 2, 32, 256), BF16), ((3, 256, 256), BF16),
    ((8, 3, 96, 256), BF16), ((8, 3, 96, 256), BF16), ((3, 96, 256), F32),
    ((128, D), BF16), ((128, D), BF16), ((128, D), F32), ((4, 32, D), BF16), ((4, 32, D), BF16),
    ((512, 256), BF16), ((8, 32, 768), BF16), ((8, 32, 768), BF16), ((4, 32, 768), BF16), ((8, 2, 768), F32), ((4, 2, 768), F32),
    ((8, 8, 768), F32), ((4, 8, 768), F32), ((4, 8, 768), F32),
    ((3, 96, 256), BF16), ((3, 96, 256), BF16),
)


def body(
    video_q, video_k, video_v, video_out, video_dout, text_q, text_k, text_v, text_out, text_dout,
    video_lse, text_lse, video_norm, text_norm, video_mod, text_mod, video_weight, text_weight,
):
    args = [a[0] for a in (
        video_q, video_k, video_v, video_out, video_dout, text_q, text_k, text_v, text_out, text_dout,
        video_lse, text_lse, video_norm, text_norm, video_mod, text_mod)]
    args += [jnp.transpose(w, (1, 0, 2)) for w in (video_weight, text_weight)]
    vmem = pl.BlockSpec(memory_space=pltpu.VMEM)
    results = pl.pallas_call(
        kernel,
        out_shape=(
            jax.ShapeDtypeStruct((32, D), BF16), jax.ShapeDtypeStruct((32, D), BF16),
            jax.ShapeDtypeStruct((3, 96, 256), F32), jax.ShapeDtypeStruct((3, 96, 256), F32),
            jax.ShapeDtypeStruct((2, D), F32), jax.ShapeDtypeStruct((2, D), F32),
        ),
        in_specs=[pl.BlockSpec(memory_space=pl.ANY)] * len(args),
        out_specs=(vmem,) * 6,
        scratch_shapes=[pltpu.VMEM(shape, kind) for shape, kind in SCRATCH] + [
            pltpu.SemaphoreType.DMA((len(NAMES),)),
            pltpu.SemaphoreType.DMA((len(NAMES),)),
            pltpu.SemaphoreType.DMA((len(LOCALS),)),
        ],
        compiler_params=pltpu.CompilerParams(collective_id=0, has_side_effects=True, vmem_limit_bytes=60 * 1024 * 1024),
    )(*args)
    anywhere = pl.BlockSpec(memory_space=pl.ANY)
    dn, tdn, wg, twg, vs, ts = pl.pallas_call(
        finish,
        out_shape=[jax.ShapeDtypeStruct(r.shape, r.dtype) for r in results],
        in_specs=[anywhere] * 6,
        out_specs=[anywhere] * 6,
        scratch_shapes=[pltpu.VMEM(r.shape, r.dtype) for r in results] + [pltpu.SemaphoreType.DMA((6,))],
        compiler_params=pltpu.CompilerParams(vmem_limit_bytes=60 * 1024 * 1024),
    )(*results)
    return (
        dn[None], tdn[None], jnp.transpose(wg, (1, 0, 2)), jnp.transpose(twg, (1, 0, 2)), vs[None], ts[None],
    )


def solution(mesh):
    tokens = P("dp", ("blk", "head"), None)
    text = P("dp", "head", None)
    whole = P("dp", None, None)
    columns = P(None, None, "head")
    return jax.shard_map(
        body,
        mesh=mesh,
        in_specs=(tokens,) * 5 + (text,) * 5 + (
            P("dp", "head", "blk"), P("dp", "head", None), tokens, text, whole, whole, columns, columns),
        out_specs=(
            tokens, text, P(("dp", "blk"), None, "head"), P(("dp", "blk"), None, "head"), whole, whole),
        check_vma=False,
    )
```

```python
import functools

import jax
import jax.numpy as jnp
from jax import lax
from jax.experimental import pallas as pl
from jax.experimental.pallas import tpu as pltpu
from jax.sharding import PartitionSpec as P

MESH = pl.DeviceIdType.MESH
D = 3072
DH = 128
SET = 512
ROWS = 544
TXT = 32
FACTOR = DH ** (-0.5)
LOG2E = 1.4426950408889634
F32 = jnp.float32
BF16 = jnp.bfloat16

NAMES = (
    "a_q", "a_d", "a_k", "a_v", "a_st", "a_lse", "a_tq", "a_td", "a_tk", "a_tv",
    "b_kv", "b_qc", "b_sc", "b_qz", "b_sz", "b_qf", "b_sf", "v0", "wq", "tin", "tq",
    "d_kv", "d_qc", "d_qz", "gkv", "gq", "e", "tz", "te",
    "bc0", "bc1", "bc2", "bc3", "bc4", "bc5", "by", "tr", "tdn", "ts", "tsx", "s1", "s2", "s3", "tw", "fin",
)
RING = tuple("r%d%d%d" % (way, step, ch) for way in range(2) for step in range(4) for ch in range(3))
INPUTS = tuple("v1%d%d" % (t, n) for t in (1, 2, 3) for n in range(4)) + tuple("v2%d" % n for n in range(4))
NAMES = NAMES + RING + INPUTS
SEM = {name: index for index, name in enumerate(NAMES)}
LOCALS = ("out", "dout", "tout", "tdout", "nrm", "tnrm", "w", "tw", "lse", "tlse", "mod", "tmod")


def nt(left, right):
    return lax.dot_general(left, right, (((1,), (1,)), ((), ())), preferred_element_type=F32)


def tn(left, right):
    return lax.dot_general(left, right, (((0,), (0,)), ((), ())), preferred_element_type=F32)


def nn(left, right):
    return jnp.dot(left, right, preferred_element_type=F32)


def kernel(*refs):
    drains = []
    kernel_body(drains, *refs)
    drains[0]()


def kernel_body(
    drains,
    q, k, v, out, dout, tq, tk, tv, tout, tdout, lse, tlse, norm, tnorm, mod, tmod, weight, tweight,
    r_dn, r_tdn, r_wg, r_twg, r_vs, r_ts,
    o_dn, o_tdn, o_wg, o_twg, o_vs, o_ts,
    l_out, l_dout, l_tout, l_tdout, l_nrm, l_tnrm, l_w, l_tw, l_lse, l_tlse, l_mod, l_tmod,
    qd, kv, st, d_send, d_recv, l_send, l_recv,
    gk_acc, gv_acc, gq_acc, dkv_s, dkv_r, dqc_s, dqc_r, dqz_s, dqz_r, gw, g_txt,
    vin_s, vin_all, wq, gain_col, shift_col, m_acc, s_acc, tin_s, tin_all, tq_all, tz, tg, gs,
    wt, ring_s, ring_r, fin_s, fin_r, b_send, b_recv, b_own, y_send, y_recv,
    t_tmp, tr_send, tr_recv, tdn_all, ts_buf, tsx_buf, s1_buf, s2_buf, s3_buf, tw_s, tw_r,
    rs, ss, ls, os_,
):
    results = (r_dn, r_tdn, r_wg, r_twg, r_vs, r_ts)
    dp = lax.axis_index("dp")
    blk = lax.axis_index("blk")
    head = lax.axis_index("head")
    z, x, y, c = blk // 4, blk % 4, head // 2, head % 2
    me = y * 4 + x
    mine = x // 2
    half = x % 2

    def dev(dz=None, dx=None, dy=None, dc=None, ddp=None):
        zz = z if dz is None else dz
        xx = x if dx is None else dx
        yy = y if dy is None else dy
        cc = c if dc is None else dc
        return {"dp": dp if ddp is None else ddp, "blk": zz * 4 + xx, "head": yy * 2 + cc}

    def remote(src, dst, name, to):
        return pltpu.make_async_remote_copy(
            src_ref=src, dst_ref=dst, send_sem=ss.at[SEM[name]], recv_sem=rs.at[SEM[name]],
            device_id=to, device_id_type=MESH)

    def local(src, dst, name):
        return pltpu.make_async_copy(src, dst, rs.at[SEM[name]])

    def got(ref, name):
        pltpu.make_async_copy(ref, ref, rs.at[SEM[name]]).wait()
        if name in expected:
            expected[name].pop(0)

    def sent(ref, name):
        pltpu.make_async_copy(ref, ref, ss.at[SEM[name]]).wait()

    expected = {}
    copies = {}
    leaving = []

    def expect(name, *refs):
        expected[name] = list(refs)

    def drain():
        for name, refs in list(expected.items()):
            for ref in list(refs):
                got(ref, name)
        for n_, cp in list(copies.items()):
            if n_ not in waited:
                cp.wait()
        for fn in leaving:
            fn()

    waited = set()
    drains.append(drain)

    def ready(name):
        copies[name].wait()
        waited.add(name)

    def leave(ref, name, times=1):
        def fn():
            for _ in range(times):
                sent(ref, name)
        leaving.append(fn)

    def leave_if(cond, ref, name, times=1):
        def fn():
            @pl.when(cond)
            def _():
                for _ in range(times):
                    sent(ref, name)
        leaving.append(fn)

    def rows32(index):
        return pl.ds(pl.multiple_of(index * 32, 32), 32)

    def lanes(index, width=128):
        return pl.ds(pl.multiple_of(index * width, 128), width)

    barrier = pltpu.get_barrier_semaphore()

    plane = [(i, j) for i in (2, 1, 3, 0) for j in (2, 1, 3, 0) if (i, j) != (0, 0)]
    pos = dp * 4 + z

    def chip(i, j):
        return (x + i) % 4, (y + j) % 4

    def along_z(t):
        at = (pos + t) % 8
        return dev(ddp=at // 4, dz=at % 4)

    greeted = [dev(dx=chip(i, j)[0], dy=chip(i, j)[1]) for i, j in plane]
    greeted += [along_z(t) for t in (4, 3, 5, 2, 6, 1, 7)]
    greeted += [dev(dx=(x + i) % 4, dc=1 - c) for i in (2, 1, 3)]
    greeted += [dev(dy=(y + j) % 4, dc=1 - c) for j in (2, 1, 3)] + [dev(dc=1 - c)]
    for to in greeted:
        pl.semaphore_signal(barrier, inc=1, device_id=to, device_id_type=MESH)
    pl.semaphore_wait(barrier, 29)

    def send_a(table):
        place_at = rows32(me)
        for i, j in plane + [(0, 0)]:
            xx, yy = chip(i, j)
            to = dev(dx=xx, dy=yy)
            for src, dst, name in table:
                piece = src.at[:, lanes(4 * yy + xx)]
                if (i, j) == (0, 0):
                    local(piece, dst.at[place_at], name).start()
                else:
                    remote(piece, dst.at[place_at], name, to).start()

    def send_text(table):
        @pl.when(y == z)
        def _():
            for j in (2, 1, 3, 0):
                yy = (y + j) % 4
                for src, dst, name in table:
                    piece = src.at[:, lanes(4 * yy + x)]
                    place = dst.at[pl.ds(SET, TXT)]
                    if j:
                        remote(piece, place, name, dev(dy=yy)).start()
                    else:
                        local(piece, place, name).start()

    send_a(((k, kv.at[0, 0], "a_k"), (v, kv.at[0, 1], "a_v")))
    send_text(((tk, kv.at[0, 0], "a_tk"), (tv, kv.at[0, 1], "a_tv")))
    send_a(((q, qd.at[0, 0], "a_q"), (dout, qd.at[0, 1], "a_d")))
    send_text(((tq, qd.at[0, 0], "a_tq"), (tdout, qd.at[0, 1], "a_td")))
    for name, ref in (("a_k", kv.at[0, 0, pl.ds(0, SET)]), ("a_v", kv.at[0, 1, pl.ds(0, SET)]),
                      ("a_q", qd.at[0, 0, pl.ds(0, SET)]), ("a_d", qd.at[0, 1, pl.ds(0, SET)])):
        expect(name, ref)
        leave(kv.at[0, 0, pl.ds(0, 480)], name)
    for name, ref in (("a_tk", kv.at[0, 0, pl.ds(SET, TXT)]), ("a_tv", kv.at[0, 1, pl.ds(SET, TXT)]),
                      ("a_tq", qd.at[0, 0, pl.ds(SET, TXT)]), ("a_td", qd.at[0, 1, pl.ds(SET, TXT)])):
        expect(name, ref)
        leave_if(y == z, kv.at[0, 0, pl.ds(0, 96)], name)

    @pl.when(c == mine)
    def _():
        for core in range(2):
            for m in range(8):
                piece = weight.at[:, pl.ds(384 * m + 192 * core, 192), lanes(half)]
                place = wq.at[:, pl.ds(192 * m, 192), :]

                @pl.when(c != core)
                def _():
                    remote(piece, place, "wq", dev(dc=core)).start()

                @pl.when(c == core)
                def _():
                    local(piece, place, "wq").start()
    expect("wq", wq)
    leave_if(c == mine, wq, "wq")
    loads = {
        "out": (out, l_out), "dout": (dout, l_dout), "tout": (tout, l_tout), "tdout": (tdout, l_tdout),
        "nrm": (norm, l_nrm), "tnrm": (tnorm, l_tnrm), "lse": (lse, l_lse), "tlse": (tlse, l_tlse),
        "mod": (mod, l_mod), "tmod": (tmod, l_tmod), "w": (weight, l_w),
        "tw": (tweight.at[:, pl.ds(pl.multiple_of(x * 768, 768), 768), :], l_tw),
    }
    copies.update({n: pltpu.make_async_copy(s, d, ls.at[LOCALS.index(n)]) for n, (s, d) in loads.items()})
    for name in ("out", "dout", "lse", "tlse", "tout", "tdout", "nrm", "mod", "tnrm", "tmod", "w", "tw"):
        copies[name].start()


    lane = lax.broadcasted_iota(jnp.int32, (16, 128), 1)
    ones = jnp.where(
        lax.broadcasted_iota(jnp.int32, (16, 2048), 1) // DH
        == lax.broadcasted_iota(jnp.int32, (16, 2048), 0), 1.0, 0.0).astype(BF16)

    def delta_rows(a_ref, b_ref):
        total = jnp.zeros((16, 128), F32)
        products = a_ref[...].astype(F32) * b_ref[...].astype(F32)
        high = products.astype(BF16)
        low = (products - high.astype(F32)).astype(BF16)
        for part in (high, low):
            total = total + nt(ones, jnp.concatenate([part] * 4, axis=0))
        return total

    ready("out")
    ready("dout")
    video_delta = jnp.where(lane // 32 == x, delta_rows(l_out, l_dout), 0.0)
    ready("tout")
    ready("tdout")
    text_delta = jnp.where(lane < 32, delta_rows(l_tout, l_tdout), 0.0)
    d_send[...] = jnp.zeros_like(d_send)
    for h in range(16):
        d_send[h, 0:1, :] = video_delta[h:h + 1, :]
        d_send[h, 1:2, :] = text_delta[h:h + 1, :]

    for i, j in plane:
        xx, yy = chip(i, j)
        remote(d_send.at[yy * 4 + xx], d_recv.at[me], "a_st", dev(dx=xx, dy=yy)).start()
    local(d_send.at[me], d_recv.at[me], "a_st").start()
    expect("a_st", d_recv)
    leave(d_recv.at[pl.ds(0, 15)], "a_st")

    ready("lse")
    ready("tlse")
    lane8 = lax.broadcasted_iota(jnp.int32, (8, 128), 1)
    l_send[...] = jnp.zeros_like(l_send)
    for j in range(2):
        for cc in range(2):
            for yy in range(4):
                row = jnp.broadcast_to(l_lse[j:j + 1, 128 * (yy // 2):128 * (yy // 2) + 128], (8, 128))
                shift = (32 * x + 256 - (yy % 2) * 64 - cc * 32) % 128
                row = jnp.where(lane8 // 32 == x, pltpu.roll(row, shift, 1), 0.0)
                l_send[j, cc, yy:yy + 1, :] = row[0:1, :]
            row = jnp.broadcast_to(l_tlse[j:j + 1, pl.ds(pl.multiple_of((z // 2) * 128, 128), 128)], (8, 128))
            shift = (256 - (z % 2) * 64 - cc * 32) % 128
            row = jnp.where(lane8 < 32, pltpu.roll(row, shift, 1), 0.0)
            l_send[j, cc, 4:5, :] = row[0:1, :]
    for j in range(2):
        for cc in range(2):
            own = jnp.logical_and(x == 2 * c + j, c == cc)

            @pl.when(jnp.logical_not(own))
            def _():
                remote(l_send.at[j, cc], l_recv.at[x], "a_lse", dev(dx=2 * c + j, dc=cc)).start()

            @pl.when(own)
            def _():
                local(l_send.at[j, cc], l_recv.at[x], "a_lse").start()

    expect("a_lse", l_recv)
    leave_if(c == mine, l_recv.at[pl.ds(0, 3)], "a_lse")
    leave_if(c != mine, l_recv, "a_lse")

    ready("nrm")
    ready("mod")

    def group(value, core):
        return jnp.concatenate([value[:, 384 * m + 192 * core:384 * m + 192 * core + 192] for m in range(8)], axis=1)

    nrm = l_nrm[...].astype(F32)
    for core in range(2):
        vin_s[core] = group(nrm, core).astype(BF16)
    local(vin_s.at[c], vin_all.at[c, y, x], "v0").start()
    remote(vin_s.at[1 - c], vin_all.at[c, y, x], "v0", dev(dc=1 - c)).start()
    expect("v0", vin_all.at[:, y, x])
    leave(vin_s.at[0], "v0")
    grouped = jnp.where(c == 0, group(l_mod[...], 0), group(l_mod[...], 1))
    shift_col[...] = jnp.transpose(jnp.broadcast_to(grouped[0:1, :], (128, 1536)))
    gain_col[...] = jnp.transpose(jnp.broadcast_to(1.0 + grouped[1:2, :], (128, 1536)))
    ready("tnrm")
    ready("tmod")
    tgain = 1.0 + l_tmod[1:2, :]
    tin_s[...] = (tgain * l_tnrm[...].astype(F32) + l_tmod[0:1, :]).astype(BF16)

    along = jnp.where(c == 0, y, x)

    def line_one(t):
        to = (along + t) % 4
        return dev(dx=jnp.where(c == 0, x, to), dy=jnp.where(c == 0, to, y))

    def line_two(t):
        to = (jnp.where(c == 0, x, y) + t) % 4
        return dev(dx=jnp.where(c == 0, to, x), dy=jnp.where(c == 0, y, to))

    first_pair = ((pos + 4) // 2) % 4
    pairs = [(first_pair + n) % 4 for n in (0, 1, 3, 2)]
    chunk = [pl.ds(pl.multiple_of(384 * i, 128), 384) for i in pairs]

    def block(t, n):
        at = (along + 4 - t) % 4
        return vin_all.at[:, jnp.where(c == 0, at, y), jnp.where(c == 0, x, at), :, chunk[n]]

    got(vin_all.at[:, y, x], "v0")
    for n in range(4):
        for t in (2, 1, 3):
            name = "v1%d%d" % (t, n)
            remote(block(0, n), block(0, n), name, line_one(t)).start()
            expect(name, block(t, n))
            leave(block(0, n), name)
        for t in (2, 1, 3):
            remote(block(0, n), block(0, n), "v2%d" % n, line_two(t)).start()
    gk_acc[...] = jnp.zeros_like(gk_acc)
    gv_acc[...] = jnp.zeros_like(gv_acc)
    gq_acc[...] = jnp.zeros_like(gq_acc)

    zn = z + 1 - 2 * (z % 2)
    zf = (z + 2) % 4

    got(kv.at[0, 0, pl.ds(0, SET)], "a_k")
    got(kv.at[0, 1, pl.ds(0, SET)], "a_v")
    got(kv.at[0, 0, pl.ds(SET, TXT)], "a_tk")
    got(kv.at[0, 1, pl.ds(SET, TXT)], "a_tv")

    def pass_on(src, dst, name, to):
        remote(src, dst, name, to).start()
        expect(name, dst)
        leave(src, name)

    pass_on(kv.at[0], kv.at[1], "b_kv", dev(dz=zn))
    got(qd.at[0, 0, pl.ds(0, SET)], "a_q")
    got(qd.at[0, 1, pl.ds(0, SET)], "a_d")
    got(qd.at[0, 0, pl.ds(SET, TXT)], "a_tq")
    got(qd.at[0, 1, pl.ds(SET, TXT)], "a_td")
    pass_on(qd.at[0], qd.at[1], "b_qz", dev(dz=zf))
    pass_on(qd.at[0], qd.at[2], "b_qc", dev(dc=1 - c))
    got(d_recv, "a_st")
    got(l_recv, "a_lse")
    for yy in range(4):
        st[0, yy:yy + 1, :] = LOG2E * (l_recv[0, yy:yy + 1, :] + l_recv[1, yy:yy + 1, :]
                                       + l_recv[2, yy:yy + 1, :] + l_recv[3, yy:yy + 1, :])
        st[0, 4 + yy:5 + yy, :] = (d_recv[4 * yy, 0:1, :] + d_recv[4 * yy + 1, 0:1, :]
                                   + d_recv[4 * yy + 2, 0:1, :] + d_recv[4 * yy + 3, 0:1, :])
    st[0, 8:9, :] = LOG2E * l_recv[0, 4:5, :]
    st[0, 9:10, :] = d_recv[z * 4 + x, 1:2, :]
    st[0, 10:16, :] = jnp.zeros((6, 128), F32)
    remote(st.at[0], st.at[1], "b_sz", dev(dz=zf)).start()
    remote(st.at[0], st.at[2], "b_sc", dev(dc=1 - c)).start()
    expect("b_sc", st.at[2])
    expect("b_sz", st.at[1])
    leave(st.at[0], "b_sc")
    leave(st.at[0], "b_sz")

    def forward(n):
        for t in (1, 3, 2):
            got(block(t, n), "v1%d%d" % (t, n))
            for u in (2, 1, 3):
                remote(block(t, n), block(t, n), "v2%d" % n, line_two(u)).start()

    for n in range(4):
        every = vin_all.at[:, pl.ds(0, 3), :, :, chunk[n]]
        expect("v2%d" % n, every)
        leave(every, "v2%d" % n)

    window = jnp.minimum((blk * 96) // 128 * 128, 1280)

    peers = [(j, m) for j in (2, 1, 3, 0) for m in (0, 1) if (j, m) != (0, 0)]
    quarter = pl.ds(pl.multiple_of(x * 768, 768), 768)

    def to_peers(copies_for, name):
        for j, m in peers:
            yy, cc = (y + j) % 4, (c + m) % 2
            for src, dst in copies_for(yy * 2 + cc):
                remote(src, dst, name, dev(dy=yy, dc=cc)).start()

    def tin_copies(hd):
        return [(tin_s.at[:, pl.ds(pl.multiple_of(other * 1536 + window, 128), 256)],
                 tin_all.at[rows32(head), pl.ds(other * 256, 256)]) for other in range(2)]

    for src, dst in tin_copies(head):
        local(src, dst, "tin").start()
    to_peers(tin_copies, "tin")
    place = tq_all.at[rows32(head)]
    local(l_tnrm.at[:, quarter], place, "tq").start()
    to_peers(lambda hd: [(l_tnrm.at[:, quarter], place)], "tq")
    expect("tq", tq_all)
    leave(tq_all.at[pl.ds(0, 7 * 32)], "tq")
    expect("tin", tin_all)
    leave(tin_all.at[pl.ds(0, 7 * 32)], "tin")

    def pair(lse_row, delta_row, query, dquery, keys, values):
        probs = jnp.exp2(nt(keys, query) * (FACTOR * LOG2E) - lse_row)
        dscores = (probs * (nt(values, dquery) - delta_row)).astype(BF16)
        return probs.astype(BF16), dscores

    def row512(i, first):
        return jnp.concatenate([st[i, first + n:first + n + 1, :] for n in range(4)], axis=1)

    def attend(step, carry):
        i = (step % 2) * 2 + step // 4
        j = ((step + 2) // 4) % 2

        @pl.when(step == 1)
        def _():
            got(qd.at[2], "b_qc")
            got(st.at[2], "b_sc")

        @pl.when(step == 2)
        def _():
            forward(0)
            forward(1)
            got(kv.at[1], "b_kv")

        @pl.when(step == 3)
        def _():
            forward(2)
            forward(3)

        @pl.when(step == 4)
        def _():
            got(qd.at[1], "b_qz")
            remote(qd.at[1], qd.at[3], "b_qf", dev(dc=1 - c)).start()
            got(st.at[1], "b_sz")
            remote(st.at[1], st.at[3], "b_sf", dev(dc=1 - c)).start()

        @pl.when(step == 5)
        def _():
            got(qd.at[3], "b_qf")
            got(st.at[3], "b_sf")

        query, dquery = qd[i, 0, 0:SET, :], qd[i, 1, 0:SET, :]
        keys, values = kv[j, 0], kv[j, 1]
        probs, dscores = pair(row512(i, 0), row512(i, 4), query, dquery, keys, values)
        gv_acc[j] += nn(probs, dquery)
        gk_acc[j] += nn(dscores, query)
        gq_acc[i, 0:SET, :] += tn(dscores, keys)
        return carry

    def attend_text(j):
        query = jnp.concatenate([qd[i, 0, SET:ROWS, :] for i in range(4)], axis=0)
        dquery = jnp.concatenate([qd[i, 1, SET:ROWS, :] for i in range(4)], axis=0)
        lse_row = jnp.zeros((8, 128), F32)
        delta_row = jnp.zeros((8, 128), F32)
        for i in range(4):
            one, two = (jnp.broadcast_to(st[i, r:r + 1, :], (8, 128)) for r in (8, 9))
            lse_row = lse_row + (pltpu.roll(one, 32 * i, 1) if i else one)
            delta_row = delta_row + (pltpu.roll(two, 32 * i, 1) if i else two)
        keys, values = kv[j, 0], kv[j, 1]
        probs, dscores = pair(lse_row[0:1, :], delta_row[0:1, :], query, dquery, keys, values)
        gv_acc[j] += nn(probs, dquery)
        gk_acc[j] += nn(dscores, query)
        from_text = tn(dscores, keys)
        for i in range(4):
            gq_acc[i, SET:ROWS, :] += from_text[32 * i:32 * i + 32, :]

    lax.fori_loop(0, 6, attend, 0)
    leave(qd.at[0], "b_qf")
    leave(st.at[0], "b_sf")
    attend_text(1)
    dkv_s[0] = (gk_acc[1] * FACTOR).astype(BF16)
    dkv_s[1] = gv_acc[1].astype(BF16)
    remote(dkv_s, dkv_r, "d_kv", dev(dz=zn)).start()
    expect("d_kv", dkv_r)
    leave(dkv_s, "d_kv")
    lax.fori_loop(6, 8, attend, 0)
    attend_text(0)
    dqc_s[0] = (gq_acc[2] * FACTOR).astype(BF16)
    dqc_s[1] = (gq_acc[3] * FACTOR).astype(BF16)
    remote(dqc_s, dqc_r, "d_qc", dev(dc=1 - c)).start()
    expect("d_qc", dqc_r)
    leave(dqc_s, "d_qc")
    got(dqc_r, "d_qc")
    dqz_s[...] = (gq_acc[1] * FACTOR + dqc_r[1].astype(F32)).astype(BF16)
    remote(dqz_s, dqz_r, "d_qz", dev(dz=zf)).start()
    expect("d_qz", dqz_r)
    leave(dqz_s, "d_qz")

    def send_grads(name, cols, table):
        own_part = gw.at[c, :, :, :, cols]
        remote(own_part, own_part, name, dev(dc=1 - c)).start()
        expect(name, gw.at[1 - c, :, :, :, cols])
        leave(own_part, name)
        for ch in table:
            for xx in (2, 1, 3, 0):
                to = (x + xx) % 4
                own = jnp.logical_and(xx == 0, c == mine)
                piece = gw.at[c, :, to, :, pl.ds(128 * ch, 128)]
                place = gs.at[c, :, :, pl.ds(pl.multiple_of(256 * ch + 128 * half, 128), 128)]

                @pl.when(jnp.logical_not(own))
                def _():
                    remote(piece, place, "e", dev(dx=to, dc=mine)).start()

                @pl.when(own)
                def _():
                    local(piece, place, "e").start()

    def finish_channel(ch, value):
        gw[c, :, :, :, 128 * ch:128 * ch + 128] = value[0:SET, :].reshape(4, 4, 32, 128)
        g_txt[ch] = value[SET:ROWS, :]

    got(dkv_r, "d_kv")
    finish_channel(1, (gk_acc[0] * FACTOR + dkv_r[0].astype(F32)).astype(BF16))
    finish_channel(2, (gv_acc[0] + dkv_r[1].astype(F32)).astype(BF16))
    send_grads("gkv", pl.ds(128, 256), (1, 2))
    got(dqz_r, "d_qz")
    finish_channel(0, (gq_acc[0] * FACTOR + dqc_r[0].astype(F32) + dqz_r[...].astype(F32)).astype(BF16))
    send_grads("gq", pl.ds(0, 128), (0,))
    expect("e", gs)
    for ch in range(3):
        one = gw.at[0, :, 0, :, pl.ds(128 * ch, 128)]
        leave_if(c == mine, one, "e", 3)
        leave_if(c != mine, one, "e", 4)
    for zz in range(4):
        @pl.when(z != zz)
        def _():
            remote(g_txt, tz.at[:, z], "tz", dev(dz=zz)).start()

        @pl.when(z == zz)
        def _():
            local(g_txt, tz.at[:, z], "tz").start()
    expect("tz", tz)
    leave(tz.at[:, pl.ds(0, 3)], "tz")

    got(gw.at[1 - c, :, :, :, pl.ds(128, 256)], "gkv")
    got(gw.at[1 - c, :, :, :, pl.ds(0, 128)], "gq")
    grads = gw[...].reshape(1024, 384)
    col = nn(jnp.ones((8, 1024), BF16), grads)[0:1, :]

    def project(n):
        i = pairs[n]
        got(vin_all.at[:, pl.ds(0, 3), :, :, chunk[n]], "v2%d" % n)
        cols = pl.ds(pl.multiple_of(384 * i, 128), 384)
        part = tn(vin_all[:, :, :, :, cols].reshape(1024, 384), grads)
        m_acc[cols, :] = part
        gain = jnp.concatenate([gain_col[cols, :]] * 3, axis=1)
        shift = jnp.concatenate([shift_col[cols, :]] * 3, axis=1)
        term = gain * part + shift * col
        wt[2 * i] = term[0:192, :]
        wt[2 * i + 1] = term[192:384, :]

    def ring_to(way):
        to = (pos + (1 if way == 0 else 7)) % 8
        return dev(ddp=to // 4, dz=to % 4)

    def ring(step):
        for ch in range(3):
            lane_cols = slice(128 * ch, 128 * ch + 128)
            for way in range(2):
                dest = (pos + (4 - step if way == 0 else 4 + step)) % 8
                rows = (slice(0, 96) if way == 0 else slice(96, 192)) if step == 0 else slice(0, 192)
                own = wt[dest, rows, lane_cols]
                if step:
                    size = 96 if step == 1 else 192
                    heard = ring_r.at[way, step - 1, ch, pl.ds(0, size)]
                    got(heard, "r%d%d%d" % (way, step - 1, ch))
                    heard = heard[...].astype(F32)
                    if step == 1:
                        near, far = own[0:96, :], own[96:192, :]
                        pair_ = (near + heard, far) if way == 0 else (near, far + heard)
                        own = jnp.concatenate(pair_, axis=0)
                    else:
                        own = own + heard
                size = 96 if step == 0 else 192
                out_ref = ring_s.at[way, step, ch, pl.ds(0, size)]
                out_ref[...] = own.astype(BF16)
                name = "r%d%d%d" % (way, step, ch)
                remote(out_ref, ring_r.at[way, step, ch, pl.ds(0, size)], name, ring_to(way)).start()
                expect(name, ring_r.at[way, step, ch, pl.ds(0, size)])
                leave(out_ref, name)

    project(0)
    ring(0)
    got(tz, "tz")
    for xx in (2, 1, 3, 0):
        to = (x + xx) % 4
        own = jnp.logical_and(xx == 0, c == mine)
        place = tg.at[:, :, c, :, lanes(half)]

        @pl.when(jnp.logical_not(own))
        def _():
            remote(tz, place, "te", dev(dx=to, dc=mine)).start()

        @pl.when(own)
        def _():
            local(tz, place, "te").start()
    expect("te", tg)
    leave_if(c == mine, tz, "te", 3)
    leave_if(c != mine, tz, "te", 4)
    project(1)
    project(2)
    project(3)
    got(wq, "wq")
    for m in range(8):
        rows = slice(192 * m, 192 * m + 192)
        zero = jnp.zeros((192, 128), F32)
        one = jnp.zeros((192, 128), F32)
        for ch in range(3):
            w_part = wq[ch, rows, :].astype(F32)
            zero = zero + w_part * col[:, 128 * ch:128 * ch + 128]
            one = one + w_part * m_acc[rows, 128 * ch:128 * ch + 128]
        s_acc[0, rows, :] = zero
        s_acc[1, rows, :] = one
    for n in range(2):
        high = s_acc[n].astype(BF16)
        low = (s_acc[n] - high.astype(F32)).astype(BF16)
        row = jnp.ones((8, 128), BF16)
        s1_buf[me, n:n + 1, :] = (nt(row, high) + nt(row, low))[0:1, :]

    for i, j in plane:
        remote(s1_buf.at[me], s1_buf.at[me], "s1", dev(dx=chip(i, j)[0], dy=chip(i, j)[1])).start()
    expect("s1", s1_buf.at[pl.ds(0, 15)])
    leave(s1_buf.at[pl.ds(0, 15)], "s1")
    ring(1)

    def back_chunk(n):
        cols = slice(512 * n, 512 * n + 512)
        rows = gs[...].reshape(256, 768)
        term = (nt(rows[:, 0:256], l_w[0, cols, :]) + nt(rows[:, 256:512], l_w[1, cols, :])
                + nt(rows[:, 512:768], l_w[2, cols, :]))

        @pl.when(c == 0)
        def _():
            b_own[:, cols] = term[0:128, :]
            b_send[:, cols] = term[128:256, :].astype(BF16)

        @pl.when(c == 1)
        def _():
            b_own[:, cols] = term[128:256, :]
            b_send[:, cols] = term[0:128, :].astype(BF16)
        remote(b_send.at[:, cols], b_recv.at[:, cols], "bc%d" % n, dev(dc=1 - c)).start()
        expect("bc%d" % n, b_recv.at[:, cols])
        leave(b_send.at[:, cols], "bc%d" % n)

    def gather_chunk(n):
        cols = slice(512 * n, 512 * n + 512)
        got(b_recv.at[:, cols], "bc%d" % n)
        total = b_own[:, cols] + b_recv[:, cols].astype(F32)
        b_own[:, cols] = total
        for yy in range(4):
            y_send[yy, :, cols] = total[32 * yy:32 * yy + 32, :].astype(BF16)

            @pl.when(yy != y)
            def _():
                remote(y_send.at[yy, :, cols], y_recv.at[y, :, cols], "by", dev(dy=yy)).start()

    ready("w")
    got(gs, "e")
    back_chunk(0)
    back_chunk(1)
    gather_chunk(0)
    back_chunk(2)
    gather_chunk(1)
    back_chunk(3)
    gather_chunk(2)
    back_chunk(4)
    gather_chunk(3)
    back_chunk(5)
    gather_chunk(4)
    gather_chunk(5)
    expect("by", y_recv.at[pl.ds(0, 3)])
    leave(y_send.at[pl.ds(0, 3)], "by")
    ring(2)

    got(tg, "te")
    ready("tw")
    term = (nt(tg[0].reshape(256, 256), l_tw[0]) + nt(tg[1].reshape(256, 256), l_tw[1])
            + nt(tg[2].reshape(256, 256), l_tw[2]))
    for hd in range(8):
        tr_send[hd] = term[32 * hd:32 * hd + 32, :].astype(BF16)
    local(tr_send.at[head], tr_recv.at[head], "tr").start()
    to_peers(lambda hd: [(tr_send.at[hd], tr_recv.at[head])], "tr")
    expect("tr", tr_recv)
    leave(tr_recv.at[pl.ds(0, 7)], "tr")
    got(tq_all, "tq")
    ts_buf[head] = jnp.concatenate([jnp.sum(term, axis=0, keepdims=True),
                                    jnp.sum(term * tq_all[...].astype(F32), axis=0, keepdims=True)], axis=0)
    to_peers(lambda hd: [(ts_buf.at[head], ts_buf.at[head])], "ts")
    expect("ts", ts_buf.at[pl.ds(0, 7)])
    leave(ts_buf.at[pl.ds(0, 7)], "ts")

    got(tin_all, "tin")
    first = pl.multiple_of(blk * 96 - window, 32)
    away = pl.multiple_of((1 - dp) * 256 + first, 32)
    near = pl.multiple_of(dp * 256 + first, 32)
    for ch in range(3):
        t_tmp[...] = tn(tin_all[...], tg[ch].reshape(256, 256)).astype(BF16)
        tw_s[ch] = t_tmp[pl.ds(away, 96), :]
        o_twg[ch] = t_tmp[pl.ds(near, 96), :].astype(F32)
    remote(tw_s, tw_r, "tw", dev(ddp=1 - dp)).start()
    expect("tw", tw_r)
    leave(tw_s, "tw")

    got(s1_buf.at[pl.ds(0, 15)], "s1")
    stat = s1_buf[0]
    for t in range(1, 16):
        stat = stat + s1_buf[t]
    s2_buf[z] = stat
    for t in (2, 1, 3):
        remote(s2_buf.at[z], s2_buf.at[z], "s2", dev(dz=(z + t) % 4)).start()
    expect("s2", s2_buf.at[pl.ds(0, 3)])
    leave(s2_buf.at[pl.ds(0, 3)], "s2")
    ring(3)
    got(ts_buf.at[pl.ds(0, 7)], "ts")
    tstat = ts_buf[0]
    for hd in range(1, 8):
        tstat = tstat + ts_buf[hd]
    tsx_buf[x] = tstat
    for t in (2, 1, 3):
        remote(tsx_buf.at[x], tsx_buf.at[x], "tsx", dev(dx=(x + t) % 4)).start()
    expect("tsx", tsx_buf.at[pl.ds(0, 3)])
    leave(tsx_buf.at[pl.ds(0, 3)], "tsx")
    got(tr_recv, "tr")
    tback = tr_recv[0].astype(F32)
    for hd in range(1, 8):
        tback = tback + tr_recv[hd].astype(F32)
    tdn_all[x] = ((1.0 + l_tmod[1:2, quarter]) * tback).astype(BF16)
    for t in (2, 1, 3):
        remote(tdn_all.at[x], tdn_all.at[x], "tdn", dev(dx=(x + t) % 4)).start()
    expect("tdn", tdn_all.at[pl.ds(0, 3)])
    leave(tdn_all.at[pl.ds(0, 3)], "tdn")
    got(s2_buf.at[pl.ds(0, 3)], "s2")
    s3_buf[c] = s2_buf[0] + s2_buf[1] + s2_buf[2] + s2_buf[3]
    remote(s3_buf.at[c], s3_buf.at[c], "s3", dev(dc=1 - c)).start()
    expect("s3", s3_buf.at[0])
    leave(s3_buf.at[0], "s3")

    for ch in range(3):
        lane_cols = slice(128 * ch, 128 * ch + 128)
        total = wt[pos, :, lane_cols]
        for way in range(2):
            got(ring_r.at[way, 3, ch], "r%d3%d" % (way, ch))
            total = total + ring_r[way, 3, ch].astype(F32)
        fin_s[0, ch] = total[0:96, :].astype(BF16)
        fin_s[1, ch] = total[96:192, :].astype(BF16)
    for n in range(2):
        own = jnp.logical_and(c == mine, n == half)

        @pl.when(jnp.logical_not(own))
        def _():
            remote(fin_s.at[n], fin_r.at[half], "fin", dev(dx=2 * c + n, dc=mine)).start()

        @pl.when(own)
        def _():
            local(fin_s.at[n], fin_r.at[half], "fin").start()
    expect("fin", fin_r)
    leave_if(c == mine, fin_s.at[0], "fin")
    leave_if(c != mine, fin_s, "fin")

    def write(n, src):
        pltpu.make_async_copy(src, results[n], os_.at[n]).start()

    got(s3_buf.at[0], "s3")
    for m in range(8):
        o_vs[:, 384 * m:384 * m + 384] = jnp.concatenate(
            [s3_buf[core, :, 192 * m:192 * m + 192] for core in range(2)], axis=1)
    write(4, o_vs)
    got(tsx_buf.at[pl.ds(0, 3)], "tsx")
    for xx in range(4):
        o_ts[:, 768 * xx:768 * xx + 768] = tsx_buf[xx]
    write(5, o_ts)
    got(y_recv.at[pl.ds(0, 3)], "by")
    back = b_own[rows32(y), :]
    for yy in range(4):
        back = back + jnp.where(yy == y, 0.0, y_recv[yy].astype(F32))
    o_dn[...] = ((1.0 + l_mod[1:2, :]) * back).astype(BF16)
    write(0, o_dn)
    got(tw_r, "tw")
    o_twg[...] += tw_r[...].astype(F32)
    write(3, o_twg)
    got(tdn_all.at[pl.ds(0, 3)], "tdn")
    for xx in range(4):
        o_tdn[:, 768 * xx:768 * xx + 768] = tdn_all[xx]
    write(1, o_tdn)
    got(fin_r, "fin")
    for ch in range(3):
        for j in range(2):
            o_wg[ch, :, 128 * j:128 * j + 128] = fin_r[j, ch].astype(F32)
    write(2, o_wg)
    for n, src in enumerate((o_dn, o_tdn, o_wg, o_twg, o_vs, o_ts)):
        pltpu.make_async_copy(src, results[n], os_.at[n]).wait()


def finish(*refs):
    into = [pltpu.make_async_copy(refs[n], refs[12 + n], refs[18].at[n]) for n in range(6)]
    back = [pltpu.make_async_copy(refs[12 + n], refs[6 + n], refs[18].at[n]) for n in range(6)]
    for copy in into:
        copy.start()
    for first, second in zip(into, back):
        first.wait()
        second.start()
    for copy in back:
        copy.wait()


SCRATCH = (
    ((32, D), BF16), ((32, D), BF16), ((3, 96, 256), F32), ((3, 96, 256), F32), ((2, D), F32), ((2, D), F32),
    ((32, 2048), BF16), ((32, 2048), BF16), ((32, 2048), BF16), ((32, 2048), BF16),
    ((32, D), BF16), ((32, D), BF16), ((3, D, 256), BF16), ((3, 768, 256), BF16),
    ((2, 256), F32), ((2, 256), F32), ((2, D), F32), ((2, D), F32),
    ((4, 2, ROWS, 128), BF16), ((2, 2, ROWS, 128), BF16), ((4, 16, 128), F32),
    ((16, 8, 128), F32), ((16, 8, 128), F32), ((2, 2, 8, 128), F32), ((4, 8, 128), F32),
    ((2, ROWS, 128), F32), ((2, ROWS, 128), F32), ((4, ROWS, 128), F32),
    ((2, ROWS, 128), BF16), ((2, ROWS, 128), BF16), ((2, ROWS, 128), BF16), ((2, ROWS, 128), BF16),
    ((ROWS, 128), BF16), ((ROWS, 128), BF16), ((2, 4, 4, 32, 384), BF16), ((3, 32, 128), BF16),
    ((2, 32, 1536), BF16), ((2, 4, 4, 32, 1536), BF16), ((3, 1536, 128), BF16),
    ((1536, 128), F32), ((1536, 128), F32), ((1536, 384), F32), ((2, 1536, 128), F32), ((32, D), BF16), ((256, 512), BF16), ((256, 768), BF16),
    ((3, 4, 32, 128), BF16), ((3, 4, 2, 32, 256), BF16), ((2, 4, 32, 768), BF16),
    ((8, 192, 384), F32), ((2, 4, 3, 192, 128), BF16), ((2, 4, 3, 192, 128), BF16),
    ((2, 3, 96, 128), BF16), ((2, 3, 96, 128), BF16),
    ((128, D), BF16), ((128, D), BF16), ((128, D), F32), ((4, 32, D), BF16), ((4, 32, D), BF16),
    ((512, 256), BF16), ((8, 32, 768), BF16), ((8, 32, 768), BF16), ((4, 32, 768), BF16), ((8, 2, 768), F32), ((4, 2, 768), F32),
    ((16, 2, 1536), F32), ((4, 2, 1536), F32), ((2, 2, 1536), F32),
    ((3, 96, 256), BF16), ((3, 96, 256), BF16),
)


def body(
    video_q, video_k, video_v, video_out, video_dout, text_q, text_k, text_v, text_out, text_dout,
    video_lse, text_lse, video_norm, text_norm, video_mod, text_mod, video_weight, text_weight,
):
    args = [a[0] for a in (
        video_q, video_k, video_v, video_out, video_dout, text_q, text_k, text_v, text_out, text_dout,
        video_lse, text_lse, video_norm, text_norm, video_mod, text_mod)]
    args += [jnp.transpose(w, (1, 0, 2)) for w in (video_weight, text_weight)]
    results = pl.pallas_call(
        kernel,
        out_shape=(
            jax.ShapeDtypeStruct((32, D), BF16), jax.ShapeDtypeStruct((32, D), BF16),
            jax.ShapeDtypeStruct((3, 96, 256), F32), jax.ShapeDtypeStruct((3, 96, 256), F32),
            jax.ShapeDtypeStruct((2, D), F32), jax.ShapeDtypeStruct((2, D), F32),
        ),
        in_specs=[pl.BlockSpec(memory_space=pl.ANY)] * len(args),
        out_specs=[pl.BlockSpec(memory_space=pl.ANY)] * 6,
        scratch_shapes=[pltpu.VMEM(shape, kind) for shape, kind in SCRATCH] + [
            pltpu.SemaphoreType.DMA((len(NAMES),)),
            pltpu.SemaphoreType.DMA((len(NAMES),)),
            pltpu.SemaphoreType.DMA((len(LOCALS),)),
            pltpu.SemaphoreType.DMA((6,)),
        ],
        compiler_params=pltpu.CompilerParams(collective_id=0, has_side_effects=True, vmem_limit_bytes=60 * 1024 * 1024),
    )(*args)
    anywhere = pl.BlockSpec(memory_space=pl.ANY)
    dn, tdn, wg, twg, vs, ts = pl.pallas_call(
        finish,
        out_shape=[jax.ShapeDtypeStruct(r.shape, r.dtype) for r in results],
        in_specs=[anywhere] * 6,
        out_specs=[anywhere] * 6,
        scratch_shapes=[pltpu.VMEM(r.shape, r.dtype) for r in results] + [pltpu.SemaphoreType.DMA((6,))],
        compiler_params=pltpu.CompilerParams(vmem_limit_bytes=60 * 1024 * 1024),
    )(*results)
    return (
        dn[None], tdn[None], jnp.transpose(wg, (1, 0, 2)), jnp.transpose(twg, (1, 0, 2)), vs[None], ts[None],
    )


def solution(mesh):
    tokens = P("dp", ("blk", "head"), None)
    text = P("dp", "head", None)
    whole = P("dp", None, None)
    columns = P(None, None, "head")
    return jax.shard_map(
        body,
        mesh=mesh,
        in_specs=(tokens,) * 5 + (text,) * 5 + (
            P("dp", "head", "blk"), P("dp", "head", None), tokens, text, whole, whole, columns, columns),
        out_specs=(
            tokens, text, P(("dp", "blk"), None, "head"), P(("dp", "blk"), None, "head"), whole, whole),
        check_vma=False,
    )
```

```python
import functools

import jax
import jax.numpy as jnp
from jax import lax
from jax.experimental import pallas as pl
from jax.experimental.pallas import tpu as pltpu
from jax.sharding import PartitionSpec as P

MESH = pl.DeviceIdType.MESH
D = 3072
DH = 128
SET = 512
ROWS = 544
TXT = 32
FACTOR = DH ** (-0.5)
LOG2E = 1.4426950408889634
F32 = jnp.float32
BF16 = jnp.bfloat16

NAMES = (
    "a_q", "a_d", "a_k", "a_v", "a_st", "a_lse", "a_tq", "a_td", "a_tk", "a_tv",
    "b_kv", "b_qc", "b_sc", "b_qz", "b_sz", "b_qf", "b_sf", "v0", "wq", "tin",
    "d_kv", "d_qc", "d_qz", "gkv", "gq", "e", "tz", "tzs", "te",
    "bc0", "bc1", "bc2", "bc3", "bc4", "bc5", "by", "tr", "tdz", "tdn", "ts", "ts2", "tsx", "s1", "s2", "s3", "tx", "tf", "fin",
)
RING = tuple("r%d%d%d" % (way, step, ch) for way in range(2) for step in range(4) for ch in range(3))
INPUTS = tuple("v1%d%d" % (t, n) for t in (1, 2, 3) for n in range(4)) + tuple("v2%d" % n for n in range(4))
NAMES = NAMES + RING + INPUTS
SEM = {name: index for index, name in enumerate(NAMES)}
LOCALS = ("out", "dout", "tout", "tdout", "nrm", "tnrm", "w", "tw", "lse", "tlse", "mod", "tmod")


def nt(left, right):
    return lax.dot_general(left, right, (((1,), (1,)), ((), ())), preferred_element_type=F32)


def tn(left, right):
    return lax.dot_general(left, right, (((0,), (0,)), ((), ())), preferred_element_type=F32)


def nn(left, right):
    return jnp.dot(left, right, preferred_element_type=F32)


def kernel(*refs):
    drains = []
    kernel_body(drains, *refs)
    drains[0]()


def kernel_body(
    drains,
    q, k, v, out, dout, tq, tk, tv, tout, tdout, lse, tlse, norm, tnorm, mod, tmod, weight, tweight,
    r_dn, r_tdn, r_wg, r_twg, r_vs, r_ts,
    o_dn, o_tdn, o_wg, o_twg, o_vs, o_ts,
    l_out, l_dout, l_tout, l_tdout, l_nrm, l_tnrm, l_w, l_tw, l_lse, l_tlse, l_mod, l_tmod,
    qd, kv, st, d_send, d_recv, l_send, l_recv,
    gk_acc, gv_acc, gq_acc, dkv_s, dkv_r, dqc_s, dqc_r, dqz_s, dqz_r, gw, g_txt,
    vin_s, vin_all, wq, gain_col, shift_col, m_acc, s_acc, tin_s, tin_x, tin_all, tzz, tgz, gs,
    wt, ring_s, ring_r, fin_s, fin_r, b_send, b_recv, b_own, y_send, y_recv,
    tr_send, tr_recv, tdn_all, ts_buf, ts2_buf, tsx_buf, s1_buf, s2_buf, s3_buf, tw_s, tf_s, tf_r,
    rs, ss, ls, os_,
):
    results = (r_dn, r_tdn, r_wg, r_twg, r_vs, r_ts)
    dp = lax.axis_index("dp")
    blk = lax.axis_index("blk")
    head = lax.axis_index("head")
    z, x, y, c = blk // 4, blk % 4, head // 2, head % 2
    me = y * 4 + x
    mine = x // 2
    half = x % 2

    def dev(dz=None, dx=None, dy=None, dc=None, ddp=None):
        zz = z if dz is None else dz
        xx = x if dx is None else dx
        yy = y if dy is None else dy
        cc = c if dc is None else dc
        return {"dp": dp if ddp is None else ddp, "blk": zz * 4 + xx, "head": yy * 2 + cc}

    def remote(src, dst, name, to):
        return pltpu.make_async_remote_copy(
            src_ref=src, dst_ref=dst, send_sem=ss.at[SEM[name]], recv_sem=rs.at[SEM[name]],
            device_id=to, device_id_type=MESH)

    def local(src, dst, name):
        return pltpu.make_async_copy(src, dst, rs.at[SEM[name]])

    def got(ref, name):
        pltpu.make_async_copy(ref, ref, rs.at[SEM[name]]).wait()
        if name in expected:
            expected[name].pop(0)

    def sent(ref, name):
        pltpu.make_async_copy(ref, ref, ss.at[SEM[name]]).wait()

    expected = {}
    copies = {}
    leaving = []

    def expect(name, *refs):
        expected[name] = list(refs)

    def drain():
        for name, refs in list(expected.items()):
            for ref in list(refs):
                got(ref, name)
        for n_, cp in list(copies.items()):
            if n_ not in waited:
                cp.wait()
        for fn in leaving:
            fn()

    waited = set()
    drains.append(drain)

    def ready(name):
        copies[name].wait()
        waited.add(name)

    def leave(ref, name, times=1):
        def fn():
            for _ in range(times):
                sent(ref, name)
        leaving.append(fn)

    def leave_if(cond, ref, name, times=1):
        def fn():
            @pl.when(cond)
            def _():
                for _ in range(times):
                    sent(ref, name)
        leaving.append(fn)

    def rows32(index):
        return pl.ds(pl.multiple_of(index * 32, 32), 32)

    def lanes(index, width=128):
        return pl.ds(pl.multiple_of(index * width, 128), width)

    barrier = pltpu.get_barrier_semaphore()

    plane = [(i, j) for i in (2, 1, 3, 0) for j in (2, 1, 3, 0) if (i, j) != (0, 0)]
    pos = dp * 4 + z

    def chip(i, j):
        return (x + i) % 4, (y + j) % 4

    def along_z(t):
        at = (pos + t) % 8
        return dev(ddp=at // 4, dz=at % 4)

    greeted = [dev(dx=chip(i, j)[0], dy=chip(i, j)[1]) for i, j in plane]
    greeted += [along_z(t) for t in (4, 3, 5, 2, 6, 1, 7)]
    greeted += [dev(dx=(x + i) % 4, dc=1 - c) for i in (2, 1, 3)]
    greeted += [dev(dy=(y + j) % 4, dc=1 - c) for j in (2, 1, 3)] + [dev(dc=1 - c)]
    for to in greeted:
        pl.semaphore_signal(barrier, inc=1, device_id=to, device_id_type=MESH)
    pl.semaphore_wait(barrier, 29)

    def send_a(table):
        place_at = rows32(me)
        for i, j in plane + [(0, 0)]:
            xx, yy = chip(i, j)
            to = dev(dx=xx, dy=yy)
            for src, dst, name in table:
                piece = src.at[:, lanes(4 * yy + xx)]
                if (i, j) == (0, 0):
                    local(piece, dst.at[place_at], name).start()
                else:
                    remote(piece, dst.at[place_at], name, to).start()

    def send_text(table):
        @pl.when(y == z)
        def _():
            for j in (2, 1, 3, 0):
                yy = (y + j) % 4
                for src, dst, name in table:
                    piece = src.at[:, lanes(4 * yy + x)]
                    place = dst.at[pl.ds(SET, TXT)]
                    if j:
                        remote(piece, place, name, dev(dy=yy)).start()
                    else:
                        local(piece, place, name).start()

    send_a(((k, kv.at[0, 0], "a_k"), (v, kv.at[0, 1], "a_v")))
    send_text(((tk, kv.at[0, 0], "a_tk"), (tv, kv.at[0, 1], "a_tv")))
    send_a(((q, qd.at[0, 0], "a_q"), (dout, qd.at[0, 1], "a_d")))
    send_text(((tq, qd.at[0, 0], "a_tq"), (tdout, qd.at[0, 1], "a_td")))
    for name, ref in (("a_k", kv.at[0, 0, pl.ds(0, SET)]), ("a_v", kv.at[0, 1, pl.ds(0, SET)]),
                      ("a_q", qd.at[0, 0, pl.ds(0, SET)]), ("a_d", qd.at[0, 1, pl.ds(0, SET)])):
        expect(name, ref)
        leave(kv.at[0, 0, pl.ds(0, 480)], name)
    for name, ref in (("a_tk", kv.at[0, 0, pl.ds(SET, TXT)]), ("a_tv", kv.at[0, 1, pl.ds(SET, TXT)]),
                      ("a_tq", qd.at[0, 0, pl.ds(SET, TXT)]), ("a_td", qd.at[0, 1, pl.ds(SET, TXT)])):
        expect(name, ref)
        leave_if(y == z, kv.at[0, 0, pl.ds(0, 96)], name)

    @pl.when(c == mine)
    def _():
        for core in range(2):
            for m in range(8):
                piece = weight.at[:, pl.ds(384 * m + 192 * core, 192), lanes(half)]
                place = wq.at[:, pl.ds(192 * m, 192), :]

                @pl.when(c != core)
                def _():
                    remote(piece, place, "wq", dev(dc=core)).start()

                @pl.when(c == core)
                def _():
                    local(piece, place, "wq").start()
    expect("wq", wq)
    leave_if(c == mine, wq, "wq")
    loads = {
        "out": (out, l_out), "dout": (dout, l_dout), "tout": (tout, l_tout), "tdout": (tdout, l_tdout),
        "nrm": (norm, l_nrm), "tnrm": (tnorm, l_tnrm), "lse": (lse, l_lse), "tlse": (tlse, l_tlse),
        "mod": (mod, l_mod), "tmod": (tmod, l_tmod), "w": (weight, l_w),
        "tw": (tweight.at[:, pl.ds(pl.multiple_of(x * 768, 768), 768), :], l_tw),
    }
    copies.update({n: pltpu.make_async_copy(s, d, ls.at[LOCALS.index(n)]) for n, (s, d) in loads.items()})
    for name in ("out", "dout", "lse", "tlse", "tout", "tdout", "nrm", "mod", "tnrm", "tmod", "w", "tw"):
        copies[name].start()


    lane = lax.broadcasted_iota(jnp.int32, (16, 128), 1)
    ones = jnp.where(
        lax.broadcasted_iota(jnp.int32, (16, 2048), 1) // DH
        == lax.broadcasted_iota(jnp.int32, (16, 2048), 0), 1.0, 0.0).astype(BF16)

    def delta_rows(a_ref, b_ref):
        total = jnp.zeros((16, 128), F32)
        products = a_ref[...].astype(F32) * b_ref[...].astype(F32)
        high = products.astype(BF16)
        low = (products - high.astype(F32)).astype(BF16)
        for part in (high, low):
            total = total + nt(ones, jnp.concatenate([part] * 4, axis=0))
        return total

    ready("out")
    ready("dout")
    video_delta = jnp.where(lane // 32 == x, delta_rows(l_out, l_dout), 0.0)
    ready("tout")
    ready("tdout")
    text_delta = jnp.where(lane < 32, delta_rows(l_tout, l_tdout), 0.0)
    d_send[...] = jnp.zeros_like(d_send)
    for h in range(16):
        d_send[h, 0:1, :] = video_delta[h:h + 1, :]
        d_send[h, 1:2, :] = text_delta[h:h + 1, :]

    for i, j in plane:
        xx, yy = chip(i, j)
        remote(d_send.at[yy * 4 + xx], d_recv.at[me], "a_st", dev(dx=xx, dy=yy)).start()
    local(d_send.at[me], d_recv.at[me], "a_st").start()
    expect("a_st", d_recv)
    leave(d_recv.at[pl.ds(0, 15)], "a_st")

    ready("lse")
    ready("tlse")
    lane8 = lax.broadcasted_iota(jnp.int32, (8, 128), 1)
    l_send[...] = jnp.zeros_like(l_send)
    for j in range(2):
        for cc in range(2):
            for yy in range(4):
                row = jnp.broadcast_to(l_lse[j:j + 1, 128 * (yy // 2):128 * (yy // 2) + 128], (8, 128))
                shift = (32 * x + 256 - (yy % 2) * 64 - cc * 32) % 128
                row = jnp.where(lane8 // 32 == x, pltpu.roll(row, shift, 1), 0.0)
                l_send[j, cc, yy:yy + 1, :] = row[0:1, :]
            row = jnp.broadcast_to(l_tlse[j:j + 1, pl.ds(pl.multiple_of((z // 2) * 128, 128), 128)], (8, 128))
            shift = (256 - (z % 2) * 64 - cc * 32) % 128
            row = jnp.where(lane8 < 32, pltpu.roll(row, shift, 1), 0.0)
            l_send[j, cc, 4:5, :] = row[0:1, :]
    for j in range(2):
        for cc in range(2):
            own = jnp.logical_and(x == 2 * c + j, c == cc)

            @pl.when(jnp.logical_not(own))
            def _():
                remote(l_send.at[j, cc], l_recv.at[x], "a_lse", dev(dx=2 * c + j, dc=cc)).start()

            @pl.when(own)
            def _():
                local(l_send.at[j, cc], l_recv.at[x], "a_lse").start()

    expect("a_lse", l_recv)
    leave_if(c == mine, l_recv.at[pl.ds(0, 3)], "a_lse")
    leave_if(c != mine, l_recv, "a_lse")

    ready("nrm")
    ready("mod")

    def group(value, core):
        return jnp.concatenate([value[:, 384 * m + 192 * core:384 * m + 192 * core + 192] for m in range(8)], axis=1)

    nrm = l_nrm[...].astype(F32)
    for core in range(2):
        vin_s[core] = group(nrm, core).astype(BF16)
    local(vin_s.at[c], vin_all.at[c, y, x], "v0").start()
    remote(vin_s.at[1 - c], vin_all.at[c, y, x], "v0", dev(dc=1 - c)).start()
    expect("v0", vin_all.at[:, y, x])
    leave(vin_s.at[0], "v0")
    grouped = jnp.where(c == 0, group(l_mod[...], 0), group(l_mod[...], 1))
    shift_col[...] = jnp.transpose(jnp.broadcast_to(grouped[0:1, :], (128, 1536)))
    gain_col[...] = jnp.transpose(jnp.broadcast_to(1.0 + grouped[1:2, :], (128, 1536)))
    ready("tnrm")
    ready("tmod")
    tgain = 1.0 + l_tmod[1:2, :]
    tin_s[...] = (tgain * l_tnrm[...].astype(F32) + l_tmod[0:1, :]).astype(BF16)

    def text_cols(clip):
        return tin_s.at[:, pl.ds(pl.multiple_of(clip * 1536 + z * 384, 128), 384)]

    remote(text_cols(1 - dp), tin_x, "tx", dev(ddp=1 - dp)).start()
    expect("tx", tin_x)
    leave(tin_x, "tx")

    along = jnp.where(c == 0, y, x)

    def line_one(t):
        to = (along + t) % 4
        return dev(dx=jnp.where(c == 0, x, to), dy=jnp.where(c == 0, to, y))

    def line_two(t):
        to = (jnp.where(c == 0, x, y) + t) % 4
        return dev(dx=jnp.where(c == 0, to, x), dy=jnp.where(c == 0, y, to))

    first_pair = ((pos + 4) // 2) % 4
    pairs = [(first_pair + n) % 4 for n in (0, 1, 3, 2)]
    chunk = [pl.ds(pl.multiple_of(384 * i, 128), 384) for i in pairs]

    def block(t, n):
        at = (along + 4 - t) % 4
        return vin_all.at[:, jnp.where(c == 0, at, y), jnp.where(c == 0, x, at), :, chunk[n]]

    got(vin_all.at[:, y, x], "v0")
    for n in range(4):
        for t in (2, 1, 3):
            name = "v1%d%d" % (t, n)
            remote(block(0, n), block(0, n), name, line_one(t)).start()
            expect(name, block(t, n))
            leave(block(0, n), name)
        for t in (2, 1, 3):
            remote(block(0, n), block(0, n), "v2%d" % n, line_two(t)).start()
    gk_acc[...] = jnp.zeros_like(gk_acc)
    gv_acc[...] = jnp.zeros_like(gv_acc)
    gq_acc[...] = jnp.zeros_like(gq_acc)

    zn = z + 1 - 2 * (z % 2)
    zf = (z + 2) % 4

    got(kv.at[0, 0, pl.ds(0, SET)], "a_k")
    got(kv.at[0, 1, pl.ds(0, SET)], "a_v")
    got(kv.at[0, 0, pl.ds(SET, TXT)], "a_tk")
    got(kv.at[0, 1, pl.ds(SET, TXT)], "a_tv")

    def pass_on(src, dst, name, to):
        remote(src, dst, name, to).start()
        expect(name, dst)
        leave(src, name)

    pass_on(kv.at[0], kv.at[1], "b_kv", dev(dz=zn))
    got(qd.at[0, 0, pl.ds(0, SET)], "a_q")
    got(qd.at[0, 1, pl.ds(0, SET)], "a_d")
    got(qd.at[0, 0, pl.ds(SET, TXT)], "a_tq")
    got(qd.at[0, 1, pl.ds(SET, TXT)], "a_td")
    pass_on(qd.at[0], qd.at[1], "b_qz", dev(dz=zf))
    pass_on(qd.at[0], qd.at[2], "b_qc", dev(dc=1 - c))
    got(d_recv, "a_st")
    got(l_recv, "a_lse")
    for yy in range(4):
        st[0, yy:yy + 1, :] = LOG2E * (l_recv[0, yy:yy + 1, :] + l_recv[1, yy:yy + 1, :]
                                       + l_recv[2, yy:yy + 1, :] + l_recv[3, yy:yy + 1, :])
        st[0, 4 + yy:5 + yy, :] = (d_recv[4 * yy, 0:1, :] + d_recv[4 * yy + 1, 0:1, :]
                                   + d_recv[4 * yy + 2, 0:1, :] + d_recv[4 * yy + 3, 0:1, :])
    st[0, 8:9, :] = LOG2E * l_recv[0, 4:5, :]
    st[0, 9:10, :] = d_recv[z * 4 + x, 1:2, :]
    st[0, 10:16, :] = jnp.zeros((6, 128), F32)
    remote(st.at[0], st.at[1], "b_sz", dev(dz=zf)).start()
    remote(st.at[0], st.at[2], "b_sc", dev(dc=1 - c)).start()
    expect("b_sc", st.at[2])
    expect("b_sz", st.at[1])
    leave(st.at[0], "b_sc")
    leave(st.at[0], "b_sz")

    def forward(n):
        for t in (1, 3, 2):
            got(block(t, n), "v1%d%d" % (t, n))
            for u in (2, 1, 3):
                remote(block(t, n), block(t, n), "v2%d" % n, line_two(u)).start()

    for n in range(4):
        every = vin_all.at[:, pl.ds(0, 3), :, :, chunk[n]]
        expect("v2%d" % n, every)
        leave(every, "v2%d" % n)

    peers = [(j, m) for j in (2, 1, 3, 0) for m in (0, 1) if (j, m) != (0, 0)]
    quarter = pl.ds(pl.multiple_of(x * 768, 768), 768)

    got(tin_x, "tx")
    for src, clip in ((text_cols(dp), dp), (tin_x, 1 - dp)):
        place = tin_all.at[clip, c, y]
        local(src, place, "tin").start()
        for j, m in peers:
            remote(src, place, "tin", dev(dy=(y + j) % 4, dc=(c + m) % 2)).start()
    expect("tin", tin_all)
    leave(tr_recv.at[pl.ds(0, 7), :, pl.ds(0, 768)], "tin")

    def pair(lse_row, delta_row, query, dquery, keys, values):
        probs = jnp.exp2(nt(keys, query) * (FACTOR * LOG2E) - lse_row)
        dscores = (probs * (nt(values, dquery) - delta_row)).astype(BF16)
        return probs.astype(BF16), dscores

    def row512(i, first):
        return jnp.concatenate([st[i, first + n:first + n + 1, :] for n in range(4)], axis=1)

    def attend(step, carry):
        i = (step % 2) * 2 + step // 4
        j = ((step + 2) // 4) % 2

        @pl.when(step == 1)
        def _():
            got(qd.at[2], "b_qc")
            got(st.at[2], "b_sc")

        @pl.when(step == 2)
        def _():
            forward(0)
            forward(1)
            got(kv.at[1], "b_kv")

        @pl.when(step == 3)
        def _():
            forward(2)
            forward(3)

        @pl.when(step == 4)
        def _():
            got(qd.at[1], "b_qz")
            remote(qd.at[1], qd.at[3], "b_qf", dev(dc=1 - c)).start()
            got(st.at[1], "b_sz")
            remote(st.at[1], st.at[3], "b_sf", dev(dc=1 - c)).start()

        @pl.when(step == 5)
        def _():
            got(qd.at[3], "b_qf")
            got(st.at[3], "b_sf")

        query, dquery = qd[i, 0, 0:SET, :], qd[i, 1, 0:SET, :]
        keys, values = kv[j, 0], kv[j, 1]
        probs, dscores = pair(row512(i, 0), row512(i, 4), query, dquery, keys, values)
        gv_acc[j] += nn(probs, dquery)
        gk_acc[j] += nn(dscores, query)
        gq_acc[i, 0:SET, :] += tn(dscores, keys)
        return carry

    def attend_text(j):
        query = jnp.concatenate([qd[i, 0, SET:ROWS, :] for i in range(4)], axis=0)
        dquery = jnp.concatenate([qd[i, 1, SET:ROWS, :] for i in range(4)], axis=0)
        lse_row = jnp.zeros((8, 128), F32)
        delta_row = jnp.zeros((8, 128), F32)
        for i in range(4):
            one, two = (jnp.broadcast_to(st[i, r:r + 1, :], (8, 128)) for r in (8, 9))
            lse_row = lse_row + (pltpu.roll(one, 32 * i, 1) if i else one)
            delta_row = delta_row + (pltpu.roll(two, 32 * i, 1) if i else two)
        keys, values = kv[j, 0], kv[j, 1]
        probs, dscores = pair(lse_row[0:1, :], delta_row[0:1, :], query, dquery, keys, values)
        gv_acc[j] += nn(probs, dquery)
        gk_acc[j] += nn(dscores, query)
        from_text = tn(dscores, keys)
        for i in range(4):
            gq_acc[i, SET:ROWS, :] += from_text[32 * i:32 * i + 32, :]

    lax.fori_loop(0, 6, attend, 0)
    leave(qd.at[0], "b_qf")
    leave(st.at[0], "b_sf")
    attend_text(1)
    dkv_s[0] = (gk_acc[1] * FACTOR).astype(BF16)
    dkv_s[1] = gv_acc[1].astype(BF16)
    remote(dkv_s, dkv_r, "d_kv", dev(dz=zn)).start()
    expect("d_kv", dkv_r)
    leave(dkv_s, "d_kv")
    lax.fori_loop(6, 8, attend, 0)
    attend_text(0)
    dqc_s[0] = (gq_acc[2] * FACTOR).astype(BF16)
    dqc_s[1] = (gq_acc[3] * FACTOR).astype(BF16)
    remote(dqc_s, dqc_r, "d_qc", dev(dc=1 - c)).start()
    expect("d_qc", dqc_r)
    leave(dqc_s, "d_qc")
    got(dqc_r, "d_qc")
    dqz_s[...] = (gq_acc[1] * FACTOR + dqc_r[1].astype(F32)).astype(BF16)
    remote(dqz_s, dqz_r, "d_qz", dev(dz=zf)).start()
    expect("d_qz", dqz_r)
    leave(dqz_s, "d_qz")

    def send_grads(name, cols, table):
        own_part = gw.at[c, :, :, :, cols]
        remote(own_part, own_part, name, dev(dc=1 - c)).start()
        expect(name, gw.at[1 - c, :, :, :, cols])
        leave(own_part, name)
        for ch in table:
            for xx in (2, 1, 3, 0):
                to = (x + xx) % 4
                own = jnp.logical_and(xx == 0, c == mine)
                piece = gw.at[c, :, to, :, pl.ds(128 * ch, 128)]
                place = gs.at[c, :, :, pl.ds(pl.multiple_of(256 * ch + 128 * half, 128), 128)]

                @pl.when(jnp.logical_not(own))
                def _():
                    remote(piece, place, "e", dev(dx=to, dc=mine)).start()

                @pl.when(own)
                def _():
                    local(piece, place, "e").start()

    def finish_channel(ch, value):
        gw[c, :, :, :, 128 * ch:128 * ch + 128] = value[0:SET, :].reshape(4, 4, 32, 128)
        g_txt[:, 128 * ch:128 * ch + 128] = value[SET:ROWS, :]

    got(dkv_r, "d_kv")
    finish_channel(1, (gk_acc[0] * FACTOR + dkv_r[0].astype(F32)).astype(BF16))
    finish_channel(2, (gv_acc[0] + dkv_r[1].astype(F32)).astype(BF16))
    send_grads("gkv", pl.ds(128, 256), (1, 2))
    got(dqz_r, "d_qz")
    finish_channel(0, (gq_acc[0] * FACTOR + dqc_r[0].astype(F32) + dqz_r[...].astype(F32)).astype(BF16))
    send_grads("gq", pl.ds(0, 128), (0,))
    expect("e", gs)
    for ch in range(3):
        one = gw.at[0, :, 0, :, pl.ds(128 * ch, 128)]
        leave_if(c == mine, one, "e", 3)
        leave_if(c != mine, one, "e", 4)
    for xx in (2, 1, 3, 0):
        own = jnp.logical_and(xx == 0, c == mine)
        for ch in range(3):
            piece = g_txt.at[:, pl.ds(128 * ch, 128)]
            place = tgz.at[c, :, pl.ds(pl.multiple_of(256 * ch + 128 * half, 128), 128)]

            @pl.when(jnp.logical_not(own))
            def _():
                remote(piece, place, "te", dev(dx=(x + xx) % 4, dc=mine)).start()

            @pl.when(own)
            def _():
                local(piece, place, "te").start()
    expect("te", tgz)
    leave_if(c == mine, g_txt, "te", 3)
    leave_if(c != mine, g_txt, "te", 4)
    local(g_txt, tzz.at[dp, c, z], "tz").start()
    for t in (4, 3, 5, 2, 6, 1, 7):
        remote(g_txt, tzz.at[dp, c, z], "tz", along_z(t)).start()
    expect("tz", tzz.at[:, c])
    leave(tr_recv.at[pl.ds(0, 7), :, pl.ds(0, 384)], "tz")

    got(gw.at[1 - c, :, :, :, pl.ds(128, 256)], "gkv")
    got(gw.at[1 - c, :, :, :, pl.ds(0, 128)], "gq")
    grads = gw[...].reshape(1024, 384)
    col = nn(jnp.ones((8, 1024), BF16), grads)[0:1, :]

    def project(n):
        i = pairs[n]
        got(vin_all.at[:, pl.ds(0, 3), :, :, chunk[n]], "v2%d" % n)
        cols = pl.ds(pl.multiple_of(384 * i, 128), 384)
        part = tn(vin_all[:, :, :, :, cols].reshape(1024, 384), grads)
        m_acc[cols, :] = part
        gain = jnp.concatenate([gain_col[cols, :]] * 3, axis=1)
        shift = jnp.concatenate([shift_col[cols, :]] * 3, axis=1)
        term = gain * part + shift * col
        wt[2 * i] = term[0:192, :]
        wt[2 * i + 1] = term[192:384, :]

    def ring_to(way):
        to = (pos + (1 if way == 0 else 7)) % 8
        return dev(ddp=to // 4, dz=to % 4)

    def ring(step):
        for ch in range(3):
            lane_cols = slice(128 * ch, 128 * ch + 128)
            for way in range(2):
                dest = (pos + (4 - step if way == 0 else 4 + step)) % 8
                rows = (slice(0, 96) if way == 0 else slice(96, 192)) if step == 0 else slice(0, 192)
                own = wt[dest, rows, lane_cols]
                if step:
                    size = 96 if step == 1 else 192
                    heard = ring_r.at[way, step - 1, ch, pl.ds(0, size)]
                    got(heard, "r%d%d%d" % (way, step - 1, ch))
                    heard = heard[...].astype(F32)
                    if step == 1:
                        near, far = own[0:96, :], own[96:192, :]
                        pair_ = (near + heard, far) if way == 0 else (near, far + heard)
                        own = jnp.concatenate(pair_, axis=0)
                    else:
                        own = own + heard
                size = 96 if step == 0 else 192
                out_ref = ring_s.at[way, step, ch, pl.ds(0, size)]
                out_ref[...] = own.astype(BF16)
                name = "r%d%d%d" % (way, step, ch)
                remote(out_ref, ring_r.at[way, step, ch, pl.ds(0, size)], name, ring_to(way)).start()
                expect(name, ring_r.at[way, step, ch, pl.ds(0, size)])
                leave(out_ref, name)

    def back_chunk(n):
        cols = slice(512 * n, 512 * n + 512)
        rows = gs[...].reshape(256, 768)
        term = (nt(rows[:, 0:256], l_w[0, cols, :]) + nt(rows[:, 256:512], l_w[1, cols, :])
                + nt(rows[:, 512:768], l_w[2, cols, :]))

        @pl.when(c == 0)
        def _():
            b_own[:, cols] = term[0:128, :]
            b_send[:, cols] = term[128:256, :].astype(BF16)

        @pl.when(c == 1)
        def _():
            b_own[:, cols] = term[128:256, :]
            b_send[:, cols] = term[0:128, :].astype(BF16)
        remote(b_send.at[:, cols], b_recv.at[:, cols], "bc%d" % n, dev(dc=1 - c)).start()
        expect("bc%d" % n, b_recv.at[:, cols])
        leave(b_send.at[:, cols], "bc%d" % n)

    def gather_chunk(n):
        cols = slice(512 * n, 512 * n + 512)
        got(b_recv.at[:, cols], "bc%d" % n)
        total = b_own[:, cols] + b_recv[:, cols].astype(F32)
        b_own[:, cols] = total
        for yy in range(4):
            y_send[yy, :, cols] = total[32 * yy:32 * yy + 32, :].astype(BF16)

            @pl.when(yy != y)
            def _():
                remote(y_send.at[yy, :, cols], y_recv.at[y, :, cols], "by", dev(dy=yy)).start()

    project(0)
    ring(0)
    project(1)
    project(2)
    project(3)
    got(wq, "wq")
    for m in range(8):
        rows = slice(192 * m, 192 * m + 192)
        zero = jnp.zeros((192, 128), F32)
        one = jnp.zeros((192, 128), F32)
        for ch in range(3):
            w_part = wq[ch, rows, :].astype(F32)
            zero = zero + w_part * col[:, 128 * ch:128 * ch + 128]
            one = one + w_part * m_acc[rows, 128 * ch:128 * ch + 128]
        s_acc[0, rows, :] = zero
        s_acc[1, rows, :] = one
    for n in range(2):
        high = s_acc[n].astype(BF16)
        low = (s_acc[n] - high.astype(F32)).astype(BF16)
        row = jnp.ones((8, 128), BF16)
        s1_buf[me, n:n + 1, :] = (nt(row, high) + nt(row, low))[0:1, :]

    for i, j in plane:
        remote(s1_buf.at[me], s1_buf.at[me], "s1", dev(dx=chip(i, j)[0], dy=chip(i, j)[1])).start()
    expect("s1", s1_buf.at[pl.ds(0, 15)])
    leave(s1_buf.at[pl.ds(0, 15)], "s1")
    got(tgz, "te")
    ready("tw")
    rows = tgz[...].reshape(64, 768)
    term = (nt(rows[:, 0:256], l_tw[0]) + nt(rows[:, 256:512], l_tw[1]) + nt(rows[:, 512:768], l_tw[2]))
    for core in range(2):
        tr_send[core] = term[32 * core:32 * core + 32, :].astype(BF16)
        own = jnp.logical_and(y == z, c == core)

        @pl.when(jnp.logical_not(own))
        def _():
            remote(tr_send.at[core], tr_recv.at[head], "tr", dev(dy=z, dc=core)).start()

        @pl.when(own)
        def _():
            local(tr_send.at[core], tr_recv.at[head], "tr").start()
    leave_if(y == z, tr_send.at[0], "tr")
    leave_if(y != z, tr_send, "tr")

    ring(1)
    ready("w")
    got(gs, "e")
    for n in range(6):
        back_chunk(n)

    for n in range(6):
        gather_chunk(n)
    expect("by", y_recv.at[pl.ds(0, 3)])
    leave(y_send.at[pl.ds(0, 3)], "by")

    @pl.when(y == z)
    def _():
        got(tr_recv, "tr")
        tback = tr_recv[0].astype(F32)
        for hd in range(1, 8):
            tback = tback + tr_recv[hd].astype(F32)
        tdn_all[x] = ((1.0 + l_tmod[1:2, quarter]) * tback).astype(BF16)
        for t in (2, 1, 3):
            remote(tdn_all.at[x], tdn_all.at[x], "tdz", dev(dz=(z + t) % 4)).start()
        ts_buf[c] = jnp.concatenate([
            jnp.sum(tback, axis=0, keepdims=True),
            jnp.sum(tback * l_tnrm[:, quarter].astype(F32), axis=0, keepdims=True)], axis=0)
        for j, m in peers:
            remote(ts_buf.at[c], ts_buf.at[c], "ts", dev(dy=(y + j) % 4, dc=(c + m) % 2)).start()
    leave_if(y == z, tdn_all.at[pl.ds(0, 3)], "tdz")
    for _ in range(7):
        leave_if(y == z, ts_buf.at[0], "ts")

    ring(2)
    got(tzz.at[:, c], "tz")
    remote(tzz.at[:, c], tzz.at[:, c], "tzs", dev(dc=1 - c)).start()
    expect("tzs", tzz.at[:, 1 - c])
    leave(tzz.at[:, c], "tzs")

    got(s1_buf.at[pl.ds(0, 15)], "s1")
    stat = s1_buf[0]
    for t in range(1, 16):
        stat = stat + s1_buf[t]
    s2_buf[z] = stat
    for t in (2, 1, 3):
        remote(s2_buf.at[z], s2_buf.at[z], "s2", dev(dz=(z + t) % 4)).start()
    expect("s2", s2_buf.at[pl.ds(0, 3)])
    leave(s2_buf.at[pl.ds(0, 3)], "s2")
    ring(3)
    @pl.when(y == z)
    def _():
        got(ts_buf.at[0], "ts")

    @pl.when(y != z)
    def _():
        got(ts_buf, "ts")
        got(tdn_all.at[x], "tdz")
    for t in (2, 1, 3):
        remote(tdn_all.at[x], tdn_all.at[x], "tdn", dev(dx=(x + t) % 4)).start()
    expect("tdn", tdn_all.at[pl.ds(0, 3)])
    leave(tdn_all.at[pl.ds(0, 3)], "tdn")
    ts2_buf[z] = ts_buf[0] + ts_buf[1]
    for t in (2, 1, 3):
        remote(ts2_buf.at[z], ts2_buf.at[z], "ts2", dev(dz=(z + t) % 4)).start()
    expect("ts2", ts2_buf.at[pl.ds(0, 3)])
    leave(ts2_buf.at[pl.ds(0, 3)], "ts2")

    got(tzz.at[:, 1 - c], "tzs")
    got(tin_all, "tin")
    tw_s[...] = tn(tin_all[...].reshape(512, 384), tzz[...].reshape(512, 384)).astype(BF16)
    for n in range(2):
        for ch in range(3):
            rows = pl.ds(pl.multiple_of(192 * c + 96 * n, 32), 96)
            tf_s[n, ch] = tw_s[rows, 128 * ch:128 * ch + 128]
        own = jnp.logical_and(c == mine, n == half)

        @pl.when(jnp.logical_not(own))
        def _():
            remote(tf_s.at[n], tf_r.at[half], "tf", dev(dx=2 * c + n, dc=mine)).start()

        @pl.when(own)
        def _():
            local(tf_s.at[n], tf_r.at[half], "tf").start()
    expect("tf", tf_r)
    leave_if(c == mine, tf_s.at[0], "tf")
    leave_if(c != mine, tf_s, "tf")

    for ch in range(3):
        lane_cols = slice(128 * ch, 128 * ch + 128)
        total = wt[pos, :, lane_cols]
        for way in range(2):
            got(ring_r.at[way, 3, ch], "r%d3%d" % (way, ch))
            total = total + ring_r[way, 3, ch].astype(F32)
        fin_s[0, ch] = total[0:96, :].astype(BF16)
        fin_s[1, ch] = total[96:192, :].astype(BF16)
    for n in range(2):
        own = jnp.logical_and(c == mine, n == half)

        @pl.when(jnp.logical_not(own))
        def _():
            remote(fin_s.at[n], fin_r.at[half], "fin", dev(dx=2 * c + n, dc=mine)).start()

        @pl.when(own)
        def _():
            local(fin_s.at[n], fin_r.at[half], "fin").start()
    expect("fin", fin_r)
    leave_if(c == mine, fin_s.at[0], "fin")
    leave_if(c != mine, fin_s, "fin")

    got(s2_buf.at[pl.ds(0, 3)], "s2")
    s3_buf[c] = s2_buf[0] + s2_buf[1] + s2_buf[2] + s2_buf[3]
    remote(s3_buf.at[c], s3_buf.at[c], "s3", dev(dc=1 - c)).start()
    expect("s3", s3_buf.at[0])
    leave(s3_buf.at[0], "s3")

    got(ts2_buf.at[pl.ds(0, 3)], "ts2")
    tsx_buf[x] = ts2_buf[0] + ts2_buf[1] + ts2_buf[2] + ts2_buf[3]
    for t in (2, 1, 3):
        remote(tsx_buf.at[x], tsx_buf.at[x], "tsx", dev(dx=(x + t) % 4)).start()
    expect("tsx", tsx_buf.at[pl.ds(0, 3)])
    leave(tsx_buf.at[pl.ds(0, 3)], "tsx")

    def write(n, src):
        pltpu.make_async_copy(src, results[n], os_.at[n]).start()

    got(s3_buf.at[0], "s3")
    for m in range(8):
        o_vs[:, 384 * m:384 * m + 384] = jnp.concatenate(
            [s3_buf[core, :, 192 * m:192 * m + 192] for core in range(2)], axis=1)
    write(4, o_vs)
    got(y_recv.at[pl.ds(0, 3)], "by")
    back = b_own[rows32(y), :]
    for yy in range(4):
        back = back + jnp.where(yy == y, 0.0, y_recv[yy].astype(F32))
    o_dn[...] = ((1.0 + l_mod[1:2, :]) * back).astype(BF16)
    write(0, o_dn)
    got(tdn_all.at[pl.ds(0, 3)], "tdn")
    for xx in range(4):
        o_tdn[:, 768 * xx:768 * xx + 768] = tdn_all[xx]
    write(1, o_tdn)
    got(tsx_buf.at[pl.ds(0, 3)], "tsx")
    for xx in range(4):
        o_ts[:, 768 * xx:768 * xx + 768] = tsx_buf[xx]
    write(5, o_ts)
    got(fin_r, "fin")
    for ch in range(3):
        for j in range(2):
            o_wg[ch, :, 128 * j:128 * j + 128] = fin_r[j, ch].astype(F32)
    write(2, o_wg)
    got(tf_r, "tf")
    for ch in range(3):
        for j in range(2):
            o_twg[ch, :, 128 * j:128 * j + 128] = tf_r[j, ch].astype(F32)
    write(3, o_twg)
    for n, src in enumerate((o_dn, o_tdn, o_wg, o_twg, o_vs, o_ts)):
        pltpu.make_async_copy(src, results[n], os_.at[n]).wait()


def finish(*refs):
    into = [pltpu.make_async_copy(refs[n], refs[12 + n], refs[18].at[n]) for n in range(6)]
    back = [pltpu.make_async_copy(refs[12 + n], refs[6 + n], refs[18].at[n]) for n in range(6)]
    for copy in into:
        copy.start()
    for first, second in zip(into, back):
        first.wait()
        second.start()
    for copy in back:
        copy.wait()


SCRATCH = (
    ((32, D), BF16), ((32, D), BF16), ((3, 96, 256), F32), ((3, 96, 256), F32), ((2, D), F32), ((2, D), F32),
    ((32, 2048), BF16), ((32, 2048), BF16), ((32, 2048), BF16), ((32, 2048), BF16),
    ((32, D), BF16), ((32, D), BF16), ((3, D, 256), BF16), ((3, 768, 256), BF16),
    ((2, 256), F32), ((2, 256), F32), ((2, D), F32), ((2, D), F32),
    ((4, 2, ROWS, 128), BF16), ((2, 2, ROWS, 128), BF16), ((4, 16, 128), F32),
    ((16, 8, 128), F32), ((16, 8, 128), F32), ((2, 2, 8, 128), F32), ((4, 8, 128), F32),
    ((2, ROWS, 128), F32), ((2, ROWS, 128), F32), ((4, ROWS, 128), F32),
    ((2, ROWS, 128), BF16), ((2, ROWS, 128), BF16), ((2, ROWS, 128), BF16), ((2, ROWS, 128), BF16),
    ((ROWS, 128), BF16), ((ROWS, 128), BF16), ((2, 4, 4, 32, 384), BF16), ((32, 384), BF16),
    ((2, 32, 1536), BF16), ((2, 4, 4, 32, 1536), BF16), ((3, 1536, 128), BF16),
    ((1536, 128), F32), ((1536, 128), F32), ((1536, 384), F32), ((2, 1536, 128), F32), ((32, D), BF16), ((32, 384), BF16), ((2, 2, 4, 32, 384), BF16),
    ((2, 2, 4, 32, 384), BF16), ((2, 32, 768), BF16), ((2, 4, 32, 768), BF16),
    ((8, 192, 384), F32), ((2, 4, 3, 192, 128), BF16), ((2, 4, 3, 192, 128), BF16),
    ((2, 3, 96, 128), BF16), ((2, 3, 96, 128), BF16),
    ((128, D), BF16), ((128, D), BF16), ((128, D), F32), ((4, 32, D), BF16), ((4, 32, D), BF16),
    ((2, 32, 768), BF16), ((8, 32, 768), BF16), ((4, 32, 768), BF16), ((2, 2, 768), F32), ((4, 2, 768), F32), ((4, 2, 768), F32),
    ((16, 2, 1536), F32), ((4, 2, 1536), F32), ((2, 2, 1536), F32),
    ((384, 384), BF16), ((2, 3, 96, 128), BF16), ((2, 3, 96, 128), BF16),
)


def body(
    video_q, video_k, video_v, video_out, video_dout, text_q, text_k, text_v, text_out, text_dout,
    video_lse, text_lse, video_norm, text_norm, video_mod, text_mod, video_weight, text_weight,
):
    args = [a[0] for a in (
        video_q, video_k, video_v, video_out, video_dout, text_q, text_k, text_v, text_out, text_dout,
        video_lse, text_lse, video_norm, text_norm, video_mod, text_mod)]
    args += [jnp.transpose(w, (1, 0, 2)) for w in (video_weight, text_weight)]
    results = pl.pallas_call(
        kernel,
        out_shape=(
            jax.ShapeDtypeStruct((32, D), BF16), jax.ShapeDtypeStruct((32, D), BF16),
            jax.ShapeDtypeStruct((3, 96, 256), F32), jax.ShapeDtypeStruct((3, 96, 256), F32),
            jax.ShapeDtypeStruct((2, D), F32), jax.ShapeDtypeStruct((2, D), F32),
        ),
        in_specs=[pl.BlockSpec(memory_space=pl.ANY)] * len(args),
        out_specs=[pl.BlockSpec(memory_space=pl.ANY)] * 6,
        scratch_shapes=[pltpu.VMEM(shape, kind) for shape, kind in SCRATCH] + [
            pltpu.SemaphoreType.DMA((len(NAMES),)),
            pltpu.SemaphoreType.DMA((len(NAMES),)),
            pltpu.SemaphoreType.DMA((len(LOCALS),)),
            pltpu.SemaphoreType.DMA((6,)),
        ],
        compiler_params=pltpu.CompilerParams(collective_id=0, has_side_effects=True, vmem_limit_bytes=60 * 1024 * 1024),
    )(*args)
    anywhere = pl.BlockSpec(memory_space=pl.ANY)
    dn, tdn, wg, twg, vs, ts = pl.pallas_call(
        finish,
        out_shape=[jax.ShapeDtypeStruct(r.shape, r.dtype) for r in results],
        in_specs=[anywhere] * 6,
        out_specs=[anywhere] * 6,
        scratch_shapes=[pltpu.VMEM(r.shape, r.dtype) for r in results] + [pltpu.SemaphoreType.DMA((6,))],
        compiler_params=pltpu.CompilerParams(vmem_limit_bytes=60 * 1024 * 1024),
    )(*results)
    return (
        dn[None], tdn[None], jnp.transpose(wg, (1, 0, 2)), jnp.transpose(twg, (1, 0, 2)), vs[None], ts[None],
    )


def solution(mesh):
    tokens = P("dp", ("blk", "head"), None)
    text = P("dp", "head", None)
    whole = P("dp", None, None)
    columns = P(None, None, "head")
    return jax.shard_map(
        body,
        mesh=mesh,
        in_specs=(tokens,) * 5 + (text,) * 5 + (
            P("dp", "head", "blk"), P("dp", "head", None), tokens, text, whole, whole, columns, columns),
        out_specs=(
            tokens, text, P(("dp", "blk"), None, "head"), P(("dp", "blk"), None, "head"), whole, whole),
        check_vma=False,
    )
```

```python
import functools

import jax
import jax.numpy as jnp
from jax import lax
from jax.experimental import pallas as pl
from jax.experimental.pallas import tpu as pltpu
from jax.sharding import PartitionSpec as P

MESH = pl.DeviceIdType.MESH
D = 3072
DH = 128
SET = 512
ROWS = 544
TXT = 32
FACTOR = DH ** (-0.5)
LOG2E = 1.4426950408889634
F32 = jnp.float32
BF16 = jnp.bfloat16

NAMES = (
    "a_q", "a_d", "a_k", "a_v", "a_st", "a_lse", "a_tq", "a_td", "a_tk", "a_tv",
    "b_kv", "b_qc", "b_sc", "b_qz", "b_sz", "b_qf", "b_sf", "v0", "wq", "tin",
    "d_kv", "d_qc", "d_qz", "gkv", "gq", "e", "tz", "tzs", "te",
    "bc0", "bc1", "bc2", "bc3", "bc4", "bc5", "by", "tr", "tdz", "tdn", "ts", "ts2", "tsx", "s1", "s2", "s3", "tx", "tf", "fin",
)
RING = tuple("r%d%d%d" % (way, step, ch) for way in range(2) for step in range(4) for ch in range(3))
INPUTS = tuple("v1%d%d" % (t, n) for t in (1, 2, 3) for n in range(4)) + tuple("v2%d" % n for n in range(4))
NAMES = NAMES + RING + INPUTS
SEM = {name: index for index, name in enumerate(NAMES)}
LOCALS = ("out", "dout", "tout", "tdout", "nrm", "tnrm", "w", "tw", "lse", "tlse", "mod", "tmod")


def nt(left, right):
    return lax.dot_general(left, right, (((1,), (1,)), ((), ())), preferred_element_type=F32)


def tn(left, right):
    return lax.dot_general(left, right, (((0,), (0,)), ((), ())), preferred_element_type=F32)


def nn(left, right):
    return jnp.dot(left, right, preferred_element_type=F32)


def kernel(*refs):
    drains = []
    kernel_body(drains, *refs)
    drains[0]()


def kernel_body(
    drains,
    q, k, v, out, dout, tq, tk, tv, tout, tdout, lse, tlse, norm, tnorm, mod, tmod, weight, tweight,
    r_dn, r_tdn, r_wg, r_twg, r_vs, r_ts,
    o_dn, o_tdn, o_wg, o_twg, o_vs, o_ts,
    l_out, l_dout, l_tout, l_tdout, l_nrm, l_tnrm, l_w, l_tw, l_lse, l_tlse, l_mod, l_tmod,
    qd, kv, st, d_send, d_recv, l_send, l_recv,
    gk_acc, gv_acc, gq_acc, dkv_s, dkv_r, dqc_s, dqc_r, dqz_s, dqz_r, gw, g_txt,
    vin_s, vin_all, wq, gain_col, shift_col, m_acc, s_acc, tin_s, tin_x, tin_all, tzz, tgz, gs,
    wt, ring_s, ring_r, fin_s, fin_r, b_send, b_recv, b_own, y_send, y_recv,
    tr_send, tr_recv, tdn_all, ts_buf, ts2_buf, tsx_buf, s1_buf, s2_buf, s3_buf, tw_s, tf_s, tf_r,
    rs, ss, ls, os_,
):
    results = (r_dn, r_tdn, r_wg, r_twg, r_vs, r_ts)
    dp = lax.axis_index("dp")
    blk = lax.axis_index("blk")
    head = lax.axis_index("head")
    z, x, y, c = blk // 4, blk % 4, head // 2, head % 2
    me = y * 4 + x
    mine = x // 2
    half = x % 2

    def dev(dz=None, dx=None, dy=None, dc=None, ddp=None):
        zz = z if dz is None else dz
        xx = x if dx is None else dx
        yy = y if dy is None else dy
        cc = c if dc is None else dc
        return {"dp": dp if ddp is None else ddp, "blk": zz * 4 + xx, "head": yy * 2 + cc}

    def remote(src, dst, name, to):
        return pltpu.make_async_remote_copy(
            src_ref=src, dst_ref=dst, send_sem=ss.at[SEM[name]], recv_sem=rs.at[SEM[name]],
            device_id=to, device_id_type=MESH)

    def local(src, dst, name):
        return pltpu.make_async_copy(src, dst, rs.at[SEM[name]])

    def got(ref, name):
        pltpu.make_async_copy(ref, ref, rs.at[SEM[name]]).wait()
        if name in expected:
            expected[name].pop(0)

    def sent(ref, name):
        pltpu.make_async_copy(ref, ref, ss.at[SEM[name]]).wait()

    expected = {}
    copies = {}
    leaving = []

    def expect(name, *refs):
        expected[name] = list(refs)

    def drain():
        for name, refs in list(expected.items()):
            for ref in list(refs):
                got(ref, name)
        for n_, cp in list(copies.items()):
            if n_ not in waited:
                cp.wait()
        for fn in leaving:
            fn()

    waited = set()
    drains.append(drain)

    def ready(name):
        copies[name].wait()
        waited.add(name)

    def leave(ref, name, times=1):
        def fn():
            for _ in range(times):
                sent(ref, name)
        leaving.append(fn)

    def leave_if(cond, ref, name, times=1):
        def fn():
            @pl.when(cond)
            def _():
                for _ in range(times):
                    sent(ref, name)
        leaving.append(fn)

    def rows32(index):
        return pl.ds(pl.multiple_of(index * 32, 32), 32)

    def lanes(index, width=128):
        return pl.ds(pl.multiple_of(index * width, 128), width)

    barrier = pltpu.get_barrier_semaphore()

    plane = [(i, j) for i in (2, 1, 3, 0) for j in (2, 1, 3, 0) if (i, j) != (0, 0)]
    pos = dp * 4 + z

    def chip(i, j):
        return (x + i) % 4, (y + j) % 4

    def along_z(t):
        at = (pos + t) % 8
        return dev(ddp=at // 4, dz=at % 4)

    greeted = [dev(dx=chip(i, j)[0], dy=chip(i, j)[1]) for i, j in plane]
    greeted += [along_z(t) for t in (4, 3, 5, 2, 6, 1, 7)]
    greeted += [dev(dx=(x + i) % 4, dc=1 - c) for i in (2, 1, 3)]
    greeted += [dev(dy=(y + j) % 4, dc=1 - c) for j in (2, 1, 3)] + [dev(dc=1 - c)]
    for to in greeted:
        pl.semaphore_signal(barrier, inc=1, device_id=to, device_id_type=MESH)
    pl.semaphore_wait(barrier, 29)

    def send_a(table):
        place_at = rows32(me)
        for i, j in plane + [(0, 0)]:
            xx, yy = chip(i, j)
            to = dev(dx=xx, dy=yy)
            for src, dst, name in table:
                piece = src.at[:, lanes(4 * yy + xx)]
                if (i, j) == (0, 0):
                    local(piece, dst.at[place_at], name).start()
                else:
                    remote(piece, dst.at[place_at], name, to).start()

    def send_text(table):
        @pl.when(y == z)
        def _():
            for j in (2, 1, 3, 0):
                yy = (y + j) % 4
                for src, dst, name in table:
                    piece = src.at[:, lanes(4 * yy + x)]
                    place = dst.at[pl.ds(SET, TXT)]
                    if j:
                        remote(piece, place, name, dev(dy=yy)).start()
                    else:
                        local(piece, place, name).start()

    send_a(((k, kv.at[0, 0], "a_k"), (v, kv.at[0, 1], "a_v")))
    send_text(((tk, kv.at[0, 0], "a_tk"), (tv, kv.at[0, 1], "a_tv")))
    send_a(((q, qd.at[0, 0], "a_q"), (dout, qd.at[0, 1], "a_d")))
    send_text(((tq, qd.at[0, 0], "a_tq"), (tdout, qd.at[0, 1], "a_td")))
    for name, ref in (("a_k", kv.at[0, 0, pl.ds(0, SET)]), ("a_v", kv.at[0, 1, pl.ds(0, SET)]),
                      ("a_q", qd.at[0, 0, pl.ds(0, SET)]), ("a_d", qd.at[0, 1, pl.ds(0, SET)])):
        expect(name, ref)
        leave(kv.at[0, 0, pl.ds(0, 480)], name)
    for name, ref in (("a_tk", kv.at[0, 0, pl.ds(SET, TXT)]), ("a_tv", kv.at[0, 1, pl.ds(SET, TXT)]),
                      ("a_tq", qd.at[0, 0, pl.ds(SET, TXT)]), ("a_td", qd.at[0, 1, pl.ds(SET, TXT)])):
        expect(name, ref)
        leave_if(y == z, kv.at[0, 0, pl.ds(0, 96)], name)

    @pl.when(c == mine)
    def _():
        for core in range(2):
            for m in range(8):
                piece = weight.at[:, pl.ds(384 * m + 192 * core, 192), lanes(half)]
                place = wq.at[:, pl.ds(192 * m, 192), :]

                @pl.when(c != core)
                def _():
                    remote(piece, place, "wq", dev(dc=core)).start()

                @pl.when(c == core)
                def _():
                    local(piece, place, "wq").start()
    expect("wq", wq)
    leave_if(c == mine, wq, "wq")
    loads = {
        "out": (out, l_out), "dout": (dout, l_dout), "tout": (tout, l_tout), "tdout": (tdout, l_tdout),
        "nrm": (norm, l_nrm), "tnrm": (tnorm, l_tnrm), "lse": (lse, l_lse), "tlse": (tlse, l_tlse),
        "mod": (mod, l_mod), "tmod": (tmod, l_tmod), "w": (weight, l_w),
        "tw": (tweight.at[:, pl.ds(pl.multiple_of(x * 768, 768), 768), :], l_tw),
    }
    copies.update({n: pltpu.make_async_copy(s, d, ls.at[LOCALS.index(n)]) for n, (s, d) in loads.items()})
    for name in ("out", "dout", "lse", "tlse", "tout", "tdout", "nrm", "mod", "tnrm", "tmod", "w", "tw"):
        copies[name].start()


    lane = lax.broadcasted_iota(jnp.int32, (16, 128), 1)
    ones = jnp.where(
        lax.broadcasted_iota(jnp.int32, (16, 2048), 1) // DH
        == lax.broadcasted_iota(jnp.int32, (16, 2048), 0), 1.0, 0.0).astype(BF16)

    def delta_rows(a_ref, b_ref):
        total = jnp.zeros((16, 128), F32)
        products = a_ref[...].astype(F32) * b_ref[...].astype(F32)
        high = products.astype(BF16)
        low = (products - high.astype(F32)).astype(BF16)
        for part in (high, low):
            total = total + nt(ones, jnp.concatenate([part] * 4, axis=0))
        return total

    ready("out")
    ready("dout")
    video_delta = jnp.where(lane // 32 == x, delta_rows(l_out, l_dout), 0.0)
    ready("tout")
    ready("tdout")
    text_delta = jnp.where(lane < 32, delta_rows(l_tout, l_tdout), 0.0)
    d_send[...] = jnp.zeros_like(d_send)
    for h in range(16):
        d_send[h, 0:1, :] = video_delta[h:h + 1, :]
        d_send[h, 1:2, :] = text_delta[h:h + 1, :]

    for i, j in plane:
        xx, yy = chip(i, j)
        remote(d_send.at[yy * 4 + xx], d_recv.at[me], "a_st", dev(dx=xx, dy=yy)).start()
    local(d_send.at[me], d_recv.at[me], "a_st").start()
    expect("a_st", d_recv)
    leave(d_recv.at[pl.ds(0, 15)], "a_st")

    ready("lse")
    ready("tlse")
    lane8 = lax.broadcasted_iota(jnp.int32, (8, 128), 1)
    l_send[...] = jnp.zeros_like(l_send)
    for j in range(2):
        for cc in range(2):
            for yy in range(4):
                row = jnp.broadcast_to(l_lse[j:j + 1, 128 * (yy // 2):128 * (yy // 2) + 128], (8, 128))
                shift = (32 * x + 256 - (yy % 2) * 64 - cc * 32) % 128
                row = jnp.where(lane8 // 32 == x, pltpu.roll(row, shift, 1), 0.0)
                l_send[j, cc, yy:yy + 1, :] = row[0:1, :]
            row = jnp.broadcast_to(l_tlse[j:j + 1, pl.ds(pl.multiple_of((z // 2) * 128, 128), 128)], (8, 128))
            shift = (256 - (z % 2) * 64 - cc * 32) % 128
            row = jnp.where(lane8 < 32, pltpu.roll(row, shift, 1), 0.0)
            l_send[j, cc, 4:5, :] = row[0:1, :]
    for j in range(2):
        for cc in range(2):
            own = jnp.logical_and(x == 2 * c + j, c == cc)

            @pl.when(jnp.logical_not(own))
            def _():
                remote(l_send.at[j, cc], l_recv.at[x], "a_lse", dev(dx=2 * c + j, dc=cc)).start()

            @pl.when(own)
            def _():
                local(l_send.at[j, cc], l_recv.at[x], "a_lse").start()

    expect("a_lse", l_recv)
    leave_if(c == mine, l_recv.at[pl.ds(0, 3)], "a_lse")
    leave_if(c != mine, l_recv, "a_lse")

    ready("nrm")
    ready("mod")

    def group(value, core):
        return jnp.concatenate([value[:, 384 * m + 192 * core:384 * m + 192 * core + 192] for m in range(8)], axis=1)

    nrm = l_nrm[...].astype(F32)
    for core in range(2):
        vin_s[core] = group(nrm, core).astype(BF16)
    local(vin_s.at[c], vin_all.at[c, y, x], "v0").start()
    remote(vin_s.at[1 - c], vin_all.at[c, y, x], "v0", dev(dc=1 - c)).start()
    expect("v0", vin_all.at[:, y, x])
    leave(vin_s.at[0], "v0")
    grouped = jnp.where(c == 0, group(l_mod[...], 0), group(l_mod[...], 1))
    shift_col[...] = jnp.transpose(jnp.broadcast_to(grouped[0:1, :], (128, 1536)))
    gain_col[...] = jnp.transpose(jnp.broadcast_to(1.0 + grouped[1:2, :], (128, 1536)))
    ready("tnrm")
    ready("tmod")
    tgain = 1.0 + l_tmod[1:2, :]
    tin_s[...] = (tgain * l_tnrm[...].astype(F32) + l_tmod[0:1, :]).astype(BF16)

    def text_cols(clip):
        return tin_s.at[:, pl.ds(pl.multiple_of(clip * 1536 + z * 384, 128), 384)]

    remote(text_cols(1 - dp), tin_x, "tx", dev(ddp=1 - dp)).start()
    expect("tx", tin_x)
    leave(tin_x, "tx")

    along = jnp.where(c == 0, y, x)

    def line_one(t):
        to = (along + t) % 4
        return dev(dx=jnp.where(c == 0, x, to), dy=jnp.where(c == 0, to, y))

    def line_two(t):
        to = (jnp.where(c == 0, x, y) + t) % 4
        return dev(dx=jnp.where(c == 0, to, x), dy=jnp.where(c == 0, y, to))

    first_pair = ((pos + 4) // 2) % 4
    pairs = [(first_pair + n) % 4 for n in (0, 1, 3, 2)]
    chunk = [pl.ds(pl.multiple_of(384 * i, 128), 384) for i in pairs]

    def block(t, n):
        at = (along + 4 - t) % 4
        return vin_all.at[:, jnp.where(c == 0, at, y), jnp.where(c == 0, x, at), :, chunk[n]]

    got(vin_all.at[:, y, x], "v0")
    for n in range(4):
        for t in (2, 1, 3):
            name = "v1%d%d" % (t, n)
            remote(block(0, n), block(0, n), name, line_one(t)).start()
            expect(name, block(t, n))
            leave(block(0, n), name)
        for t in (2, 1, 3):
            remote(block(0, n), block(0, n), "v2%d" % n, line_two(t)).start()
    gk_acc[...] = jnp.zeros_like(gk_acc)
    gv_acc[...] = jnp.zeros_like(gv_acc)
    gq_acc[...] = jnp.zeros_like(gq_acc)

    zn = z + 1 - 2 * (z % 2)
    zf = (z + 2) % 4

    got(kv.at[0, 0, pl.ds(0, SET)], "a_k")
    got(kv.at[0, 1, pl.ds(0, SET)], "a_v")
    got(kv.at[0, 0, pl.ds(SET, TXT)], "a_tk")
    got(kv.at[0, 1, pl.ds(SET, TXT)], "a_tv")

    def pass_on(src, dst, name, to):
        remote(src, dst, name, to).start()
        expect(name, dst)
        leave(src, name)

    pass_on(kv.at[0], kv.at[1], "b_kv", dev(dz=zn))
    got(qd.at[0, 0, pl.ds(0, SET)], "a_q")
    got(qd.at[0, 1, pl.ds(0, SET)], "a_d")
    got(qd.at[0, 0, pl.ds(SET, TXT)], "a_tq")
    got(qd.at[0, 1, pl.ds(SET, TXT)], "a_td")
    pass_on(qd.at[0], qd.at[1], "b_qz", dev(dz=zf))
    pass_on(qd.at[0], qd.at[2], "b_qc", dev(dc=1 - c))
    got(d_recv, "a_st")
    got(l_recv, "a_lse")
    for yy in range(4):
        st[0, yy:yy + 1, :] = LOG2E * (l_recv[0, yy:yy + 1, :] + l_recv[1, yy:yy + 1, :]
                                       + l_recv[2, yy:yy + 1, :] + l_recv[3, yy:yy + 1, :])
        st[0, 4 + yy:5 + yy, :] = (d_recv[4 * yy, 0:1, :] + d_recv[4 * yy + 1, 0:1, :]
                                   + d_recv[4 * yy + 2, 0:1, :] + d_recv[4 * yy + 3, 0:1, :])
    st[0, 8:9, :] = LOG2E * l_recv[0, 4:5, :]
    st[0, 9:10, :] = d_recv[z * 4 + x, 1:2, :]
    st[0, 10:16, :] = jnp.zeros((6, 128), F32)
    remote(st.at[0], st.at[1], "b_sz", dev(dz=zf)).start()
    remote(st.at[0], st.at[2], "b_sc", dev(dc=1 - c)).start()
    expect("b_sc", st.at[2])
    expect("b_sz", st.at[1])
    leave(st.at[0], "b_sc")
    leave(st.at[0], "b_sz")

    def forward(n):
        for t in (1, 3, 2):
            got(block(t, n), "v1%d%d" % (t, n))
            for u in (2, 1, 3):
                remote(block(t, n), block(t, n), "v2%d" % n, line_two(u)).start()

    for n in range(4):
        every = vin_all.at[:, pl.ds(0, 3), :, :, chunk[n]]
        expect("v2%d" % n, every)
        leave(every, "v2%d" % n)

    peers = [(j, m) for j in (2, 1, 3, 0) for m in (0, 1) if (j, m) != (0, 0)]
    quarter = pl.ds(pl.multiple_of(x * 768, 768), 768)

    got(tin_x, "tx")
    for src, clip in ((text_cols(dp), dp), (tin_x, 1 - dp)):
        place = tin_all.at[clip, c, y]
        local(src, place, "tin").start()
        for j, m in peers:
            remote(src, place, "tin", dev(dy=(y + j) % 4, dc=(c + m) % 2)).start()
    expect("tin", tin_all)
    leave(tr_recv.at[pl.ds(0, 7), :, pl.ds(0, 768)], "tin")

    def pair(lse_row, delta_row, query, dquery, keys, values):
        probs = jnp.exp2(nt(keys, query) * (FACTOR * LOG2E) - lse_row)
        dscores = (probs * (nt(values, dquery) - delta_row)).astype(BF16)
        return probs.astype(BF16), dscores

    def row512(i, first):
        return jnp.concatenate([st[i, first + n:first + n + 1, :] for n in range(4)], axis=1)

    def attend(step, carry):
        i = (step % 2) * 2 + step // 4
        j = ((step + 2) // 4) % 2

        @pl.when(step == 1)
        def _():
            got(qd.at[2], "b_qc")
            got(st.at[2], "b_sc")

        @pl.when(step == 2)
        def _():
            forward(0)
            forward(1)
            got(kv.at[1], "b_kv")

        @pl.when(step == 3)
        def _():
            forward(2)
            forward(3)

        @pl.when(step == 4)
        def _():
            got(qd.at[1], "b_qz")
            remote(qd.at[1], qd.at[3], "b_qf", dev(dc=1 - c)).start()
            got(st.at[1], "b_sz")
            remote(st.at[1], st.at[3], "b_sf", dev(dc=1 - c)).start()

        @pl.when(step == 5)
        def _():
            got(qd.at[3], "b_qf")
            got(st.at[3], "b_sf")

        query, dquery = qd[i, 0, 0:SET, :], qd[i, 1, 0:SET, :]
        keys, values = kv[j, 0], kv[j, 1]
        probs, dscores = pair(row512(i, 0), row512(i, 4), query, dquery, keys, values)
        gv_acc[j] += nn(probs, dquery)
        gk_acc[j] += nn(dscores, query)
        gq_acc[i, 0:SET, :] += tn(dscores, keys)
        return carry

    def attend_text(j):
        query = jnp.concatenate([qd[i, 0, SET:ROWS, :] for i in range(4)], axis=0)
        dquery = jnp.concatenate([qd[i, 1, SET:ROWS, :] for i in range(4)], axis=0)
        lse_row = jnp.zeros((8, 128), F32)
        delta_row = jnp.zeros((8, 128), F32)
        for i in range(4):
            one, two = (jnp.broadcast_to(st[i, r:r + 1, :], (8, 128)) for r in (8, 9))
            lse_row = lse_row + (pltpu.roll(one, 32 * i, 1) if i else one)
            delta_row = delta_row + (pltpu.roll(two, 32 * i, 1) if i else two)
        keys, values = kv[j, 0], kv[j, 1]
        probs, dscores = pair(lse_row[0:1, :], delta_row[0:1, :], query, dquery, keys, values)
        gv_acc[j] += nn(probs, dquery)
        gk_acc[j] += nn(dscores, query)
        from_text = tn(dscores, keys)
        for i in range(4):
            gq_acc[i, SET:ROWS, :] += from_text[32 * i:32 * i + 32, :]

    lax.fori_loop(0, 6, attend, 0)
    leave(qd.at[0], "b_qf")
    leave(st.at[0], "b_sf")
    attend_text(1)
    dkv_s[0] = (gk_acc[1] * FACTOR).astype(BF16)
    dkv_s[1] = gv_acc[1].astype(BF16)
    remote(dkv_s, dkv_r, "d_kv", dev(dz=zn)).start()
    expect("d_kv", dkv_r)
    leave(dkv_s, "d_kv")
    lax.fori_loop(6, 8, attend, 0)
    attend_text(0)
    dqc_s[0] = (gq_acc[2] * FACTOR).astype(BF16)
    dqc_s[1] = (gq_acc[3] * FACTOR).astype(BF16)
    remote(dqc_s, dqc_r, "d_qc", dev(dc=1 - c)).start()
    expect("d_qc", dqc_r)
    leave(dqc_s, "d_qc")
    got(dqc_r, "d_qc")
    dqz_s[...] = (gq_acc[1] * FACTOR + dqc_r[1].astype(F32)).astype(BF16)
    remote(dqz_s, dqz_r, "d_qz", dev(dz=zf)).start()
    expect("d_qz", dqz_r)
    leave(dqz_s, "d_qz")

    def send_grads(name, cols, table):
        own_part = gw.at[c, :, :, :, cols]
        remote(own_part, own_part, name, dev(dc=1 - c)).start()
        expect(name, gw.at[1 - c, :, :, :, cols])
        leave(own_part, name)
        for ch in table:
            for xx in (2, 1, 3, 0):
                to = (x + xx) % 4
                own = jnp.logical_and(xx == 0, c == mine)
                piece = gw.at[c, :, to, :, pl.ds(128 * ch, 128)]
                place = gs.at[c, :, :, pl.ds(pl.multiple_of(256 * ch + 128 * half, 128), 128)]

                @pl.when(jnp.logical_not(own))
                def _():
                    remote(piece, place, "e", dev(dx=to, dc=mine)).start()

                @pl.when(own)
                def _():
                    local(piece, place, "e").start()

    def finish_channel(ch, value):
        gw[c, :, :, :, 128 * ch:128 * ch + 128] = value[0:SET, :].reshape(4, 4, 32, 128)
        g_txt[:, 128 * ch:128 * ch + 128] = value[SET:ROWS, :]

    got(dkv_r, "d_kv")
    finish_channel(1, (gk_acc[0] * FACTOR + dkv_r[0].astype(F32)).astype(BF16))
    finish_channel(2, (gv_acc[0] + dkv_r[1].astype(F32)).astype(BF16))
    send_grads("gkv", pl.ds(128, 256), (1, 2))
    got(dqz_r, "d_qz")
    finish_channel(0, (gq_acc[0] * FACTOR + dqc_r[0].astype(F32) + dqz_r[...].astype(F32)).astype(BF16))
    send_grads("gq", pl.ds(0, 128), (0,))
    expect("e", gs)
    for ch in range(3):
        one = gw.at[0, :, 0, :, pl.ds(128 * ch, 128)]
        leave_if(c == mine, one, "e", 3)
        leave_if(c != mine, one, "e", 4)
    for xx in (2, 1, 3, 0):
        own = jnp.logical_and(xx == 0, c == mine)
        for ch in range(3):
            piece = g_txt.at[:, pl.ds(128 * ch, 128)]
            place = tgz.at[c, :, pl.ds(pl.multiple_of(256 * ch + 128 * half, 128), 128)]

            @pl.when(jnp.logical_not(own))
            def _():
                remote(piece, place, "te", dev(dx=(x + xx) % 4, dc=mine)).start()

            @pl.when(own)
            def _():
                local(piece, place, "te").start()
    expect("te", tgz)
    leave_if(c == mine, g_txt, "te", 3)
    leave_if(c != mine, g_txt, "te", 4)
    local(g_txt, tzz.at[dp, c, z], "tz").start()
    for t in (4, 3, 5, 2, 6, 1, 7):
        remote(g_txt, tzz.at[dp, c, z], "tz", along_z(t)).start()
    expect("tz", tzz.at[:, c])
    leave(tr_recv.at[pl.ds(0, 7), :, pl.ds(0, 384)], "tz")

    got(gw.at[1 - c, :, :, :, pl.ds(128, 256)], "gkv")
    got(gw.at[1 - c, :, :, :, pl.ds(0, 128)], "gq")
    grads = gw[...].reshape(1024, 384)
    col = nn(jnp.ones((8, 1024), BF16), grads)[0:1, :]

    def project(n):
        i = pairs[n]
        got(vin_all.at[:, pl.ds(0, 3), :, :, chunk[n]], "v2%d" % n)
        cols = pl.ds(pl.multiple_of(384 * i, 128), 384)
        part = tn(vin_all[:, :, :, :, cols].reshape(1024, 384), grads)
        m_acc[cols, :] = part
        gain = jnp.concatenate([gain_col[cols, :]] * 3, axis=1)
        shift = jnp.concatenate([shift_col[cols, :]] * 3, axis=1)
        term = gain * part + shift * col
        wt[2 * i] = term[0:192, :]
        wt[2 * i + 1] = term[192:384, :]

    def ring_to(way):
        to = (pos + (1 if way == 0 else 7)) % 8
        return dev(ddp=to // 4, dz=to % 4)

    def ring(step):
        for ch in range(3):
            lane_cols = slice(128 * ch, 128 * ch + 128)
            for way in range(2):
                dest = (pos + (4 - step if way == 0 else 4 + step)) % 8
                rows = (slice(0, 96) if way == 0 else slice(96, 192)) if step == 0 else slice(0, 192)
                own = wt[dest, rows, lane_cols]
                if step:
                    size = 96 if step == 1 else 192
                    heard = ring_r.at[way, step - 1, ch, pl.ds(0, size)]
                    got(heard, "r%d%d%d" % (way, step - 1, ch))
                    heard = heard[...].astype(F32)
                    if step == 1:
                        near, far = own[0:96, :], own[96:192, :]
                        pair_ = (near + heard, far) if way == 0 else (near, far + heard)
                        own = jnp.concatenate(pair_, axis=0)
                    else:
                        own = own + heard
                size = 96 if step == 0 else 192
                out_ref = ring_s.at[way, step, ch, pl.ds(0, size)]
                out_ref[...] = own.astype(BF16)
                name = "r%d%d%d" % (way, step, ch)
                remote(out_ref, ring_r.at[way, step, ch, pl.ds(0, size)], name, ring_to(way)).start()
                expect(name, ring_r.at[way, step, ch, pl.ds(0, size)])
                leave(out_ref, name)

    def back_chunk(n):
        cols = slice(512 * n, 512 * n + 512)
        rows = gs[...].reshape(256, 768)
        term = (nt(rows[:, 0:256], l_w[0, cols, :]) + nt(rows[:, 256:512], l_w[1, cols, :])
                + nt(rows[:, 512:768], l_w[2, cols, :]))

        @pl.when(c == 0)
        def _():
            b_own[:, cols] = term[0:128, :]
            b_send[:, cols] = term[128:256, :].astype(BF16)

        @pl.when(c == 1)
        def _():
            b_own[:, cols] = term[128:256, :]
            b_send[:, cols] = term[0:128, :].astype(BF16)
        remote(b_send.at[:, cols], b_recv.at[:, cols], "bc%d" % n, dev(dc=1 - c)).start()
        expect("bc%d" % n, b_recv.at[:, cols])
        leave(b_send.at[:, cols], "bc%d" % n)

    def gather_chunk(n):
        cols = slice(512 * n, 512 * n + 512)
        got(b_recv.at[:, cols], "bc%d" % n)
        total = b_own[:, cols] + b_recv[:, cols].astype(F32)
        b_own[:, cols] = total
        for yy in range(4):
            y_send[yy, :, cols] = total[32 * yy:32 * yy + 32, :].astype(BF16)

            @pl.when(yy != y)
            def _():
                remote(y_send.at[yy, :, cols], y_recv.at[y, :, cols], "by", dev(dy=yy)).start()

    project(0)
    ring(0)
    project(1)
    project(2)
    project(3)
    got(wq, "wq")
    for m in range(8):
        rows = slice(192 * m, 192 * m + 192)
        zero = jnp.zeros((192, 128), F32)
        one = jnp.zeros((192, 128), F32)
        for ch in range(3):
            w_part = wq[ch, rows, :].astype(F32)
            zero = zero + w_part * col[:, 128 * ch:128 * ch + 128]
            one = one + w_part * m_acc[rows, 128 * ch:128 * ch + 128]
        s_acc[0, rows, :] = zero
        s_acc[1, rows, :] = one
    for n in range(2):
        high = s_acc[n].astype(BF16)
        low = (s_acc[n] - high.astype(F32)).astype(BF16)
        row = jnp.ones((8, 128), BF16)
        s1_buf[me, n:n + 1, :] = (nt(row, high) + nt(row, low))[0:1, :]

    for i, j in plane:
        remote(s1_buf.at[me], s1_buf.at[me], "s1", dev(dx=chip(i, j)[0], dy=chip(i, j)[1])).start()
    expect("s1", s1_buf.at[pl.ds(0, 15)])
    leave(s1_buf.at[pl.ds(0, 15)], "s1")
    got(tgz, "te")
    ready("tw")
    rows = tgz[...].reshape(64, 768)
    term = (nt(rows[:, 0:256], l_tw[0]) + nt(rows[:, 256:512], l_tw[1]) + nt(rows[:, 512:768], l_tw[2]))
    for core in range(2):
        tr_send[core] = term[32 * core:32 * core + 32, :].astype(BF16)
        own = jnp.logical_and(y == z, c == core)

        @pl.when(jnp.logical_not(own))
        def _():
            remote(tr_send.at[core], tr_recv.at[head], "tr", dev(dy=z, dc=core)).start()

        @pl.when(own)
        def _():
            local(tr_send.at[core], tr_recv.at[head], "tr").start()
    leave_if(y == z, tr_send.at[0], "tr")
    leave_if(y != z, tr_send, "tr")

    ring(1)
    ready("w")
    got(gs, "e")
    for n in range(6):
        back_chunk(n)

    got(tzz.at[:, c], "tz")
    remote(tzz.at[:, c], tzz.at[:, c], "tzs", dev(dc=1 - c)).start()
    expect("tzs", tzz.at[:, 1 - c])
    leave(tzz.at[:, c], "tzs")

    for n in range(6):
        gather_chunk(n)
    expect("by", y_recv.at[pl.ds(0, 3)])
    leave(y_send.at[pl.ds(0, 3)], "by")

    @pl.when(y == z)
    def _():
        got(tr_recv, "tr")
        tback = tr_recv[0].astype(F32)
        for hd in range(1, 8):
            tback = tback + tr_recv[hd].astype(F32)
        tdn_all[x] = ((1.0 + l_tmod[1:2, quarter]) * tback).astype(BF16)
        for t in (2, 1, 3):
            remote(tdn_all.at[x], tdn_all.at[x], "tdz", dev(dz=(z + t) % 4)).start()
        ts_buf[c] = jnp.concatenate([
            jnp.sum(tback, axis=0, keepdims=True),
            jnp.sum(tback * l_tnrm[:, quarter].astype(F32), axis=0, keepdims=True)], axis=0)
        for j, m in peers:
            remote(ts_buf.at[c], ts_buf.at[c], "ts", dev(dy=(y + j) % 4, dc=(c + m) % 2)).start()
    leave_if(y == z, tdn_all.at[pl.ds(0, 3)], "tdz")
    for _ in range(7):
        leave_if(y == z, ts_buf.at[0], "ts")

    ring(2)
    got(tzz.at[:, 1 - c], "tzs")
    got(tin_all, "tin")
    tw_s[...] = tn(tin_all[...].reshape(512, 384), tzz[...].reshape(512, 384)).astype(BF16)
    for n in range(2):
        for ch in range(3):
            rows = pl.ds(pl.multiple_of(192 * c + 96 * n, 32), 96)
            tf_s[n, ch] = tw_s[rows, 128 * ch:128 * ch + 128]
        own = jnp.logical_and(c == mine, n == half)

        @pl.when(jnp.logical_not(own))
        def _():
            remote(tf_s.at[n], tf_r.at[half], "tf", dev(dx=2 * c + n, dc=mine)).start()

        @pl.when(own)
        def _():
            local(tf_s.at[n], tf_r.at[half], "tf").start()
    expect("tf", tf_r)
    leave_if(c == mine, tf_s.at[0], "tf")
    leave_if(c != mine, tf_s, "tf")

    got(s1_buf.at[pl.ds(0, 15)], "s1")
    stat = s1_buf[0]
    for t in range(1, 16):
        stat = stat + s1_buf[t]
    s2_buf[z] = stat
    for t in (2, 1, 3):
        remote(s2_buf.at[z], s2_buf.at[z], "s2", dev(dz=(z + t) % 4)).start()
    expect("s2", s2_buf.at[pl.ds(0, 3)])
    leave(s2_buf.at[pl.ds(0, 3)], "s2")
    ring(3)
    @pl.when(y == z)
    def _():
        got(ts_buf.at[0], "ts")

    @pl.when(y != z)
    def _():
        got(ts_buf, "ts")
        got(tdn_all.at[x], "tdz")
    for t in (2, 1, 3):
        remote(tdn_all.at[x], tdn_all.at[x], "tdn", dev(dx=(x + t) % 4)).start()
    expect("tdn", tdn_all.at[pl.ds(0, 3)])
    leave(tdn_all.at[pl.ds(0, 3)], "tdn")
    ts2_buf[z] = ts_buf[0] + ts_buf[1]
    for t in (2, 1, 3):
        remote(ts2_buf.at[z], ts2_buf.at[z], "ts2", dev(dz=(z + t) % 4)).start()
    expect("ts2", ts2_buf.at[pl.ds(0, 3)])
    leave(ts2_buf.at[pl.ds(0, 3)], "ts2")

    for ch in range(3):
        lane_cols = slice(128 * ch, 128 * ch + 128)
        total = wt[pos, :, lane_cols]
        for way in range(2):
            got(ring_r.at[way, 3, ch], "r%d3%d" % (way, ch))
            total = total + ring_r[way, 3, ch].astype(F32)
        fin_s[0, ch] = total[0:96, :].astype(BF16)
        fin_s[1, ch] = total[96:192, :].astype(BF16)
    for n in range(2):
        own = jnp.logical_and(c == mine, n == half)

        @pl.when(jnp.logical_not(own))
        def _():
            remote(fin_s.at[n], fin_r.at[half], "fin", dev(dx=2 * c + n, dc=mine)).start()

        @pl.when(own)
        def _():
            local(fin_s.at[n], fin_r.at[half], "fin").start()
    expect("fin", fin_r)
    leave_if(c == mine, fin_s.at[0], "fin")
    leave_if(c != mine, fin_s, "fin")

    got(s2_buf.at[pl.ds(0, 3)], "s2")
    s3_buf[c] = s2_buf[0] + s2_buf[1] + s2_buf[2] + s2_buf[3]
    remote(s3_buf.at[c], s3_buf.at[c], "s3", dev(dc=1 - c)).start()
    expect("s3", s3_buf.at[0])
    leave(s3_buf.at[0], "s3")

    got(ts2_buf.at[pl.ds(0, 3)], "ts2")
    tsx_buf[x] = ts2_buf[0] + ts2_buf[1] + ts2_buf[2] + ts2_buf[3]
    for t in (2, 1, 3):
        remote(tsx_buf.at[x], tsx_buf.at[x], "tsx", dev(dx=(x + t) % 4)).start()
    expect("tsx", tsx_buf.at[pl.ds(0, 3)])
    leave(tsx_buf.at[pl.ds(0, 3)], "tsx")

    def write(n, src):
        pltpu.make_async_copy(src, results[n], os_.at[n]).start()

    got(s3_buf.at[0], "s3")
    for m in range(8):
        o_vs[:, 384 * m:384 * m + 384] = jnp.concatenate(
            [s3_buf[core, :, 192 * m:192 * m + 192] for core in range(2)], axis=1)
    write(4, o_vs)
    got(y_recv.at[pl.ds(0, 3)], "by")
    back = b_own[rows32(y), :]
    for yy in range(4):
        back = back + jnp.where(yy == y, 0.0, y_recv[yy].astype(F32))
    o_dn[...] = ((1.0 + l_mod[1:2, :]) * back).astype(BF16)
    write(0, o_dn)
    got(tdn_all.at[pl.ds(0, 3)], "tdn")
    for xx in range(4):
        o_tdn[:, 768 * xx:768 * xx + 768] = tdn_all[xx]
    write(1, o_tdn)
    got(tsx_buf.at[pl.ds(0, 3)], "tsx")
    for xx in range(4):
        o_ts[:, 768 * xx:768 * xx + 768] = tsx_buf[xx]
    write(5, o_ts)
    got(fin_r, "fin")
    for ch in range(3):
        for j in range(2):
            o_wg[ch, :, 128 * j:128 * j + 128] = fin_r[j, ch].astype(F32)
    write(2, o_wg)
    got(tf_r, "tf")
    for ch in range(3):
        for j in range(2):
            o_twg[ch, :, 128 * j:128 * j + 128] = tf_r[j, ch].astype(F32)
    write(3, o_twg)
    for n, src in enumerate((o_dn, o_tdn, o_wg, o_twg, o_vs, o_ts)):
        pltpu.make_async_copy(src, results[n], os_.at[n]).wait()


def finish(*refs):
    into = [pltpu.make_async_copy(refs[n], refs[12 + n], refs[18].at[n]) for n in range(6)]
    back = [pltpu.make_async_copy(refs[12 + n], refs[6 + n], refs[18].at[n]) for n in range(6)]
    for copy in into:
        copy.start()
    for first, second in zip(into, back):
        first.wait()
        second.start()
    for copy in back:
        copy.wait()


SCRATCH = (
    ((32, D), BF16), ((32, D), BF16), ((3, 96, 256), F32), ((3, 96, 256), F32), ((2, D), F32), ((2, D), F32),
    ((32, 2048), BF16), ((32, 2048), BF16), ((32, 2048), BF16), ((32, 2048), BF16),
    ((32, D), BF16), ((32, D), BF16), ((3, D, 256), BF16), ((3, 768, 256), BF16),
    ((2, 256), F32), ((2, 256), F32), ((2, D), F32), ((2, D), F32),
    ((4, 2, ROWS, 128), BF16), ((2, 2, ROWS, 128), BF16), ((4, 16, 128), F32),
    ((16, 8, 128), F32), ((16, 8, 128), F32), ((2, 2, 8, 128), F32), ((4, 8, 128), F32),
    ((2, ROWS, 128), F32), ((2, ROWS, 128), F32), ((4, ROWS, 128), F32),
    ((2, ROWS, 128), BF16), ((2, ROWS, 128), BF16), ((2, ROWS, 128), BF16), ((2, ROWS, 128), BF16),
    ((ROWS, 128), BF16), ((ROWS, 128), BF16), ((2, 4, 4, 32, 384), BF16), ((32, 384), BF16),
    ((2, 32, 1536), BF16), ((2, 4, 4, 32, 1536), BF16), ((3, 1536, 128), BF16),
    ((1536, 128), F32), ((1536, 128), F32), ((1536, 384), F32), ((2, 1536, 128), F32), ((32, D), BF16), ((32, 384), BF16), ((2, 2, 4, 32, 384), BF16),
    ((2, 2, 4, 32, 384), BF16), ((2, 32, 768), BF16), ((2, 4, 32, 768), BF16),
    ((8, 192, 384), F32), ((2, 4, 3, 192, 128), BF16), ((2, 4, 3, 192, 128), BF16),
    ((2, 3, 96, 128), BF16), ((2, 3, 96, 128), BF16),
    ((128, D), BF16), ((128, D), BF16), ((128, D), F32), ((4, 32, D), BF16), ((4, 32, D), BF16),
    ((2, 32, 768), BF16), ((8, 32, 768), BF16), ((4, 32, 768), BF16), ((2, 2, 768), F32), ((4, 2, 768), F32), ((4, 2, 768), F32),
    ((16, 2, 1536), F32), ((4, 2, 1536), F32), ((2, 2, 1536), F32),
    ((384, 384), BF16), ((2, 3, 96, 128), BF16), ((2, 3, 96, 128), BF16),
)


def body(
    video_q, video_k, video_v, video_out, video_dout, text_q, text_k, text_v, text_out, text_dout,
    video_lse, text_lse, video_norm, text_norm, video_mod, text_mod, video_weight, text_weight,
):
    args = [a[0] for a in (
        video_q, video_k, video_v, video_out, video_dout, text_q, text_k, text_v, text_out, text_dout,
        video_lse, text_lse, video_norm, text_norm, video_mod, text_mod)]
    args += [jnp.transpose(w, (1, 0, 2)) for w in (video_weight, text_weight)]
    results = pl.pallas_call(
        kernel,
        out_shape=(
            jax.ShapeDtypeStruct((32, D), BF16), jax.ShapeDtypeStruct((32, D), BF16),
            jax.ShapeDtypeStruct((3, 96, 256), F32), jax.ShapeDtypeStruct((3, 96, 256), F32),
            jax.ShapeDtypeStruct((2, D), F32), jax.ShapeDtypeStruct((2, D), F32),
        ),
        in_specs=[pl.BlockSpec(memory_space=pl.ANY)] * len(args),
        out_specs=[pl.BlockSpec(memory_space=pl.ANY)] * 6,
        scratch_shapes=[pltpu.VMEM(shape, kind) for shape, kind in SCRATCH] + [
            pltpu.SemaphoreType.DMA((len(NAMES),)),
            pltpu.SemaphoreType.DMA((len(NAMES),)),
            pltpu.SemaphoreType.DMA((len(LOCALS),)),
            pltpu.SemaphoreType.DMA((6,)),
        ],
        compiler_params=pltpu.CompilerParams(collective_id=0, has_side_effects=True, vmem_limit_bytes=60 * 1024 * 1024),
    )(*args)
    anywhere = pl.BlockSpec(memory_space=pl.ANY)
    dn, tdn, wg, twg, vs, ts = pl.pallas_call(
        finish,
        out_shape=[jax.ShapeDtypeStruct(r.shape, r.dtype) for r in results],
        in_specs=[anywhere] * 6,
        out_specs=[anywhere] * 6,
        scratch_shapes=[pltpu.VMEM(r.shape, r.dtype) for r in results] + [pltpu.SemaphoreType.DMA((6,))],
        compiler_params=pltpu.CompilerParams(vmem_limit_bytes=60 * 1024 * 1024),
    )(*results)
    return (
        dn[None], tdn[None], jnp.transpose(wg, (1, 0, 2)), jnp.transpose(twg, (1, 0, 2)), vs[None], ts[None],
    )


def solution(mesh):
    tokens = P("dp", ("blk", "head"), None)
    text = P("dp", "head", None)
    whole = P("dp", None, None)
    columns = P(None, None, "head")
    return jax.shard_map(
        body,
        mesh=mesh,
        in_specs=(tokens,) * 5 + (text,) * 5 + (
            P("dp", "head", "blk"), P("dp", "head", None), tokens, text, whole, whole, columns, columns),
        out_specs=(
            tokens, text, P(("dp", "blk"), None, "head"), P(("dp", "blk"), None, "head"), whole, whole),
        check_vma=False,
    )
```
